256 devices in a mesh: grp: 8 (over z_lo, core), seq: 32 (over z_hi, y, x).
Axes of the slice: x: 4, y: 4, z: 8 (z_hi: 2, z_lo: 4; z = z_hi * 4 + z_lo), core: 2. Of those that a mesh axis runs over, the one named last changes fastest.
Arguments:
- resp_len: int32 [128], P('grp'), parts along dimension 0, may hold values from 1 to 384, 4096 in all
- prompt_keys: bfloat16 [16384, 512], P(('grp', 'seq')), parts along dimension 0, may hold values from -6 to 6
- prompt_values: bfloat16 [16384, 512], P(('grp', 'seq')), parts along dimension 0, may hold values from -6 to 6
- resp_q: bfloat16 [32768, 2560], P(('grp', 'seq')), parts along dimension 0, may hold values from -16 to 16
- resp_k: bfloat16 [32768, 512], P(('grp', 'seq')), parts along dimension 0, may hold values from -6 to 6
- resp_v: bfloat16 [32768, 512], P(('grp', 'seq')), parts along dimension 0, may hold values from -6 to 6
- out_grad: bfloat16 [32768, 2560], P(('grp', 'seq')), parts along dimension 0, may hold values from -6 to 6
Outputs:
- attn_out: bfloat16 [32768, 2560], P(('grp', 'seq')), parts along dimension 0
- q_grad: bfloat16 [32768, 2560], P(('grp', 'seq')), parts along dimension 0
- resp_k_grad: bfloat16 [32768, 512], P(('grp', 'seq')), parts along dimension 0
- resp_v_grad: bfloat16 [32768, 512], P(('grp', 'seq')), parts along dimension 0
- prompt_k_grad: bfloat16 [16384, 512], P(('grp', 'seq')), parts along dimension 0
- prompt_v_grad: bfloat16 [16384, 512], P(('grp', 'seq')), parts along dimension 0
The draws below stay inside these ranges and needn't reach their ends.
There are 8 independent parts, one for each index of `grp`. The reference program is written for one: setup_inputs(seed, part) draws one part's arguments, and reference() takes and returns one part's arrays. A program takes and returns all parts, laid end to end along the dimension named above; each array names one. Nothing has to cross between parts.
Inputs may be any that keep to these rules, and one draw needn't show every extreme that they name: `resp_len`: the 16 responses lie one after another in the response tokens, in this order, and their lengths sum to 4096.
All inputs are finite; a program needn't handle non-finite values.
Results may differ from the reference program's by a relative error of at most 0.04.
Values may be sent and summed in bfloat16 or wider, within the bound.
No kernel may reach another device: no remote copies, remote signals or barrier semaphores. Data moves between devices by JAX's collectives and lax.ppermute only.
A program may use at most 128 MiB of HBM per device.

```python
import math
import jax
import jax.numpy as jnp
import numpy as np
from jax import lax

HEADS = 20
KV_HEADS = 4
HEAD_DIM = 128
NRESP = 16
RESP_DEV = 128
RTOT = 4096
PROMPT = 2048
MOST = 384


def draw_prompt_keys(key, part):
    key = jax.random.fold_in(key, 1)
    key_rows = jnp.clip(jax.random.normal(key, (PROMPT, KV_HEADS * HEAD_DIM), jnp.float32), -6.0, 6.0)
    return key_rows.astype(jnp.bfloat16)


def draw_resp_q(key, part):
    key = jax.random.fold_in(key, 2)
    drawn = jnp.clip(jax.random.normal(key, (RTOT, HEADS * HEAD_DIM), jnp.float32), -6.0, 6.0)
    return drawn.astype(jnp.bfloat16)


def level_of(stream_key, extent, pieces, smallest, largest):
    def one(axis_at, shards_of):
        heights = jax.random.uniform(jax.random.fold_in(jax.random.fold_in(stream_key, 6), axis_at), (shards_of,), jnp.float32, smallest / len(pieces), largest / len(pieces))
        return jnp.repeat(jnp.exp(heights), extent[axis_at] // shards_of).reshape((-1,) + (1,) * (len(extent) - axis_at - 1))

    loudness = one(*pieces[0])
    for cut in pieces[1:]:
        loudness = loudness * one(*cut)
    return loudness


def split_up(count, total, limit, lean):
    weights = [(1 << 20) // math.isqrt(rank ** lean) + 1 for rank in range(2, count + 1)]
    spare, given = total - limit - (count - 1), [1] * (count - 1)
    while spare > 0:
        free = [i for i in range(count - 1) if given[i] < limit]
        whole, left = sum([weights[i] for i in free]), spare
        for i in free:
            extra = min(limit - given[i], max(1, left * weights[i] // whole), spare)
            given[i] = given[i] + extra
            spare = spare - extra
    return np.array([limit] + given)


def ragged(key, amount, total, limit, slope):
    if amount == 2:
        one = jax.random.randint(key, (), max(1, total - limit), min(limit, total - 1) + 1)
        return jnp.stack([one, total - one])
    tallies = jnp.asarray(split_up(amount, total, limit, slope), jnp.int32)
    couples = (amount - 1) // 2
    donor, receiver = tallies[1:1 + 2 * couples:2], tallies[2:2 + 2 * couples:2]
    margin = jnp.minimum(donor - 1, limit - receiver)
    passed = jax.random.randint(jax.random.fold_in(key, 1), (couples,), 0, 1 << 20) % (margin + 1)
    tallies = tallies.at[1:1 + 2 * couples:2].set(donor - passed).at[2:2 + 2 * couples:2].set(receiver + passed)
    return tallies[jax.random.permutation(jax.random.fold_in(key, 2), amount)]


def bell_draw(own_key, extent, scale, reach, split=(), kind=jnp.bfloat16):
    level = level_of(own_key, extent, split, -0.22, 0.18) if split else 1.0
    entries = jax.random.normal(own_key, extent, jnp.float32) * scale * level
    return jnp.minimum(jnp.maximum(entries, -reach), reach).astype(kind)


def setup_inputs(seed: int = 0, part: int = 0) -> dict:
    key_list = jax.random.split(jax.random.key(seed), 8)
    part_splits = jax.random.split(jax.random.fold_in(key_list[7], part), 8)
    return {
        "resp_len": ragged(part_splits[0], NRESP, RTOT, MOST, 2).astype(jnp.int32),
        "prompt_keys": draw_prompt_keys(jax.random.fold_in(jax.random.fold_in(key_list[7], part), 71), part),
        "prompt_values": bell_draw(part_splits[2], (PROMPT, KV_HEADS * HEAD_DIM), 1.0, 6.0, ((0, 32),)),
        "resp_q": draw_resp_q(jax.random.fold_in(jax.random.fold_in(key_list[7], part), 71), part),
        "resp_k": bell_draw(part_splits[4], (RTOT, KV_HEADS * HEAD_DIM), 1.0, 6.0, ((0, 32),)),
        "resp_v": bell_draw(part_splits[5], (RTOT, KV_HEADS * HEAD_DIM), 1.0, 6.0, ((0, 32),)),
        "out_grad": bell_draw(part_splits[6], (RTOT, HEADS * HEAD_DIM), 1.0, 6.0, ((0, 32),)),
    }


negative_big = -1e30


def segments_of(positions, resp_ends):
    return jnp.sum((positions[:, None] >= resp_ends[None, :]).astype(jnp.int32), axis=1)


def reference(resp_len, prompt_keys, prompt_values, resp_q, resp_k, resp_v, out_grad):
    per_group = HEADS // KV_HEADS
    factor = HEAD_DIM ** -0.5
    resp_ends = jnp.cumsum(resp_len).astype(jnp.int32)
    positions = jnp.arange(RTOT, dtype=jnp.int32)
    resp_seg = segments_of(positions, resp_ends)
    all_keys = jnp.concatenate([prompt_keys, resp_k], 0).reshape(PROMPT + RTOT, KV_HEADS, HEAD_DIM).astype(jnp.float32)
    all_values = jnp.concatenate([prompt_values, resp_v], 0).reshape(PROMPT + RTOT, KV_HEADS, HEAD_DIM).astype(jnp.float32)
    queries = resp_q.reshape(RTOT, KV_HEADS, per_group, HEAD_DIM)
    upstream = out_grad.reshape(RTOT, KV_HEADS, per_group, HEAD_DIM)

    def one_block(carry, block_index):
        key_grad, value_grad = carry
        first_row = (block_index * RESP_DEV).astype(jnp.int32)
        query_tile = lax.dynamic_slice_in_dim(queries, first_row, RESP_DEV, 0).astype(jnp.float32)
        grad_tile = lax.dynamic_slice_in_dim(upstream, first_row, RESP_DEV, 0).astype(jnp.float32)
        query_pos = first_row + jnp.arange(RESP_DEV, dtype=jnp.int32)
        query_seg = lax.dynamic_slice_in_dim(resp_seg, first_row, RESP_DEV, 0)
        resp_visible = (positions[None, :] <= query_pos[:, None]) & (resp_seg[None, :] == query_seg[:, None])
        visible = jnp.concatenate([jnp.ones((RESP_DEV, PROMPT), dtype=jnp.bool_), resp_visible], 1)
        scores = jnp.einsum("qhgd,nhd->qhgn", query_tile, all_keys) * factor
        scores = jnp.where(visible[:, None, None, :], scores, negative_big)
        row_max = jnp.max(scores, -1, keepdims=True)
        log_total = row_max + jnp.log(jnp.sum(jnp.exp(scores - row_max), -1, keepdims=True))
        weights = jnp.exp(scores - log_total)
        rounded = lax.optimization_barrier(weights.astype(jnp.bfloat16)).astype(jnp.float32)
        output = jnp.einsum("qhgn,nhd->qhgd", rounded, all_values).astype(jnp.bfloat16)
        output_wide = lax.optimization_barrier(output).astype(jnp.float32)
        row_dot = jnp.sum(grad_tile * output_wide, -1, keepdims=True)
        weight_grad = jnp.einsum("qhgd,nhd->qhgn", grad_tile, all_values)
        score_grad = lax.optimization_barrier((weights * (weight_grad - row_dot)).astype(jnp.bfloat16)).astype(jnp.float32)
        query_grad = (jnp.einsum("qhgn,nhd->qhgd", score_grad, all_keys) * factor).astype(jnp.bfloat16)
        key_grad = key_grad + jnp.einsum("qhgn,qhgd->nhd", score_grad, query_tile) * factor
        value_grad = value_grad + jnp.einsum("qhgn,qhgd->nhd", rounded, grad_tile)
        return (key_grad, value_grad), (output, query_grad)

    start_grads = (jnp.zeros((PROMPT + RTOT, KV_HEADS, HEAD_DIM), jnp.float32), jnp.zeros((PROMPT + RTOT, KV_HEADS, HEAD_DIM), jnp.float32))
    (key_grad, value_grad), (outputs, query_grads) = lax.scan(one_block, start_grads, jnp.arange(RTOT // RESP_DEV, dtype=jnp.int32))
    kv_width = KV_HEADS * HEAD_DIM
    attn_out = outputs.reshape(RTOT, HEADS * HEAD_DIM)
    q_grad = query_grads.reshape(RTOT, HEADS * HEAD_DIM)
    key_flat = key_grad.reshape(PROMPT + RTOT, kv_width)
    value_flat = value_grad.reshape(PROMPT + RTOT, kv_width)
    return (attn_out, q_grad, key_flat[PROMPT:].astype(jnp.bfloat16), value_flat[PROMPT:].astype(jnp.bfloat16), key_flat[:PROMPT].astype(jnp.bfloat16), value_flat[:PROMPT].astype(jnp.bfloat16))
```

```python
import jax
import jax.numpy as jnp
from jax import lax
from jax.experimental import pallas as pl
from jax.experimental.pallas import tpu as pltpu
from jax.sharding import PartitionSpec as P

HEADS = 20
KV_HEADS = 4
HEAD_DIM = 128
PER_GROUP = HEADS // KV_HEADS
BACK = 384
NEGATIVE = -1e30
LOG2E = 1.4426950408889634
FACTOR = HEAD_DIM ** (-0.5)

ROWS = 256
KEYS = 512
SPAN = 640
PROMPT_ROWS = 2048
OWN_ROWS = 512
WIDE = PER_GROUP * HEAD_DIM


def nt(a, b):
    return lax.dot_general(a, b, (((1,), (1,)), ((), ())), preferred_element_type=jnp.float32)


def nn(a, b):
    return lax.dot_general(a, b, (((1,), (0,)), ((), ())), preferred_element_type=jnp.float32)


def block_at(x, distance):
    return pl.ds(pl.multiple_of(lax.rem(x + 4 - distance, 4) * 128, 128), 128)


def attention_kernel(
    len_ref, where_ref, q0, q1, q2, q3, s0, s1, s2, s3, before_ref, p0, p1, p2a, p2b, p3,
    o0, o1, o2, o3, stay_ref, minus_ref, plus_ref, minus2_ref, plus2_ref, back_grad_ref, own_grad_ref,
    key2, value1, key_t, value_t, q_all, o_all, s_ref, p_ref, key_sum, value_sum,
):
    base, x = where_ref[0], where_ref[1]
    window = PROMPT_ROWS
    total_rows = PROMPT_ROWS + BACK + OWN_ROWS

    def place(at, source):
        key2[at, :128] = source[:, :128]
        key2[at, 128:] = source[:, :128]
        value1[at, :128] = source[:, 128:]

    value1[:, 128:] = jnp.ones((total_rows, 128), jnp.bfloat16)
    for at, source in ((0, p0), (512, p1), (1024, p2a), (1280, p2b), (1536, p3), (window, before_ref)):
        place(pl.ds(at, source.shape[0]), source)
    for d, source in enumerate((s0, s1, s2, s3)):
        first = window + BACK + lax.rem(x + 4 - d, 4) * 128
        place(pl.ds(pl.multiple_of(first, 128), 128), source.at[128:256, :])
    value_t[128:, :] = jnp.ones((16, total_rows), jnp.bfloat16)
    for c in range(0, total_rows, 128):
        at = slice(c, c + 128)
        key_t[:, at] = key2[at, :128].astype(jnp.float32).T.astype(jnp.bfloat16)
        value_t[:128, at] = value1[at, :128].astype(jnp.float32).T.astype(jnp.bfloat16)
    for d, source in enumerate((q0, q1, q2, q3)):
        q_all[block_at(x, d), :] = source[...]
    key_sum[...] = jnp.zeros_like(key_sum)
    value_sum[...] = jnp.zeros_like(value_sum)

    def step(i, carry):
        block, head = i // PER_GROUP, lax.rem(i, PER_GROUP)
        mine = pl.ds(pl.multiple_of(block * ROWS, ROWS), ROWS)
        q_cols = pl.ds(pl.multiple_of(head * 128, 128), 128)
        g_cols = pl.ds(pl.multiple_of(WIDE + head * 128, 128), 128)
        q = q_all[mine, q_cols]
        scaled = q.astype(jnp.float32).T * (FACTOR * LOG2E)
        grad_t = q_all[mine, g_cols].astype(jnp.float32).T
        high = scaled.astype(jnp.bfloat16)
        low = (scaled - high.astype(jnp.float32)).astype(jnp.bfloat16)
        q2t = jnp.concatenate([high, low], 0)

        own = base + block * ROWS
        row_pos = own + lax.broadcasted_iota(jnp.int32, (1, ROWS), 1)
        seg_start = jnp.zeros((1, ROWS), jnp.int32)
        end = jnp.int32(0)
        for j in range(16):
            end = end + len_ref[j]
            seg_start = jnp.maximum(seg_start, jnp.where(row_pos >= end, end, 0))
        key_pos = own - BACK + lax.broadcasted_iota(jnp.int32, (SPAN, ROWS), 0)
        seen = (key_pos <= row_pos) & (key_pos >= seg_start)
        span_first = window + block * ROWS
        span = pl.ds(pl.multiple_of(span_first, 128), SPAN)
        tiles = [(slice(c, c + KEYS), slice(c, c + KEYS)) for c in range(0, PROMPT_ROWS, KEYS)]
        tiles.append((span, slice(PROMPT_ROWS, PROMPT_ROWS + SPAN)))

        top = None
        for keys, at in tiles:
            s = nn(key2[keys, :], q2t)
            if keys is span:
                s = jnp.where(seen, s, NEGATIVE)
            s_ref[at, :] = s
            tile_top = jnp.max(s, axis=0, keepdims=True)
            top = tile_top if top is None else jnp.maximum(top, tile_top)

        total = jnp.zeros((144, ROWS), jnp.float32)
        for keys, at in tiles:
            p = jnp.exp2(s_ref[at, :] - top).astype(jnp.bfloat16)
            p_ref[at, :] = p
            total = total + nn(value_t[:, keys], p)

        inverse = 1.0 / total[128:129, :]
        out = (total[:128, :] * inverse).astype(jnp.bfloat16).astype(jnp.float32)
        o_all[mine, q_cols] = out.T.astype(jnp.bfloat16)
        grad_n = (grad_t * inverse).astype(jnp.bfloat16)
        row_dot = -jnp.sum(grad_n.astype(jnp.float32) * out, axis=0, keepdims=True)
        dot_high = row_dot.astype(jnp.bfloat16).astype(jnp.float32)
        line = lax.broadcasted_iota(jnp.int32, (128, ROWS), 0)
        extra = jnp.where(line == 0, dot_high, jnp.where(line == 1, row_dot - dot_high, 0.0))
        grad2 = jnp.concatenate([grad_n, extra.astype(jnp.bfloat16)], 0)

        dq = jnp.zeros((HEAD_DIM, ROWS), jnp.float32)
        for keys, at in tiles:
            p = p_ref[at, :]
            ds = (p.astype(jnp.float32) * nn(value1[keys, :], grad2)).astype(jnp.bfloat16)
            dq = dq + nn(key_t[:, keys], ds)
            key_sum[keys, :] += nn(ds, q)
            value_sum[keys, :] += nt(p, grad_n)
        o_all[mine, g_cols] = (dq * FACTOR).T.astype(jnp.bfloat16)
        return carry

    lax.fori_loop(0, OWN_ROWS // ROWS * PER_GROUP, step, 0)

    for d, target in enumerate((o0, o1, o2, o3)):
        target[...] = o_all[block_at(x, d), :]
    places = (
        (0, 512, stay_ref, 0), (1024, 1280, minus_ref, 0), (768, 1024, minus_ref, 256),
        (1280, 1536, plus_ref, 0), (1536, 1792, plus_ref, 256),
        (512, 768, minus2_ref, 0), (1792, 2048, plus2_ref, 0),
        (window, window + BACK, back_grad_ref, 0), (window + BACK, total_rows, own_grad_ref, 0),
    )
    for first, last, target, at in places:
        target[at : at + last - first, :128] = key_sum[first:last, :] * FACTOR
        target[at : at + last - first, 128:] = value_sum[first:last, :]


def call(body, scalars, operands, outs, name, scratch=(), limit=24, after=(), cost=None):
    vmem, smem = pl.BlockSpec(memory_space=pltpu.VMEM), pl.BlockSpec(memory_space=pltpu.SMEM)
    count = len(scalars) + len(operands)

    def kernel(*refs):
        body(*refs[:count], *refs[count + len(after) :])

    return pl.pallas_call(
        kernel,
        in_specs=[smem] * len(scalars) + [vmem] * len(operands) + [pl.BlockSpec(memory_space=pl.ANY)] * len(after),
        out_specs=[vmem] * len(outs),
        out_shape=[jax.ShapeDtypeStruct(shape, dtype) for shape, dtype in outs],
        scratch_shapes=list(scratch),
        compiler_params=pltpu.CompilerParams(vmem_limit_bytes=limit * 1024 * 1024),
        cost_estimate=cost,
        name=name,
    )(*scalars, *operands, *after)


def attention(resp_len, where, operands):
    rows = PROMPT_ROWS + BACK + OWN_ROWS
    bf16, f32 = jnp.bfloat16, jnp.float32
    return call(
        attention_kernel, (resp_len, where), operands,
        [((128, 2 * WIDE), bf16)] * 4 + [((n, 256), f32) for n in (512, 512, 512, 256, 256, BACK, OWN_ROWS)],
        "attention",
        scratch=[
            pltpu.VMEM((rows, 256), bf16),
            pltpu.VMEM((rows, 256), bf16),
            pltpu.VMEM((128, rows), bf16),
            pltpu.VMEM((144, rows), bf16),
            pltpu.VMEM((OWN_ROWS, 2 * WIDE), bf16),
            pltpu.VMEM((OWN_ROWS, 2 * WIDE), bf16),
            pltpu.VMEM((PROMPT_ROWS + SPAN, ROWS), f32),
            pltpu.VMEM((PROMPT_ROWS + SPAN, ROWS), bf16),
            pltpu.VMEM((rows, 128), f32),
            pltpu.VMEM((rows, 128), f32),
        ],
        limit=40,
        cost=pl.CostEstimate(
            flops=6 * 2 * 2560 * 2560 * 128, bytes_accessed=10_000_000, transcendentals=2560 * 2560
        ),
    )


def head_columns(x, distance, width):
    return pl.ds(pl.multiple_of(lax.rem(x + distance, 4) * width, 128), width)


def pack_small_kernel(where_ref, pk_ref, pv_ref, pk_far, pv_far, k_ref, v_ref, s0, s1, s2, s3):
    x = where_ref[1]
    for d, target in enumerate((s0, s1, s2, s3)):
        for at, keys, values in ((0, pk_ref, pv_ref), (64, pk_far, pv_far), (128, k_ref, v_ref)):
            target[at : at + keys.shape[0], :128] = keys[:, head_columns(x, d, 128)]
            target[at : at + keys.shape[0], 128:] = values[:, head_columns(x, d, 128)]


def pack_rows_kernel(where_ref, q_ref, g_ref, q0, q1, q2, q3):
    x = where_ref[1]
    for d, target in enumerate((q0, q1, q2, q3)):
        target[:, :WIDE] = q_ref[:, head_columns(x, d, WIDE)]
        target[:, WIDE:] = g_ref[:, head_columns(x, d, WIDE)]


def collect_kernel(where_ref, s0, s1, s2, s3, mine_ref, ahead_ref):
    x = where_ref[1]
    for d, source in enumerate((s0, s1, s2, s3)):
        mine_ref[d * 128 : d * 128 + 128, :] = source[:128, :]
        block = lax.rem(x + 4 - d, 4)

        @pl.when(block > 0)
        def _():
            ahead_ref[pl.ds(pl.multiple_of((block - 1) * 128, 128), 128), :] = source[128:, :]


def prompt_sum_kernel(stay, minus, plus, minus2, plus2, back, keep_ref, give_ref, back_ref):
    for d in range(4):
        for z, target in ((0, keep_ref), (1, give_ref)):
            at = (d * 2 + z) * 64
            total = stay[at : at + 64, :]
            if d < 2:
                total = total + minus2[at : at + 64, :] + plus[256 + at : 320 + at, :]
            else:
                total = total + plus2[at - 256 : at - 192, :] + minus[at : at + 64, :]
            target[d * 64 : d * 64 + 64, :] = total
    back_ref[...] = back[...]


def final_sum_kernel(where_ref, keep_ref, got_ref, own_ref, back_ref, f0, f1, f2, f3):
    x = where_ref[1]
    for d, target in enumerate((f0, f1, f2, f3)):
        at = slice(d * 64, d * 64 + 64)
        target[:64, :] = (keep_ref[at, :] + got_ref[at, :]).astype(jnp.bfloat16)
        block = lax.rem(x + 4 - d, 4)
        behind = pl.ds(pl.multiple_of(jnp.maximum(block - 1, 0) * 128, 128), 128)
        extra = jnp.where(block > 0, back_ref[behind, :], 0.0)
        target[64:, :] = (own_ref[block_at(x, d), :] + extra).astype(jnp.bfloat16)


def unpack_rows_kernel(where_ref, o0, o1, o2, o3, out_ref, dq_ref):
    x = where_ref[1]
    for d, source in enumerate((o0, o1, o2, o3)):
        out_ref[:, head_columns(x, d, WIDE)] = source[:, :WIDE]
        dq_ref[:, head_columns(x, d, WIDE)] = source[:, WIDE:]


def unpack_small_kernel(where_ref, f0, f1, f2, f3, k_ref, v_ref, pk_ref, pv_ref):
    x = where_ref[1]
    for d, source in enumerate((f0, f1, f2, f3)):
        at = head_columns(x, d, 128)
        pk_ref[:, at] = source[:64, :128]
        pv_ref[:, at] = source[:64, 128:]
        k_ref[:, at] = source[64:, :128]
        v_ref[:, at] = source[64:, 128:]


def along_x(value, step):
    return lax.ppermute(value, "seq", [(i, i // 4 * 4 + (i + step) % 4) for i in range(32)])


def along_y(value, step):
    return lax.ppermute(value, "seq", [(i, i // 16 * 16 + (i + 4 * step) % 16) for i in range(32)])


def along_z(value):
    return lax.ppermute(value, "seq", [(i, (i + 16) % 32) for i in range(32)])


def along_rows(value, step):
    return lax.ppermute(value, "seq", [(i, (i + 4 * step) % 32) for i in range(32)])


def local(resp_len, prompt_keys, prompt_values, resp_q, resp_k, resp_v, out_grad):
    me = lax.axis_index("seq").astype(jnp.int32)
    where = jnp.stack([me // 4 * OWN_ROWS, me % 4])
    rows, bf16, f32 = resp_q.shape[0], jnp.bfloat16, jnp.float32

    far_keys, far_values = along_z(prompt_keys), along_z(prompt_values)
    s = call(
        pack_small_kernel, (where,), (prompt_keys, prompt_values, far_keys, far_values, resp_k, resp_v),
        [((256, 256), bf16)] * 4, "pack_small",
    )
    queries = call(
        pack_rows_kernel, (where,), (resp_q, out_grad), [((rows, 2 * WIDE), bf16)] * 4, "pack_rows", after=(s[0],)
    )
    s = [s[0]] + [along_x(s[d], d) for d in (1, 2, 3)]
    queries = [queries[0]] + [along_x(queries[d], d) for d in (1, 2, 3)]
    mine, ahead = call(collect_kernel, (where,), s, [((512, 256), bf16), ((BACK, 256), bf16)], "collect")
    p1, p3 = along_y(mine, 1), along_y(mine, -1)
    before = along_rows(ahead, 1)
    p2a, p2b = along_y(p1[:256], 1), along_y(p3[256:], -1)

    results = attention(resp_len, where, (*queries, *s, before, mine, p1, p2a, p2b, p3))
    o, (stay, minus, plus, minus2, plus2, back_grad, own_grad) = results[:4], results[4:]

    minus, plus = along_y(minus, -1), along_y(plus, 1)
    o = [o[0]] + [along_x(o[d], -d) for d in (1, 2, 3)]
    minus2 = along_y(minus2 + minus[:256], -1)
    plus2 = along_y(plus2 + plus[:256], 1)
    keep, give, back_grad = call(
        prompt_sum_kernel, (), (stay, minus, plus, minus2, plus2, back_grad),
        [((256, 256), f32)] * 2 + [((BACK, 256), f32)], "prompt_sum", after=tuple(o[1:]),
    )
    got = along_z(give)
    back = along_rows(back_grad, -1)
    attn_out, q_grad = call(
        unpack_rows_kernel, (where,), o, [((rows, HEADS * HEAD_DIM), bf16)] * 2, "unpack_rows"
    )

    f = call(final_sum_kernel, (where,), (keep, got, own_grad, back), [((192, 256), bf16)] * 4, "final_sum")
    f = [f[0]] + [along_x(f[d], -d) for d in (1, 2, 3)]
    resp_k_grad, resp_v_grad, prompt_k_grad, prompt_v_grad = call(
        unpack_small_kernel, (where,), f, [((rows, 512), bf16)] * 2 + [((64, 512), bf16)] * 2, "unpack_small"
    )
    return attn_out, q_grad, resp_k_grad, resp_v_grad, prompt_k_grad, prompt_v_grad


def solution(mesh):
    split = P(("grp", "seq"), None)
    return jax.shard_map(
        local,
        mesh=mesh,
        in_specs=(P("grp"),) + (split,) * 6,
        out_specs=(split,) * 6,
        check_vma=False,
    )
```

```python
import jax
import jax.numpy as jnp
from jax import lax
from jax.experimental import pallas as pl
from jax.experimental.pallas import tpu as pltpu
from jax.sharding import PartitionSpec as P

HEADS = 20
KV_HEADS = 4
HEAD_DIM = 128
PER_GROUP = HEADS // KV_HEADS
BACK = 384
NEGATIVE = -1e30
LOG2E = 1.4426950408889634
FACTOR = HEAD_DIM ** (-0.5)

ROWS = 256
KEYS = 512
SPAN = 640
PROMPT_ROWS = 2048
OWN_ROWS = 512
WIDE = PER_GROUP * HEAD_DIM
LIMIT = 16


def nt(a, b):
    return lax.dot_general(a, b, (((1,), (1,)), ((), ())), preferred_element_type=jnp.float32)


def nn(a, b):
    return lax.dot_general(a, b, (((1,), (0,)), ((), ())), preferred_element_type=jnp.float32)


def block_at(x, distance):
    return pl.ds(pl.multiple_of(lax.rem(x + 4 - distance, 4) * 128, 128), 128)


def forward_kernel(
    len_ref, where_ref, q0, q1, q2, q3, s0, s1, s2, s3, before_ref, h0, h1, h2, h3, l0, l1, l2, l3,
    out_all, q_all, p_all, grad2_all, dq_all, key_t, value1, back_grad_ref, own_grad_ref,
    key2, value_t, wkey2, wvalue1, wkey_t, wvalue_t, s_first, s_second, key_sum, value_sum,
):
    base, x = where_ref[0], where_ref[1]
    window_rows = BACK + OWN_ROWS

    def place(keys, values, at, source):
        keys[at, :128] = source[:, :128]
        keys[at, 128:] = source[:, :128]
        values[at, :128] = source[:, 128:]

    for i, source in enumerate((h0, h1, h2, h3, l0, l1, l2, l3)):
        place(key2, value1, slice(i * 256, i * 256 + 256), source)
    place(wkey2, wvalue1, slice(0, BACK), before_ref)
    for d, source in enumerate((s0, s1, s2, s3)):
        first = BACK + lax.rem(x + 4 - d, 4) * 128
        place(wkey2, wvalue1, pl.ds(pl.multiple_of(first, 128), 128), source.at[64:192, :])
    for rows, keys, values, keys_t, values_t in (
        (PROMPT_ROWS, key2, value1, key_t, value_t), (window_rows, wkey2, wvalue1, wkey_t, wvalue_t),
    ):
        values[:, 128:] = jnp.ones((rows, 128), jnp.bfloat16)
        values_t[128:, :] = jnp.ones((16, rows), jnp.bfloat16)
        for c in range(0, rows, 128):
            at = slice(c, c + 128)
            keys_t[:, at] = keys[at, :128].astype(jnp.float32).T.astype(jnp.bfloat16)
            values_t[:128, at] = values[at, :128].astype(jnp.float32).T.astype(jnp.bfloat16)
    for d, source in enumerate((q0, q1, q2, q3)):
        q_all[block_at(x, d), :] = source[...]
    key_sum[...] = jnp.zeros_like(key_sum)
    value_sum[...] = jnp.zeros_like(value_sum)

    def one_head(head, carry):
        q_cols = pl.ds(pl.multiple_of(head * 128, 128), 128)
        g_cols = pl.ds(pl.multiple_of(WIDE + head * 128, 128), 128)
        state = []
        for block, s_ref in enumerate((s_first, s_second)):
            mine = slice(block * ROWS, block * ROWS + ROWS)
            q = q_all[mine, q_cols]
            scaled = q.astype(jnp.float32).T * (FACTOR * LOG2E)
            high = scaled.astype(jnp.bfloat16)
            low = (scaled - high.astype(jnp.float32)).astype(jnp.bfloat16)
            q2t = jnp.concatenate([high, low], 0)
            top = None
            for c in range(0, PROMPT_ROWS, KEYS):
                s = nn(key2[c : c + KEYS, :], q2t)
                s_ref[c : c + KEYS, :] = s
                tile_top = jnp.max(s, axis=0, keepdims=True)
                top = tile_top if top is None else jnp.maximum(top, tile_top)

            own = base + block * ROWS
            row_pos = own + lax.broadcasted_iota(jnp.int32, (1, ROWS), 1)
            seg_start = jnp.zeros((1, ROWS), jnp.int32)
            end = jnp.int32(0)
            for j in range(16):
                end = end + len_ref[j]
                seg_start = jnp.maximum(seg_start, jnp.where(row_pos >= end, end, 0))
            key_pos = own - BACK + lax.broadcasted_iota(jnp.int32, (SPAN, ROWS), 0)
            seen = (key_pos <= row_pos) & (key_pos >= seg_start)
            span = slice(block * ROWS, block * ROWS + SPAN)
            s = jnp.where(seen, nn(wkey2[span, :], q2t), NEGATIVE)
            s_ref[PROMPT_ROWS:, :] = s
            top = jnp.maximum(top, jnp.max(s, axis=0, keepdims=True))
            state.append((block, s_ref, mine, span, q, top))

        for block, s_ref, mine, span, q, top in state:
            item = block * PER_GROUP + head
            total = jnp.zeros((144, ROWS), jnp.float32)
            for c in range(0, PROMPT_ROWS, KEYS):
                p = jnp.exp2(s_ref[c : c + KEYS, :] - top).astype(jnp.bfloat16)
                p_all[item, c : c + KEYS, :] = p
                total = total + nn(value_t[:, c : c + KEYS], p)
            p = jnp.exp2(s_ref[PROMPT_ROWS:, :] - top).astype(jnp.bfloat16)
            total = total + nn(wvalue_t[:, span], p)

            inverse = 1.0 / total[128:129, :]
            out = (total[:128, :] * inverse).astype(jnp.bfloat16).astype(jnp.float32)
            out_all[mine, q_cols] = out.T.astype(jnp.bfloat16)
            grad_n = (q_all[mine, g_cols].astype(jnp.float32).T * inverse).astype(jnp.bfloat16)
            row_dot = -jnp.sum(grad_n.astype(jnp.float32) * out, axis=0, keepdims=True)
            dot_high = row_dot.astype(jnp.bfloat16).astype(jnp.float32)
            line = lax.broadcasted_iota(jnp.int32, (128, ROWS), 0)
            extra = jnp.where(line == 0, dot_high, jnp.where(line == 1, row_dot - dot_high, 0.0))
            grad2 = jnp.concatenate([grad_n, extra.astype(jnp.bfloat16)], 0)
            grad2_all[item] = grad2

            ds = (p.astype(jnp.float32) * nn(wvalue1[span, :], grad2)).astype(jnp.bfloat16)
            dq_all[item] = nn(wkey_t[:, span], ds)
            key_sum[span, :] += nn(ds, q)
            value_sum[span, :] += nt(p, grad_n)
        return carry

    lax.fori_loop(0, PER_GROUP, one_head, 0)

    for target, at in ((back_grad_ref, slice(0, BACK)), (own_grad_ref, slice(BACK, window_rows))):
        target[:, :128] = key_sum[at, :] * FACTOR
        target[:, 128:] = value_sum[at, :]


def backward(first, q_all, p_all, grad2_all, dq_all, key_t, value1, key_sum, value_sum, finish):
    key_sum[...] = jnp.zeros_like(key_sum)
    value_sum[...] = jnp.zeros_like(value_sum)

    def one_head(head, carry):
        q_cols = pl.ds(pl.multiple_of(head * 128, 128), 128)
        dq = [dq_all[block * PER_GROUP + head] for block in range(2)]
        for c in range(0, PROMPT_ROWS // 2, KEYS):
            at, keys = slice(c, c + KEYS), slice(first + c, first + c + KEYS)
            key_term, value_term = None, None
            for block in range(2):
                item = block * PER_GROUP + head
                grad2 = grad2_all[item]
                p = p_all[item, keys, :]
                ds = (p.astype(jnp.float32) * nn(value1[keys, :], grad2)).astype(jnp.bfloat16)
                dq[block] = dq[block] + nn(key_t[:, keys], ds)
                k = nn(ds, q_all[block * ROWS : block * ROWS + ROWS, q_cols])
                v = nt(p, grad2[:128, :])
                key_term = k if key_term is None else key_term + k
                value_term = v if value_term is None else value_term + v
            key_sum[at, :] += key_term
            value_sum[at, :] += value_term
        for block in range(2):
            finish(head, block, dq[block])
        return carry

    lax.fori_loop(0, PER_GROUP, one_head, 0)


def write_sums(key_sum, value_sum, targets):
    for i, target in enumerate(targets):
        at = slice(i * 256, i * 256 + 256)
        target[:, :128] = key_sum[at, :] * FACTOR
        target[:, 128:] = value_sum[at, :]


def far_backward_kernel(
    q_all, p_all, grad2_all, dq_in, key_t, value1, dq_out, g0, g1, g2, g3, key_sum, value_sum
):
    def finish(head, block, dq):
        dq_out[block * PER_GROUP + head] = dq

    backward(0, q_all, p_all, grad2_all, dq_in, key_t, value1, key_sum, value_sum, finish)
    write_sums(key_sum, value_sum, (g0, g1, g2, g3))


def near_backward_kernel(
    where_ref, q_all, p_all, grad2_all, dq_in, key_t, value1, out_all,
    g0, g1, g2, g3, o0, o1, o2, o3, dq_rows, key_sum, value_sum,
):
    def finish(head, block, dq):
        cols = pl.ds(pl.multiple_of(head * 128, 128), 128)
        dq_rows[block * ROWS : block * ROWS + ROWS, cols] = (dq * FACTOR).T.astype(jnp.bfloat16)

    backward(PROMPT_ROWS // 2, q_all, p_all, grad2_all, dq_in, key_t, value1, key_sum, value_sum, finish)
    write_sums(key_sum, value_sum, (g0, g1, g2, g3))
    for d, target in enumerate((o0, o1, o2, o3)):
        at = block_at(where_ref[1], d)
        target[:, :WIDE] = out_all[at, :]
        target[:, WIDE:] = dq_rows[at, :]


def call(body, scalars, operands, outs, name, scratch=(), limit=24, cost=None, space=pltpu.VMEM):
    vmem, smem = pl.BlockSpec(memory_space=pltpu.VMEM), pl.BlockSpec(memory_space=pltpu.SMEM)
    return pl.pallas_call(
        body,
        in_specs=[smem] * len(scalars) + [pl.BlockSpec(memory_space=space)] * len(operands),
        out_specs=[vmem] * len(outs),
        out_shape=[jax.ShapeDtypeStruct(shape, dtype) for shape, dtype in outs],
        scratch_shapes=list(scratch),
        compiler_params=pltpu.CompilerParams(vmem_limit_bytes=limit * 1024 * 1024),
        cost_estimate=cost,
        name=name,
    )(*scalars, *operands)


def work(share):
    total = int(share * 12 * 2560 * 2560 * 128)
    return pl.CostEstimate(flops=total, bytes_accessed=8_000_000, transcendentals=total // 1536)


def forward(resp_len, where, operands):
    bf16, f32 = jnp.bfloat16, jnp.float32
    window_rows, items = BACK + OWN_ROWS, OWN_ROWS // ROWS * PER_GROUP
    return call(
        forward_kernel, (resp_len, where), operands,
        [
            ((OWN_ROWS, WIDE), bf16), ((OWN_ROWS, 2 * WIDE), bf16), ((items, PROMPT_ROWS, ROWS), bf16),
            ((items, 256, ROWS), bf16), ((items, 128, ROWS), f32), ((128, PROMPT_ROWS), bf16),
            ((PROMPT_ROWS, 256), bf16), ((BACK, 256), f32), ((OWN_ROWS, 256), f32),
        ],
        "forward",
        scratch=[
            pltpu.VMEM((PROMPT_ROWS, 256), bf16),
            pltpu.VMEM((144, PROMPT_ROWS), bf16),
            pltpu.VMEM((window_rows, 256), bf16),
            pltpu.VMEM((window_rows, 256), bf16),
            pltpu.VMEM((128, window_rows), bf16),
            pltpu.VMEM((144, window_rows), bf16),
            pltpu.VMEM((PROMPT_ROWS + SPAN, ROWS), f32),
            pltpu.VMEM((PROMPT_ROWS + SPAN, ROWS), f32),
            pltpu.VMEM((window_rows, 128), f32),
            pltpu.VMEM((window_rows, 128), f32),
        ],
        limit=LIMIT, cost=work(0.5),
    )


SUMS = [pltpu.VMEM((PROMPT_ROWS // 2, 128), jnp.float32)] * 2


def head_columns(x, distance, width):
    return pl.ds(pl.multiple_of(lax.rem(x + distance, 4) * width, 128), width)


def pack_kernel(where_ref, pk, pv, k, v, q, g, s0, s1, s2, s3, q0, q1, q2, q3, sems):
    x = where_ref[1]
    copies = []
    for d, small, rows in ((0, s0, q0), (1, s1, q1), (2, s2, q2), (3, s3, q3)):
        narrow, wide = head_columns(x, d, 128), head_columns(x, d, WIDE)
        for source, target in (
            (pk.at[:, narrow], small.at[0:64, 0:128]),
            (pv.at[:, narrow], small.at[0:64, 128:256]),
            (k.at[:, narrow], small.at[64:192, 0:128]),
            (v.at[:, narrow], small.at[64:192, 128:256]),
            (q.at[:, wide], rows.at[:, 0:WIDE]),
            (g.at[:, wide], rows.at[:, WIDE : 2 * WIDE]),
        ):
            copies.append(pltpu.make_async_copy(source, target, sems.at[len(copies)]))
    for copy in copies:
        copy.start()
    for copy in copies:
        copy.wait()


def collect_kernel(where_ref, s0, s1, s2, s3, mine_ref, ahead_ref):
    x = where_ref[1]
    for d, source in enumerate((s0, s1, s2, s3)):
        mine_ref[d * 64 : d * 64 + 64, :] = source[:64, :]
        block = lax.rem(x + 4 - d, 4)

        @pl.when(block > 0)
        def _():
            ahead_ref[pl.ds(pl.multiple_of((block - 1) * 128, 128), 128), :] = source[64:, :]


def final_sum_kernel(where_ref, n0, n1, n2, got_ref, own_ref, back_ref, f0, f1, f2, f3):
    x = where_ref[1]
    for d, target in enumerate((f0, f1, f2, f3)):
        at = slice(d * 64, d * 64 + 64)
        total = (n0[at, :] + n1[at, :]) + (n2[at, :] + got_ref[at, :])
        target[:64, :] = total.astype(jnp.bfloat16)
        block = lax.rem(x + 4 - d, 4)
        behind = pl.ds(pl.multiple_of(jnp.maximum(block - 1, 0) * 128, 128), 128)
        extra = jnp.where(block > 0, back_ref[behind, :], 0.0)
        target[64:, :] = (own_ref[block_at(x, d), :] + extra).astype(jnp.bfloat16)


def unpack_rows_kernel(where_ref, o0, o1, o2, o3, out_ref, dq_ref):
    x = where_ref[1]
    for d, source in enumerate((o0, o1, o2, o3)):
        out_ref[:, head_columns(x, d, WIDE)] = source[:, :WIDE]
        dq_ref[:, head_columns(x, d, WIDE)] = source[:, WIDE:]


def unpack_small_kernel(where_ref, f0, f1, f2, f3, k_ref, v_ref, pk_ref, pv_ref):
    x = where_ref[1]
    for d, source in enumerate((f0, f1, f2, f3)):
        at = head_columns(x, d, 128)
        pk_ref[:, at] = source[:64, :128]
        pv_ref[:, at] = source[:64, 128:]
        k_ref[:, at] = source[64:, :128]
        v_ref[:, at] = source[64:, 128:]


def along_x(value, step):
    return lax.ppermute(value, "seq", [(i, i // 4 * 4 + (i + step) % 4) for i in range(32)])


def along_y(value, step):
    return lax.ppermute(value, "seq", [(i, i // 16 * 16 + (i + 4 * step) % 16) for i in range(32)])


def along_z(value):
    return lax.ppermute(value, "seq", [(i, (i + 16) % 32) for i in range(32)])


def along_rows(value, step):
    pairs = [(i, i + 4 * step) for i in range(32)]
    return lax.ppermute(value, "seq", [(i, j) for i, j in pairs if 0 <= j < 32])


def local(resp_len, prompt_keys, prompt_values, resp_q, resp_k, resp_v, out_grad):
    me = lax.axis_index("seq").astype(jnp.int32)
    where = jnp.stack([me // 4 * OWN_ROWS, me % 4])
    rows, bf16, f32 = resp_q.shape[0], jnp.bfloat16, jnp.float32

    packed = call(
        pack_kernel, (where,), (prompt_keys, prompt_values, resp_k, resp_v, resp_q, out_grad),
        [((192, 256), bf16)] * 4 + [((rows, 2 * WIDE), bf16)] * 4, "pack",
        scratch=[pltpu.SemaphoreType.DMA((24,))], space=pl.ANY, limit=60,
    )
    s = [packed[0]] + [along_x(packed[d], d) for d in (1, 2, 3)]
    queries = [packed[4]] + [along_x(packed[4 + d], d) for d in (1, 2, 3)]
    mine, ahead = call(collect_kernel, (where,), s, [((256, 256), bf16), ((BACK, 256), bf16)], "collect")
    far = along_z(mine)
    near_keys = [mine] + [along_y(mine, d) for d in (1, 2, 3)]
    before = along_rows(ahead, 1)
    far_keys = [far] + [along_y(far, d) for d in (1, 2, 3)]

    out_all, q_all, p_all, grad2, dq, key_t, value1, back_grad, own_grad = forward(
        resp_len, where, (*queries, *s, before, *far_keys, *near_keys)
    )
    back = along_rows(back_grad, -1)

    dq, stay, minus, through, plus = call(
        far_backward_kernel, (), (q_all, p_all, grad2, dq, key_t, value1),
        [((OWN_ROWS // ROWS * PER_GROUP, 128, ROWS), f32)]
        + [((256, 256), f32)] * 4, "far_backward", scratch=SUMS, limit=LIMIT, cost=work(0.25),
    )
    through = along_y(through, 1)
    minus = along_y(minus, -1)
    plus = along_y(plus + through, 1)
    got = along_z(stay + minus + plus)

    near = call(
        near_backward_kernel, (where,), (q_all, p_all, grad2, dq, key_t, value1, out_all),
        [((256, 256), f32)] * 4 + [((rows, 2 * WIDE), bf16)] * 4, "near_backward",
        scratch=[pltpu.VMEM((OWN_ROWS, WIDE), bf16)] + SUMS, limit=LIMIT, cost=work(0.25),
    )
    stay, minus, through, plus = near[:4]
    through = along_y(through, -1)
    plus = along_y(plus, 1)
    minus = along_y(minus + through, -1)

    o = [near[4]] + [along_x(near[4 + d], -d) for d in (1, 2, 3)]
    attn_out, q_grad = call(
        unpack_rows_kernel, (where,), o, [((rows, HEADS * HEAD_DIM), bf16)] * 2, "unpack_rows"
    )

    f = call(
        final_sum_kernel, (where,), (stay, minus, plus, got, own_grad, back), [((192, 256), bf16)] * 4, "final_sum"
    )
    f = [f[0]] + [along_x(f[d], -d) for d in (1, 2, 3)]
    resp_k_grad, resp_v_grad, prompt_k_grad, prompt_v_grad = call(
        unpack_small_kernel, (where,), f, [((rows, 512), bf16)] * 2 + [((64, 512), bf16)] * 2, "unpack_small"
    )
    return attn_out, q_grad, resp_k_grad, resp_v_grad, prompt_k_grad, prompt_v_grad


def solution(mesh):
    split = P(("grp", "seq"), None)
    return jax.shard_map(
        local,
        mesh=mesh,
        in_specs=(P("grp"),) + (split,) * 6,
        out_specs=(split,) * 6,
        check_vma=False,
    )
```

```python
import jax
import jax.numpy as jnp
from jax import lax
from jax.experimental import pallas as pl
from jax.experimental.pallas import tpu as pltpu
from jax.sharding import PartitionSpec as P

HEADS = 20
KV_HEADS = 4
HEAD_DIM = 128
PER_GROUP = HEADS // KV_HEADS
BACK = 384
NEGATIVE = -1e30
LOG2E = 1.4426950408889634
FACTOR = HEAD_DIM ** (-0.5)

X_GROUPS = [[first + x for x in range(4)] for first in range(0, 32, 4)]
ROWS = 256
KEYS = 512
SPAN = 640
PROMPT_ROWS = 2048
OWN_ROWS = 512
WIDE = PER_GROUP * HEAD_DIM
LIMIT = 16
TILE = 1024


def nt(a, b):
    return lax.dot_general(a, b, (((1,), (1,)), ((), ())), preferred_element_type=jnp.float32)


def nn(a, b):
    return lax.dot_general(a, b, (((1,), (0,)), ((), ())), preferred_element_type=jnp.float32)


def block_at(x, distance):
    return pl.ds(pl.multiple_of(lax.rem(x + 4 - distance, 4) * 128, 128), 128)


def forward_kernel(
    len_ref, where_ref, q_all, s0, s1, s2, s3, before_ref, h0, h1, h2, h3, l0, l1, l2, l3,
    out_all, p_all, grad2_all, dq_all, key_t, value1, back_grad_ref, own_grad_ref,
    key2, value_t, wkey2, wvalue1, wkey_t, wvalue_t, s_first, s_second, key_sum, value_sum,
):
    base, x = where_ref[0], where_ref[1]
    window_rows = BACK + OWN_ROWS

    def place(keys, values, at, source):
        keys[at, :128] = source[:, :128]
        keys[at, 128:] = source[:, :128]
        values[at, :128] = source[:, 128:]

    for i, source in enumerate((h0, h1, h2, h3, l0, l1, l2, l3)):
        place(key2, value1, slice(i * 256, i * 256 + 256), source)
    place(wkey2, wvalue1, slice(0, BACK), before_ref)
    for d, source in enumerate((s0, s1, s2, s3)):
        first = BACK + lax.rem(x + 4 - d, 4) * 128
        place(wkey2, wvalue1, pl.ds(pl.multiple_of(first, 128), 128), source.at[64:192, :])
    for rows, keys, values, keys_t, values_t in (
        (PROMPT_ROWS, key2, value1, key_t, value_t), (window_rows, wkey2, wvalue1, wkey_t, wvalue_t),
    ):
        values[:, 128:] = jnp.ones((rows, 128), jnp.bfloat16)
        values_t[128:, :] = jnp.ones((16, rows), jnp.bfloat16)
        for c in range(0, rows, 128):
            at = slice(c, c + 128)
            keys_t[:, at] = keys[at, :128].astype(jnp.float32).T.astype(jnp.bfloat16)
            values_t[:128, at] = values[at, :128].astype(jnp.float32).T.astype(jnp.bfloat16)
    key_sum[...] = jnp.zeros_like(key_sum)
    value_sum[...] = jnp.zeros_like(value_sum)

    def one_head(head, carry):
        q_cols = pl.ds(pl.multiple_of(head * 128, 128), 128)
        g_cols = pl.ds(pl.multiple_of(WIDE + head * 128, 128), 128)
        state = []
        for block, s_ref in enumerate((s_first, s_second)):
            mine = slice(block * 2, block * 2 + 2)
            q = q_all[mine, :, q_cols].reshape(ROWS, 128)
            scaled = q.astype(jnp.float32) * (FACTOR * LOG2E)
            high = scaled.astype(jnp.bfloat16)
            low = (scaled - high.astype(jnp.float32)).astype(jnp.bfloat16)
            q2 = jnp.concatenate([high, low], 1)
            top = None
            for c in range(0, PROMPT_ROWS, KEYS):
                s = nt(key2[c : c + KEYS, :], q2)
                s_ref[c : c + KEYS, :] = s
                tile_top = jnp.max(s, axis=0, keepdims=True)
                top = tile_top if top is None else jnp.maximum(top, tile_top)

            own = base + block * ROWS
            row_pos = own + lax.broadcasted_iota(jnp.int32, (1, ROWS), 1)
            seg_start = jnp.zeros((1, ROWS), jnp.int32)
            end = jnp.int32(0)
            for j in range(16):
                end = end + len_ref[j]
                seg_start = jnp.maximum(seg_start, jnp.where(row_pos >= end, end, 0))
            key_pos = own - BACK + lax.broadcasted_iota(jnp.int32, (SPAN, ROWS), 0)
            seen = (key_pos <= row_pos) & (key_pos >= seg_start)
            span = slice(block * ROWS, block * ROWS + SPAN)
            s = jnp.where(seen, nt(wkey2[span, :], q2), NEGATIVE)
            s_ref[PROMPT_ROWS:, :] = s
            top = jnp.maximum(top, jnp.max(s, axis=0, keepdims=True))
            state.append((block, s_ref, mine, span, q, top))

        for block, s_ref, mine, span, q, top in state:
            item = block * PER_GROUP + head
            total = jnp.zeros((144, ROWS), jnp.float32)
            for c in range(0, PROMPT_ROWS, KEYS):
                p = jnp.exp2(s_ref[c : c + KEYS, :] - top).astype(jnp.bfloat16)
                p_all[item, c : c + KEYS, :] = p
                total = total + nn(value_t[:, c : c + KEYS], p)
            p = jnp.exp2(s_ref[PROMPT_ROWS:, :] - top).astype(jnp.bfloat16)
            total = total + nn(wvalue_t[:, span], p)

            inverse = 1.0 / total[128:129, :]
            out = (total[:128, :] * inverse).T.astype(jnp.bfloat16)
            out_all[mine, :, q_cols] = out.reshape(2, 128, 128)
            column = jnp.broadcast_to(inverse, (8, ROWS)).T[:, :1]
            grad = q_all[mine, :, g_cols].reshape(ROWS, 128)
            grad_n = (grad.astype(jnp.float32) * column).astype(jnp.bfloat16)
            row_dot = -jnp.sum(grad_n.astype(jnp.float32) * out.astype(jnp.float32), axis=1, keepdims=True)
            dot_high = row_dot.astype(jnp.bfloat16).astype(jnp.float32)
            lane = lax.broadcasted_iota(jnp.int32, (ROWS, 128), 1)
            extra = jnp.where(lane == 0, dot_high, jnp.where(lane == 1, row_dot - dot_high, 0.0))
            grad2 = jnp.concatenate([grad_n, extra.astype(jnp.bfloat16)], 1)
            grad2_all[item] = grad2

            ds = (p.astype(jnp.float32) * nt(wvalue1[span, :], grad2)).astype(jnp.bfloat16)
            dq_all[item] = nn(wkey_t[:, span], ds)
            key_sum[span, :] += nn(ds, q)
            value_sum[span, :] += nn(p, grad_n)
        return carry

    lax.fori_loop(0, PER_GROUP, one_head, 0)

    for target, at in ((back_grad_ref, slice(0, BACK)), (own_grad_ref, slice(BACK, window_rows))):
        target[:, :128] = key_sum[at, :] * FACTOR
        target[:, 128:] = value_sum[at, :]


def backward(first, q_all, p_all, grad2_all, dq_all, key_t, value1, key_sum, value_sum, finish):
    key_sum[...] = jnp.zeros_like(key_sum)
    value_sum[...] = jnp.zeros_like(value_sum)

    def one_head(head, carry):
        q_cols = pl.ds(pl.multiple_of(head * 128, 128), 128)
        dq = [dq_all[block * PER_GROUP + head] for block in range(2)]
        for c in range(0, PROMPT_ROWS // 2, TILE):
            at, keys = slice(c, c + TILE), slice(first + c, first + c + TILE)
            key_term, value_term = None, None
            for block in range(2):
                item = block * PER_GROUP + head
                grad2 = grad2_all[item]
                p = p_all[item, keys, :]
                ds = (p.astype(jnp.float32) * nt(value1[keys, :], grad2)).astype(jnp.bfloat16)
                dq[block] = dq[block] + nn(key_t[:, keys], ds)
                k = nn(ds, q_all[block * 2 : block * 2 + 2, :, q_cols].reshape(ROWS, 128))
                v = nn(p, grad2[:, :128])
                key_term = k if key_term is None else key_term + k
                value_term = v if value_term is None else value_term + v
            key_sum[at, :] += key_term
            value_sum[at, :] += value_term
        for block in range(2):
            finish(head, block, dq[block])
        return carry

    lax.fori_loop(0, PER_GROUP, one_head, 0)


def write_sums(key_sum, value_sum, targets):
    for i, target in enumerate(targets):
        at = slice(i * 256, i * 256 + 256)
        target[:, :128] = key_sum[at, :] * FACTOR
        target[:, 128:] = value_sum[at, :]


def far_backward_kernel(
    q_all, p_all, grad2_all, dq_in, key_t, value1, dq_out, g0, g1, g2, g3, key_sum, value_sum
):
    def finish(head, block, dq):
        dq_out[block * PER_GROUP + head] = dq

    backward(0, q_all, p_all, grad2_all, dq_in, key_t, value1, key_sum, value_sum, finish)
    write_sums(key_sum, value_sum, (g0, g1, g2, g3))


def near_backward_kernel(
    q_all, p_all, grad2_all, dq_in, key_t, value1, out_all, back, g0, g1, g2, g3, o_ref, key_sum, value_sum
):
    def finish(head, block, dq):
        cols = pl.ds(pl.multiple_of(WIDE + head * 128, 128), 128)
        dq = (dq * FACTOR).T.astype(jnp.bfloat16)
        o_ref[block * 2 : block * 2 + 2, :, cols] = dq.reshape(2, 128, 128)

    backward(PROMPT_ROWS // 2, q_all, p_all, grad2_all, dq_in, key_t, value1, key_sum, value_sum, finish)
    write_sums(key_sum, value_sum, (g0, g1, g2, g3))
    o_ref[:, :, :WIDE] = out_all[...]


def call(body, scalars, operands, outs, name, scratch=(), limit=24, cost=None, space=pltpu.VMEM, extra=()):
    smem = pl.BlockSpec(memory_space=pltpu.SMEM)
    return pl.pallas_call(
        body,
        in_specs=[smem] * len(scalars) + [pl.BlockSpec(memory_space=space)] * len(operands)
        + [pl.BlockSpec(memory_space=pl.ANY)] * len(extra),
        out_specs=[pl.BlockSpec(memory_space=space)] * len(outs),
        out_shape=[jax.ShapeDtypeStruct(shape, dtype) for shape, dtype in outs],
        scratch_shapes=list(scratch),
        compiler_params=pltpu.CompilerParams(vmem_limit_bytes=limit * 1024 * 1024),
        cost_estimate=cost,
        name=name,
    )(*scalars, *operands, *extra)


def work(share):
    total = int(share * 12 * 2560 * 2560 * 128)
    return pl.CostEstimate(flops=total, bytes_accessed=8_000_000, transcendentals=total // 1536)


def forward(resp_len, where, operands):
    bf16, f32 = jnp.bfloat16, jnp.float32
    window_rows, items = BACK + OWN_ROWS, OWN_ROWS // ROWS * PER_GROUP
    return call(
        forward_kernel, (resp_len, where), operands,
        [
            ((4, 128, WIDE), bf16), ((items, PROMPT_ROWS, ROWS), bf16),
            ((items, 256, ROWS), bf16), ((items, 128, ROWS), f32), ((128, PROMPT_ROWS), bf16),
            ((PROMPT_ROWS, 256), bf16), ((BACK, 256), f32), ((OWN_ROWS, 256), f32),
        ],
        "forward",
        scratch=[
            pltpu.VMEM((PROMPT_ROWS, 256), bf16),
            pltpu.VMEM((144, PROMPT_ROWS), bf16),
            pltpu.VMEM((window_rows, 256), bf16),
            pltpu.VMEM((window_rows, 256), bf16),
            pltpu.VMEM((128, window_rows), bf16),
            pltpu.VMEM((144, window_rows), bf16),
            pltpu.VMEM((PROMPT_ROWS + SPAN, ROWS), f32),
            pltpu.VMEM((PROMPT_ROWS + SPAN, ROWS), f32),
            pltpu.VMEM((window_rows, 128), f32),
            pltpu.VMEM((window_rows, 128), f32),
        ],
        limit=LIMIT, cost=work(0.5),
    )


SUMS = [pltpu.VMEM((PROMPT_ROWS // 2, 128), jnp.float32)] * 2


def head_columns(x, distance, width):
    return pl.ds(pl.multiple_of(lax.rem(x + distance, 4) * width, 128), width)


def run_copies(pairs, sems):
    copies = [pltpu.make_async_copy(source, target, sems.at[i]) for i, (source, target) in enumerate(pairs)]
    for copy in copies:
        copy.start()
    for copy in copies:
        copy.wait()


def pack_small_kernel(where_ref, pk, pv, k, v, s0, s1, s2, s3, sems):
    pairs = []
    for d, target in enumerate((s0, s1, s2, s3)):
        cols = head_columns(where_ref[1], d, 128)
        for source, lines, lanes in ((pk, (0, 64), 0), (pv, (0, 64), 128), (k, (64, 192), 0), (v, (64, 192), 128)):
            pairs.append((source.at[:, cols], target.at[slice(*lines), lanes : lanes + 128]))
    run_copies(pairs, sems)


def pack_rows_kernel(q, g, target, sems):
    pairs = []
    for h in range(KV_HEADS):
        for source, first in ((q, 0), (g, WIDE)):
            pairs.append((source.at[:, h * WIDE : h * WIDE + WIDE], target.at[h, :, first : first + WIDE]))
    run_copies(pairs, sems)


def collect_kernel(where_ref, s0, s1, s2, s3, mine_ref, ahead_ref):
    x = where_ref[1]
    for d, source in enumerate((s0, s1, s2, s3)):
        mine_ref[d * 64 : d * 64 + 64, :] = source[:64, :]
        block = lax.rem(x + 4 - d, 4)

        @pl.when(block > 0)
        def _():
            ahead_ref[pl.ds(pl.multiple_of((block - 1) * 128, 128), 128), :] = source[64:, :]


def final_sum_kernel(where_ref, n0, n1, n2, got_ref, own_ref, back_ref, f0, f1, f2, f3):
    x = where_ref[1]
    for d, target in enumerate((f0, f1, f2, f3)):
        at = slice(d * 64, d * 64 + 64)
        total = (n0[at, :] + n1[at, :]) + (n2[at, :] + got_ref[at, :])
        target[:64, :] = total.astype(jnp.bfloat16)
        block = lax.rem(x + 4 - d, 4)
        behind = pl.ds(pl.multiple_of(jnp.maximum(block - 1, 0) * 128, 128), 128)
        extra = jnp.where(block > 0, back_ref[behind, :], 0.0)
        target[64:, :] = (own_ref[block_at(x, d), :] + extra).astype(jnp.bfloat16)


def add_kernel(a, b, c, d, after, ab_ref, cd_ref):
    ab_ref[...] = a[...] + b[...]
    cd_ref[...] = c[...] + d[...]


def unpack_rows_kernel(o_ref, out_ref, dq_ref):
    for h in range(KV_HEADS):
        at = slice(h * WIDE, h * WIDE + WIDE)
        out_ref[:, at] = o_ref[h, :, :WIDE]
        dq_ref[:, at] = o_ref[h, :, WIDE:]


def unpack_small_kernel(where_ref, f0, f1, f2, f3, k_ref, v_ref, pk_ref, pv_ref):
    x = where_ref[1]
    for d, source in enumerate((f0, f1, f2, f3)):
        at = head_columns(x, d, 128)
        pk_ref[:, at] = source[:64, :128]
        pv_ref[:, at] = source[:64, 128:]
        k_ref[:, at] = source[64:, :128]
        v_ref[:, at] = source[64:, 128:]


def along_x(value, step):
    return lax.ppermute(value, "seq", [(i, i // 4 * 4 + (i + step) % 4) for i in range(32)])


def exchange_x(value):
    return lax.all_to_all(value, "seq", 0, 0, axis_index_groups=X_GROUPS, tiled=True)


def along_y(value, step):
    return lax.ppermute(value, "seq", [(i, i // 16 * 16 + (i + 4 * step) % 16) for i in range(32)])


def along_z(value):
    return lax.ppermute(value, "seq", [(i, (i + 16) % 32) for i in range(32)])


def along_rows(value, step):
    pairs = [(i, i + 4 * step) for i in range(32)]
    return lax.ppermute(value, "seq", [(i, j) for i, j in pairs if 0 <= j < 32])


def local(resp_len, prompt_keys, prompt_values, resp_q, resp_k, resp_v, out_grad):
    me = lax.axis_index("seq").astype(jnp.int32)
    where = jnp.stack([me // 4 * OWN_ROWS, me % 4])
    rows, bf16, f32 = resp_q.shape[0], jnp.bfloat16, jnp.float32

    s = call(
        pack_small_kernel, (where,), (prompt_keys, prompt_values, resp_k, resp_v), [((192, 256), bf16)] * 4,
        "pack_small", scratch=[pltpu.SemaphoreType.DMA((16,))], space=pl.ANY, limit=60,
    )
    (q_all,) = call(
        pack_rows_kernel, (), (resp_q, out_grad), [((4, rows, 2 * WIDE), bf16)],
        "pack_rows", scratch=[pltpu.SemaphoreType.DMA((8,))], space=pl.ANY, limit=60,
    )
    s = [s[0]] + [along_x(s[d], d) for d in (1, 2, 3)]
    q_all = exchange_x(q_all)
    mine, ahead = call(collect_kernel, (where,), s, [((256, 256), bf16), ((BACK, 256), bf16)], "collect")
    far = along_z(mine)
    near_keys = [mine] + [along_y(mine, d) for d in (1, 2, 3)]
    before = along_rows(ahead, 1)
    far_keys = [far] + [along_y(far, d) for d in (1, 2, 3)]

    out_all, p_all, grad2, dq, key_t, value1, back_grad, own_grad = forward(
        resp_len, where, (q_all, *s, before, *far_keys, *near_keys)
    )
    back = along_rows(back_grad, -1)

    dq, stay, minus, through, plus = call(
        far_backward_kernel, (), (q_all, p_all, grad2, dq, key_t, value1),
        [((OWN_ROWS // ROWS * PER_GROUP, 128, ROWS), f32)]
        + [((256, 256), f32)] * 4, "far_backward", scratch=SUMS, limit=LIMIT, cost=work(0.25),
    )
    through = along_y(through, 1)
    minus = along_y(minus, -1)
    near = call(
        near_backward_kernel, (), (q_all, p_all, grad2, dq, key_t, value1, out_all),
        [((256, 256), f32)] * 4 + [((4, rows, 2 * WIDE), bf16)], "near_backward",
        scratch=SUMS, limit=LIMIT, cost=work(0.25), extra=(back,),
    )
    plus, stay = call(
        add_kernel, (), (plus, through, stay, minus), [((256, 256), f32)] * 2, "far_sum", extra=(near[0],)
    )
    plus = along_y(plus, 1)
    got = along_z(stay + plus)
    stay, minus, through, plus, o = near
    through = along_y(through, -1)
    plus = along_y(plus, 1)
    minus = along_y(minus + through, -1)

    attn_out, q_grad = call(
        unpack_rows_kernel, (), (exchange_x(o),), [((rows, HEADS * HEAD_DIM), bf16)] * 2, "unpack_rows"
    )

    f = call(
        final_sum_kernel, (where,), (stay, minus, plus, got, own_grad, back), [((192, 256), bf16)] * 4, "final_sum"
    )
    f = [f[0]] + [along_x(f[d], -d) for d in (1, 2, 3)]
    resp_k_grad, resp_v_grad, prompt_k_grad, prompt_v_grad = call(
        unpack_small_kernel, (where,), f, [((rows, 512), bf16)] * 2 + [((64, 512), bf16)] * 2, "unpack_small"
    )
    return attn_out, q_grad, resp_k_grad, resp_v_grad, prompt_k_grad, prompt_v_grad


def solution(mesh):
    split = P(("grp", "seq"), None)
    return jax.shard_map(
        local,
        mesh=mesh,
        in_specs=(P("grp"),) + (split,) * 6,
        out_specs=(split,) * 6,
        check_vma=False,
    )
```

```python
import functools

import jax
import jax.numpy as jnp
from jax import lax
from jax.experimental import pallas as pl
from jax.experimental.pallas import tpu as pltpu
from jax.sharding import PartitionSpec as P

HEADS = 20
KV_HEADS = 4
HEAD_DIM = 128
PER_GROUP = HEADS // KV_HEADS
BACK = 384
NEGATIVE = -1e30
LOG2E = 1.4426950408889634
FACTOR = HEAD_DIM ** (-0.5)

X_GROUPS = [[first + x for x in range(4)] for first in range(0, 32, 4)]
ROWS = 256
KEYS = 1024
SPAN = 640
PROMPT_ROWS = 2048
OWN_ROWS = 512
WIDE = PER_GROUP * HEAD_DIM
LIMIT = 16
SHARE = 512


def nt(a, b):
    return lax.dot_general(a, b, (((1,), (1,)), ((), ())), preferred_element_type=jnp.float32)


def nn(a, b):
    return lax.dot_general(a, b, (((1,), (0,)), ((), ())), preferred_element_type=jnp.float32)


def block_at(x, distance):
    return pl.ds(pl.multiple_of(lax.rem(x + 4 - distance, 4) * 128, 128), 128)


def forward_kernel(
    len_ref, where_ref, q_all, s0, s1, s2, s3, before_ref, h0, h1, h2, h3, l0, l1, l2, l3,
    out_all, p_all, grad2_all, grad_all, dq_all, key_t, value1, back_grad_ref, own_grad_ref,
    key2, value_t, wkey2, wvalue1, wkey_t, wvalue_t, s_first, s_second, key_sum, value_sum,
):
    base, x = where_ref[0], where_ref[1]
    window_rows = BACK + OWN_ROWS

    def place(keys, values, at, source):
        keys[at, :128] = source[:, :128]
        keys[at, 128:] = source[:, :128]
        values[at, :128] = source[:, 128:]

    for i, source in enumerate((h2, h1, h0, h3, l2, l1, l0, l3)):
        place(key2, value1, slice(i * 256, i * 256 + 256), source)
    place(wkey2, wvalue1, slice(0, BACK), before_ref)
    for d, source in enumerate((s0, s1, s2, s3)):
        first = BACK + lax.rem(x + 4 - d, 4) * 128
        place(wkey2, wvalue1, pl.ds(pl.multiple_of(first, 128), 128), source.at[64:192, :])
    for rows, keys, values, keys_t, values_t in (
        (PROMPT_ROWS, key2, value1, key_t, value_t), (window_rows, wkey2, wvalue1, wkey_t, wvalue_t),
    ):
        values[:, 128:] = jnp.ones((rows, 128), jnp.bfloat16)
        values_t[128:, :] = jnp.ones((16, rows), jnp.bfloat16)
        for c in range(0, rows, 128):
            at = slice(c, c + 128)
            keys_t[:, at] = keys[at, :128].astype(jnp.float32).T.astype(jnp.bfloat16)
            values_t[:128, at] = values[at, :128].astype(jnp.float32).T.astype(jnp.bfloat16)
    key_sum[...] = jnp.zeros_like(key_sum)
    value_sum[...] = jnp.zeros_like(value_sum)

    def one_head(head, carry):
        q_cols = pl.ds(pl.multiple_of(head * 128, 128), 128)
        g_cols = pl.ds(pl.multiple_of(WIDE + head * 128, 128), 128)
        state = []
        for block, s_ref in enumerate((s_first, s_second)):
            mine = slice(block * 2, block * 2 + 2)
            q = q_all[mine, :, q_cols].reshape(ROWS, 128)
            scaled = q.astype(jnp.float32).T * (FACTOR * LOG2E)
            high = scaled.astype(jnp.bfloat16)
            low = (scaled - high.astype(jnp.float32)).astype(jnp.bfloat16)
            q2t = jnp.concatenate([high, low], 0)
            top = None
            for c in range(0, PROMPT_ROWS, KEYS):
                s = nn(key2[c : c + KEYS, :], q2t)
                s_ref[c : c + KEYS, :] = s
                tile_top = jnp.max(s, axis=0, keepdims=True)
                top = tile_top if top is None else jnp.maximum(top, tile_top)

            own = base + block * ROWS
            row_pos = own + lax.broadcasted_iota(jnp.int32, (1, ROWS), 1)
            seg_start = jnp.zeros((1, ROWS), jnp.int32)
            end = jnp.int32(0)
            for j in range(16):
                end = end + len_ref[j]
                seg_start = jnp.maximum(seg_start, jnp.where(row_pos >= end, end, 0))
            key_pos = own - BACK + lax.broadcasted_iota(jnp.int32, (SPAN, ROWS), 0)
            seen = (key_pos <= row_pos) & (key_pos >= seg_start)
            span = slice(block * ROWS, block * ROWS + SPAN)
            s = jnp.where(seen, nn(wkey2[span, :], q2t), NEGATIVE)
            s_ref[PROMPT_ROWS:, :] = s
            top = jnp.maximum(top, jnp.max(s, axis=0, keepdims=True))
            state.append((block, s_ref, mine, span, q, top))

        for block, s_ref, mine, span, q, top in state:
            item = block * PER_GROUP + head
            total = jnp.zeros((144, ROWS), jnp.float32)
            for c in range(0, PROMPT_ROWS, KEYS):
                p = jnp.exp2(s_ref[c : c + KEYS, :] - top).astype(jnp.bfloat16)
                p_all[item, c : c + KEYS, :] = p
                total = total + nn(value_t[:, c : c + KEYS], p)
            p = jnp.exp2(s_ref[PROMPT_ROWS:, :] - top).astype(jnp.bfloat16)
            total = total + nn(wvalue_t[:, span], p)

            inverse = 1.0 / total[128:129, :]
            out = (total[:128, :] * inverse).astype(jnp.bfloat16).astype(jnp.float32)
            out_all[mine, :, q_cols] = out.T.astype(jnp.bfloat16).reshape(2, 128, 128)
            grad_t = q_all[mine, :, g_cols].reshape(ROWS, 128).astype(jnp.float32).T
            grad_n = (grad_t * inverse).astype(jnp.bfloat16)
            grad_wide = grad_n.astype(jnp.float32)
            row_dot = -jnp.sum(grad_wide * out, axis=0, keepdims=True)
            dot_high = row_dot.astype(jnp.bfloat16).astype(jnp.float32)
            line = lax.broadcasted_iota(jnp.int32, (128, ROWS), 0)
            extra = jnp.where(line == 0, dot_high, jnp.where(line == 1, row_dot - dot_high, 0.0))
            grad2 = jnp.concatenate([grad_n, extra.astype(jnp.bfloat16)], 0)
            grad_rows = grad_wide.T.astype(jnp.bfloat16)
            grad_all[item] = grad_rows
            grad2_all[item] = grad2

            ds = (p.astype(jnp.float32) * nn(wvalue1[span, :], grad2)).astype(jnp.bfloat16)
            dq_all[item] = nn(wkey_t[:, span], ds)
            key_sum[span, :] += nn(ds, q)
            value_sum[span, :] += nn(p, grad_rows)
        return carry

    lax.fori_loop(0, PER_GROUP, one_head, 0)

    for target, at in ((back_grad_ref, slice(0, BACK)), (own_grad_ref, slice(BACK, window_rows))):
        target[:, :128] = key_sum[at, :] * FACTOR
        target[:, 128:] = value_sum[at, :]


def backward(first, q_all, p_all, grad2_all, grad_all, dq_all, key_t, value1, key_sum, value_sum, finish):
    keys = slice(first, first + SHARE)
    key_sum[...] = jnp.zeros_like(key_sum)
    value_sum[...] = jnp.zeros_like(value_sum)

    def one_head(head, carry):
        q_cols = pl.ds(pl.multiple_of(head * 128, 128), 128)
        key_term, value_term = None, None
        for block in range(2):
            item = block * PER_GROUP + head
            p = p_all[item, keys, :]
            ds = (p.astype(jnp.float32) * nn(value1[keys, :], grad2_all[item])).astype(jnp.bfloat16)
            finish(head, block, dq_all[item] + nn(key_t[:, keys], ds))
            k = nn(ds, q_all[block * 2 : block * 2 + 2, :, q_cols].reshape(ROWS, 128))
            v = nn(p, grad_all[item])
            key_term = k if key_term is None else key_term + k
            value_term = v if value_term is None else value_term + v
        key_sum[...] += key_term
        value_sum[...] += value_term
        return carry

    lax.fori_loop(0, PER_GROUP, one_head, 0)


def write_sums(key_sum, value_sum, targets):
    for i, target in enumerate(targets):
        at = slice(i * 256, i * 256 + 256)
        target[:, :128] = key_sum[at, :] * FACTOR
        target[:, 128:] = value_sum[at, :]


def middle_backward_kernel(
    first, q_all, p_all, grad2_all, grad_all, dq_in, key_t, value1, after, dq_out, a_ref, b_ref, key_sum, value_sum
):
    def finish(head, block, dq):
        dq_out[block * PER_GROUP + head] = dq

    backward(first, q_all, p_all, grad2_all, grad_all, dq_in, key_t, value1, key_sum, value_sum, finish)
    write_sums(key_sum, value_sum, (a_ref, b_ref))


def last_backward_kernel(
    first, q_all, p_all, grad2_all, grad_all, dq_in, key_t, value1, out_all, after, a_ref, b_ref, o_ref,
    key_sum, value_sum,
):
    def finish(head, block, dq):
        cols = pl.ds(pl.multiple_of(WIDE + head * 128, 128), 128)
        dq = (dq * FACTOR).T.astype(jnp.bfloat16)
        o_ref[block * 2 : block * 2 + 2, :, cols] = dq.reshape(2, 128, 128)

    backward(first, q_all, p_all, grad2_all, grad_all, dq_in, key_t, value1, key_sum, value_sum, finish)
    write_sums(key_sum, value_sum, (a_ref, b_ref))
    o_ref[:, :, :WIDE] = out_all[...]


def call(body, scalars, operands, outs, name, scratch=(), limit=24, cost=None, space=pltpu.VMEM, extra=()):
    smem = pl.BlockSpec(memory_space=pltpu.SMEM)
    return pl.pallas_call(
        body,
        in_specs=[smem] * len(scalars) + [pl.BlockSpec(memory_space=space)] * len(operands)
        + [pl.BlockSpec(memory_space=pl.ANY)] * len(extra),
        out_specs=[pl.BlockSpec(memory_space=pltpu.VMEM)] * len(outs),
        out_shape=[jax.ShapeDtypeStruct(shape, dtype) for shape, dtype in outs],
        scratch_shapes=list(scratch),
        compiler_params=pltpu.CompilerParams(vmem_limit_bytes=limit * 1024 * 1024),
        cost_estimate=cost,
        name=name,
    )(*scalars, *operands, *extra)


def work(share):
    total = int(share * 12 * 2560 * 2560 * 128)
    return pl.CostEstimate(flops=total, bytes_accessed=8_000_000, transcendentals=total // 1536)


def forward(resp_len, where, operands):
    bf16, f32 = jnp.bfloat16, jnp.float32
    window_rows, items = BACK + OWN_ROWS, OWN_ROWS // ROWS * PER_GROUP
    return call(
        forward_kernel, (resp_len, where), operands,
        [
            ((4, 128, WIDE), bf16), ((items, PROMPT_ROWS, ROWS), bf16),
            ((items, 256, ROWS), bf16), ((items, ROWS, 128), bf16), ((items, 128, ROWS), f32), ((128, PROMPT_ROWS), bf16),
            ((PROMPT_ROWS, 256), bf16), ((BACK, 256), f32), ((OWN_ROWS, 256), f32),
        ],
        "forward",
        scratch=[
            pltpu.VMEM((PROMPT_ROWS, 256), bf16),
            pltpu.VMEM((144, PROMPT_ROWS), bf16),
            pltpu.VMEM((window_rows, 256), bf16),
            pltpu.VMEM((window_rows, 256), bf16),
            pltpu.VMEM((128, window_rows), bf16),
            pltpu.VMEM((144, window_rows), bf16),
            pltpu.VMEM((PROMPT_ROWS + SPAN, ROWS), f32),
            pltpu.VMEM((PROMPT_ROWS + SPAN, ROWS), f32),
            pltpu.VMEM((window_rows, 128), f32),
            pltpu.VMEM((window_rows, 128), f32),
        ],
        limit=LIMIT, cost=work(0.5),
    )


SUMS = [pltpu.VMEM((SHARE, 128), jnp.float32)] * 2


def head_columns(x, distance, width):
    return pl.ds(pl.multiple_of(lax.rem(x + distance, 4) * width, 128), width)


def pack_kernel(where_ref, pk, pv, k, v, q, g, s0, s1, s2, s3, rows, sems):
    pairs = []
    for d, target in enumerate((s0, s1, s2, s3)):
        cols = head_columns(where_ref[1], d, 128)
        for source, lines, lanes in ((pk, (0, 64), 0), (pv, (0, 64), 128), (k, (64, 192), 0), (v, (64, 192), 128)):
            pairs.append((source.at[:, cols], target.at[slice(*lines), lanes : lanes + 128]))
    for h in range(KV_HEADS):
        for source, first in ((q, 0), (g, WIDE)):
            pairs.append((source.at[:, h * WIDE : h * WIDE + WIDE], rows.at[h, :, first : first + WIDE]))
    copies = [pltpu.make_async_copy(source, target, sems.at[i]) for i, (source, target) in enumerate(pairs)]
    for copy in copies:
        copy.start()
    for copy in copies:
        copy.wait()


def collect_kernel(where_ref, s0, s1, s2, s3, mine_ref, ahead_ref):
    x = where_ref[1]
    for d, source in enumerate((s0, s1, s2, s3)):
        mine_ref[d * 64 : d * 64 + 64, :] = source[:64, :]
        block = lax.rem(x + 4 - d, 4)

        @pl.when(block > 0)
        def _():
            ahead_ref[pl.ds(pl.multiple_of((block - 1) * 128, 128), 128), :] = source[64:, :]


def final_sum_kernel(where_ref, n0, n1, n2, n3, got_ref, own_ref, back_ref, f0, f1, f2, f3):
    x = where_ref[1]
    for d, target in enumerate((f0, f1, f2, f3)):
        at = slice(d * 64, d * 64 + 64)
        total = (n0[at, :] + n1[at, :]) + (n2[at, :] + n3[at, :]) + got_ref[at, :]
        target[:64, :] = total.astype(jnp.bfloat16)
        block = lax.rem(x + 4 - d, 4)
        behind = pl.ds(pl.multiple_of(jnp.maximum(block - 1, 0) * 128, 128), 128)
        extra = jnp.where(block > 0, back_ref[behind, :], 0.0)
        target[64:, :] = (own_ref[block_at(x, d), :] + extra).astype(jnp.bfloat16)


def add_kernel(a, b, c, d, ab_ref, cd_ref):
    ab_ref[...] = a[...] + b[...]
    cd_ref[...] = c[...] + d[...]


def unpack_rows_kernel(o_ref, out_ref, dq_ref):
    for h in range(KV_HEADS):
        at = slice(h * WIDE, h * WIDE + WIDE)
        out_ref[:, at] = o_ref[h, :, :WIDE]
        dq_ref[:, at] = o_ref[h, :, WIDE:]


def unpack_small_kernel(where_ref, f0, f1, f2, f3, k_ref, v_ref, pk_ref, pv_ref):
    x = where_ref[1]
    for d, source in enumerate((f0, f1, f2, f3)):
        at = head_columns(x, d, 128)
        pk_ref[:, at] = source[:64, :128]
        pv_ref[:, at] = source[:64, 128:]
        k_ref[:, at] = source[64:, :128]
        v_ref[:, at] = source[64:, 128:]


def along_x(value, step):
    return lax.ppermute(value, "seq", [(i, i // 4 * 4 + (i + step) % 4) for i in range(32)])


def exchange_x(value):
    return lax.all_to_all(value, "seq", 0, 0, axis_index_groups=X_GROUPS, tiled=True)


def along_y(value, step):
    return lax.ppermute(value, "seq", [(i, i // 16 * 16 + (i + 4 * step) % 16) for i in range(32)])


def along_z(value):
    return lax.ppermute(value, "seq", [(i, (i + 16) % 32) for i in range(32)])


def along_rows(value, step):
    pairs = [(i, i + 4 * step) for i in range(32)]
    return lax.ppermute(value, "seq", [(i, j) for i, j in pairs if 0 <= j < 32])


def local(resp_len, prompt_keys, prompt_values, resp_q, resp_k, resp_v, out_grad):
    me = lax.axis_index("seq").astype(jnp.int32)
    where = jnp.stack([me // 4 * OWN_ROWS, me % 4])
    rows, bf16, f32 = resp_q.shape[0], jnp.bfloat16, jnp.float32

    *s, q_all = call(
        pack_kernel, (where,), (prompt_keys, prompt_values, resp_k, resp_v, resp_q, out_grad),
        [((192, 256), bf16)] * 4 + [((4, rows, 2 * WIDE), bf16)], "pack",
        scratch=[pltpu.SemaphoreType.DMA((24,))], space=pl.ANY, limit=60,
    )
    s = [s[0]] + [along_x(s[d], d) for d in (1, 2, 3)]
    q_all = exchange_x(q_all)
    mine, ahead = call(collect_kernel, (where,), s, [((256, 256), bf16), ((BACK, 256), bf16)], "collect")
    far = along_z(mine)
    near_keys = [mine] + [along_y(mine, d) for d in (1, 2, 3)]
    before = along_rows(ahead, 1)
    far_keys = [far] + [along_y(far, d) for d in (1, 2, 3)]

    out_all, p_all, grad2, grad, dq, key_t, value1, back_grad, own_grad = forward(
        resp_len, where, (q_all, *s, before, *far_keys, *near_keys)
    )
    back = along_rows(back_grad, -1)

    def middle(share, dq, after):
        return call(
            functools.partial(middle_backward_kernel, share * SHARE), (),
            (q_all, p_all, grad2, grad, dq, key_t, value1),
            [(dq.shape, f32)] + [((256, 256), f32)] * 2, "backward%d" % share,
            scratch=SUMS, limit=LIMIT, cost=work(0.12), extra=(after,),
        )

    dq, through, minus = middle(0, dq, grad)
    through = along_y(through, 1)
    minus = along_y(minus, -1)
    dq, stay, plus = middle(1, dq, back)
    plus, stay = call(add_kernel, (), (plus, through, stay, minus), [((256, 256), f32)] * 2, "far_sum")
    after = plus
    plus = along_y(plus, 1)

    dq, two, one = middle(2, dq, after)
    got = stay + plus
    after = got
    got = along_z(got)
    stay, three, o = call(
        functools.partial(last_backward_kernel, 3 * SHARE), (), (q_all, p_all, grad2, grad, dq, key_t, value1, out_all),
        [((256, 256), f32)] * 2 + [((4, rows, 2 * WIDE), bf16)], "backward3",
        scratch=SUMS, limit=LIMIT, cost=work(0.12), extra=(after,),
    )
    minus, through, plus = along_y(one, -1), along_y(two, -2), along_y(three, 1)

    attn_out, q_grad = call(
        unpack_rows_kernel, (), (exchange_x(o),), [((rows, HEADS * HEAD_DIM), bf16)] * 2, "unpack_rows"
    )

    f = call(
        final_sum_kernel, (where,), (stay, minus, through, plus, got, own_grad, back),
        [((192, 256), bf16)] * 4, "final_sum",
    )
    f = [f[0]] + [along_x(f[d], -d) for d in (1, 2, 3)]
    resp_k_grad, resp_v_grad, prompt_k_grad, prompt_v_grad = call(
        unpack_small_kernel, (where,), f, [((rows, 512), bf16)] * 2 + [((64, 512), bf16)] * 2, "unpack_small"
    )
    return attn_out, q_grad, resp_k_grad, resp_v_grad, prompt_k_grad, prompt_v_grad


def solution(mesh):
    split = P(("grp", "seq"), None)
    return jax.shard_map(
        local,
        mesh=mesh,
        in_specs=(P("grp"),) + (split,) * 6,
        out_specs=(split,) * 6,
        check_vma=False,
    )
```

```python
import jax
import jax.numpy as jnp
from jax import lax
from jax.experimental import pallas as pl
from jax.experimental.pallas import tpu as pltpu
from jax.sharding import PartitionSpec as P

HEADS = 20
KV_HEADS = 4
HEAD_DIM = 128
PER_GROUP = HEADS // KV_HEADS
BACK = 384
NEGATIVE = -1e30
LOG2E = 1.4426950408889634
FACTOR = HEAD_DIM ** (-0.5)

X_GROUPS = [[first + x for x in range(4)] for first in range(0, 32, 4)]
ROWS = 256
KEYS = 1024
SPAN = 640
PROMPT_ROWS = 2048
OWN_ROWS = 512
WIDE = PER_GROUP * HEAD_DIM


def nt(a, b):
    return lax.dot_general(a, b, (((1,), (1,)), ((), ())), preferred_element_type=jnp.float32)


def nn(a, b):
    return lax.dot_general(a, b, (((1,), (0,)), ((), ())), preferred_element_type=jnp.float32)


def block_at(x, distance):
    return pl.ds(pl.multiple_of(lax.rem(x + 4 - distance, 4) * 128, 128), 128)


def attention_kernel(
    len_ref, where_ref, q_all, s0, s1, s2, s3, before_ref, h0, h1, h2, h3, l0, l1, l2, l3,
    o_ref, g0, g1, g2, g3, g4, g5, g6, g7, back_grad_ref, own_grad_ref,
    key2, value1, key_t, value_t, s_first, s_second, p_first, p_second,
    grad2_first, grad2_second, rows_first, rows_second, key_sum, value_sum,
):
    base, x = where_ref[0], where_ref[1]
    all_rows = PROMPT_ROWS + BACK + OWN_ROWS

    def place(at, source):
        key2[at, :128] = source[:, :128]
        key2[at, 128:] = source[:, :128]
        value1[at, :128] = source[:, 128:]

    for i, source in enumerate((h2, h1, h0, h3, l2, l1, l0, l3)):
        place(slice(i * 256, i * 256 + 256), source)
    place(slice(PROMPT_ROWS, PROMPT_ROWS + BACK), before_ref)
    for d, source in enumerate((s0, s1, s2, s3)):
        first = PROMPT_ROWS + BACK + lax.rem(x + 4 - d, 4) * 128
        place(pl.ds(pl.multiple_of(first, 128), 128), source.at[64:192, :])
    value1[:, 128:] = jnp.ones((all_rows, 128), jnp.bfloat16)
    value_t[128:, :] = jnp.ones((16, all_rows), jnp.bfloat16)
    for c in range(0, all_rows, 128):
        at = slice(c, c + 128)
        key_t[:, at] = key2[at, :128].astype(jnp.float32).T.astype(jnp.bfloat16)
        value_t[:128, at] = value1[at, :128].astype(jnp.float32).T.astype(jnp.bfloat16)
    for ref in (key_sum, value_sum, p_second, grad2_second, rows_second):
        ref[...] = jnp.zeros_like(ref)

    s_refs, p_refs = (s_first, s_second), (p_first, p_second)
    grad2_refs, rows_refs = (grad2_first, grad2_second), (rows_first, rows_second)

    def tiles(block):
        span = PROMPT_ROWS + block * ROWS
        out = [(c, c, KEYS) for c in range(0, PROMPT_ROWS, KEYS)] + [(span, PROMPT_ROWS, SPAN)]
        return [(slice(keys, keys + size), slice(at, at + size)) for keys, at, size in out]

    def rows_of(block, head, first):
        cols = pl.ds(pl.multiple_of(first + head * 128, 128), 128)
        return q_all[block * 2 : block * 2 + 2, :, cols].reshape(ROWS, 128)

    def scores(block, head):
        scaled = rows_of(block, head, 0).astype(jnp.float32).T * (FACTOR * LOG2E)
        high = scaled.astype(jnp.bfloat16)
        low = (scaled - high.astype(jnp.float32)).astype(jnp.bfloat16)
        q2t = jnp.concatenate([high, low], 0)
        top = None
        for keys, at in tiles(block):
            s = nn(key2[keys, :], q2t)
            if at.start == PROMPT_ROWS:
                own = base + block * ROWS
                row_pos = own + lax.broadcasted_iota(jnp.int32, (1, ROWS), 1)
                seg_start = jnp.zeros((1, ROWS), jnp.int32)
                end = jnp.int32(0)
                for j in range(16):
                    end = end + len_ref[j]
                    seg_start = jnp.maximum(seg_start, jnp.where(row_pos >= end, end, 0))
                key_pos = own - BACK + lax.broadcasted_iota(jnp.int32, (SPAN, ROWS), 0)
                s = jnp.where((key_pos <= row_pos) & (key_pos >= seg_start), s, NEGATIVE)
            s_refs[block][at, :] = s
            tile_top = jnp.max(s, axis=0, keepdims=True)
            top = tile_top if top is None else jnp.maximum(top, tile_top)
            yield top

    def weigh(block, head, top):
        total = jnp.zeros((144, ROWS), jnp.float32)
        for i, (keys, at) in enumerate(tiles(block)):
            p = jnp.exp2(s_refs[block][at, :] - top).astype(jnp.bfloat16)
            p_refs[block][at, :] = p
            total = total + nn(value_t[:, keys], p)
            if i < len(tiles(block)) - 1:
                yield
        inverse = 1.0 / total[128:129, :]
        out = (total[:128, :] * inverse).astype(jnp.bfloat16).astype(jnp.float32)
        cols = pl.ds(pl.multiple_of(head * 128, 128), 128)
        o_ref[block * 2 : block * 2 + 2, :, cols] = out.T.astype(jnp.bfloat16).reshape(2, 128, 128)
        grad_n = (rows_of(block, head, WIDE).astype(jnp.float32).T * inverse).astype(jnp.bfloat16)
        wide = grad_n.astype(jnp.float32)
        row_dot = -jnp.sum(wide * out, axis=0, keepdims=True)
        dot_high = row_dot.astype(jnp.bfloat16).astype(jnp.float32)
        line = lax.broadcasted_iota(jnp.int32, (128, ROWS), 0)
        extra = jnp.where(line == 0, dot_high, jnp.where(line == 1, row_dot - dot_high, 0.0))
        grad2_refs[block][:128, :] = grad_n
        grad2_refs[block][128:, :] = extra.astype(jnp.bfloat16)
        rows_refs[block][...] = wide.T.astype(jnp.bfloat16)
        yield

    def backward(block, head):
        q = rows_of(block, head, 0)
        dq = jnp.zeros((HEAD_DIM, ROWS), jnp.float32)
        for i, (keys, at) in enumerate(tiles(block)):
            p = p_refs[block][at, :]
            ds = (p.astype(jnp.float32) * nn(value1[keys, :], grad2_refs[block][...])).astype(jnp.bfloat16)
            dq = dq + nn(key_t[:, keys], ds)
            key_sum[keys, :] += nn(ds, q)
            value_sum[keys, :] += nn(p, rows_refs[block][...])
            if i < len(tiles(block)) - 1:
                yield
        cols = pl.ds(pl.multiple_of(WIDE + head * 128, 128), 128)
        dq = (dq * FACTOR).T.astype(jnp.bfloat16)
        o_ref[block * 2 : block * 2 + 2, :, cols] = dq.reshape(2, 128, 128)
        yield

    def beside(one, other):
        last = None
        for _, last in zip(one, other):
            pass
        return last

    def step(head, carry):
        top_first = beside(backward(1, jnp.maximum(head - 1, 0)), scores(0, head))
        top_second = beside(weigh(0, head, top_first), scores(1, head))
        beside(backward(0, head), weigh(1, head, top_second))
        return carry

    lax.fori_loop(0, PER_GROUP, step, 0)
    for _ in backward(1, PER_GROUP - 1):
        pass

    outs = [(i * 256, i * 256 + 256, ref) for i, ref in enumerate((g0, g1, g2, g3, g4, g5, g6, g7))]
    outs += [(PROMPT_ROWS, PROMPT_ROWS + BACK, back_grad_ref), (PROMPT_ROWS + BACK, all_rows, own_grad_ref)]
    for first, last, target in outs:
        target[:, :128] = key_sum[first:last, :] * FACTOR
        target[:, 128:] = value_sum[first:last, :]


def call(body, scalars, operands, outs, name, scratch=(), limit=24, cost=None, space=pltpu.VMEM, extra=(), passed={}):
    smem = pl.BlockSpec(memory_space=pltpu.SMEM)
    return pl.pallas_call(
        body,
        in_specs=[smem] * len(scalars) + [pl.BlockSpec(memory_space=space)] * len(operands)
        + [pl.BlockSpec(memory_space=pl.ANY)] * len(extra),
        out_specs=[
            pl.BlockSpec(memory_space=pl.ANY if i in passed.values() else pltpu.VMEM) for i in range(len(outs))
        ],
        input_output_aliases=passed,
        out_shape=[jax.ShapeDtypeStruct(shape, dtype) for shape, dtype in outs],
        scratch_shapes=list(scratch),
        compiler_params=pltpu.CompilerParams(vmem_limit_bytes=limit * 1024 * 1024),
        cost_estimate=cost,
        name=name,
    )(*scalars, *operands, *extra)


def attention(resp_len, where, operands):
    bf16, f32 = jnp.bfloat16, jnp.float32
    rows = PROMPT_ROWS + BACK + OWN_ROWS
    flops = 12 * 2560 * 2560 * 128
    return call(
        attention_kernel, (resp_len, where), operands,
        [((4, 128, 2 * WIDE), bf16)] + [((256, 256), f32)] * 8 + [((BACK, 256), f32), ((OWN_ROWS, 256), f32)],
        "attention",
        scratch=[
            pltpu.VMEM((rows, 256), bf16),
            pltpu.VMEM((rows, 256), bf16),
            pltpu.VMEM((128, rows), bf16),
            pltpu.VMEM((144, rows), bf16),
            pltpu.VMEM((PROMPT_ROWS + SPAN, ROWS), f32),
            pltpu.VMEM((PROMPT_ROWS + SPAN, ROWS), f32),
            pltpu.VMEM((PROMPT_ROWS + SPAN, ROWS), bf16),
            pltpu.VMEM((PROMPT_ROWS + SPAN, ROWS), bf16),
            pltpu.VMEM((256, ROWS), bf16),
            pltpu.VMEM((256, ROWS), bf16),
            pltpu.VMEM((ROWS, 128), bf16),
            pltpu.VMEM((ROWS, 128), bf16),
            pltpu.VMEM((rows, 128), f32),
            pltpu.VMEM((rows, 128), f32),
        ],
        limit=32,
        cost=pl.CostEstimate(flops=flops, bytes_accessed=8_000_000, transcendentals=flops // 1536),
    )


def head_columns(x, distance, width):
    return pl.ds(pl.multiple_of(lax.rem(x + distance, 4) * width, 128), width)


def pack_kernel(where_ref, pk, pv, k, v, q, g, s0, s1, s2, s3, rows, sems):
    pairs = []
    for d, target in enumerate((s0, s1, s2, s3)):
        cols = head_columns(where_ref[1], d, 128)
        for source, lines, lanes in ((pk, (0, 64), 0), (pv, (0, 64), 128), (k, (64, 192), 0), (v, (64, 192), 128)):
            pairs.append((source.at[:, cols], target.at[slice(*lines), lanes : lanes + 128]))
    for h in range(KV_HEADS):
        for source, first in ((q, 0), (g, WIDE)):
            pairs.append((source.at[:, h * WIDE : h * WIDE + WIDE], rows.at[h, :, first : first + WIDE]))
    copies = [pltpu.make_async_copy(source, target, sems.at[i]) for i, (source, target) in enumerate(pairs)]
    for copy in copies:
        copy.start()
    for copy in copies:
        copy.wait()


def collect_kernel(where_ref, s0, s1, s2, s3, rows_in, mine_ref, ahead_ref, rows_out):
    x = where_ref[1]
    for d, source in enumerate((s0, s1, s2, s3)):
        mine_ref[d * 64 : d * 64 + 64, :] = source[:64, :]
        block = lax.rem(x + 4 - d, 4)

        @pl.when(block > 0)
        def _():
            ahead_ref[pl.ds(pl.multiple_of((block - 1) * 128, 128), 128), :] = source[64:, :]


def final_sum_kernel(where_ref, n0, n1, n2, n3, got_ref, own_ref, back_ref, f0, f1, f2, f3):
    x = where_ref[1]
    for d, target in enumerate((f0, f1, f2, f3)):
        at = slice(d * 64, d * 64 + 64)
        total = (n0[at, :] + n1[at, :]) + (n2[at, :] + n3[at, :]) + got_ref[at, :]
        target[:64, :] = total.astype(jnp.bfloat16)
        block = lax.rem(x + 4 - d, 4)
        behind = pl.ds(pl.multiple_of(jnp.maximum(block - 1, 0) * 128, 128), 128)
        extra = jnp.where(block > 0, back_ref[behind, :], 0.0)
        target[64:, :] = (own_ref[block_at(x, d), :] + extra).astype(jnp.bfloat16)


def unpack_rows_kernel(o_ref, out_ref, dq_ref):
    for h in range(KV_HEADS):
        at = slice(h * WIDE, h * WIDE + WIDE)
        out_ref[:, at] = o_ref[h, :, :WIDE]
        dq_ref[:, at] = o_ref[h, :, WIDE:]


def unpack_small_kernel(where_ref, f0, f1, f2, f3, k_ref, v_ref, pk_ref, pv_ref):
    x = where_ref[1]
    for d, source in enumerate((f0, f1, f2, f3)):
        at = head_columns(x, d, 128)
        pk_ref[:, at] = source[:64, :128]
        pv_ref[:, at] = source[:64, 128:]
        k_ref[:, at] = source[64:, :128]
        v_ref[:, at] = source[64:, 128:]


def along_x(value, step):
    return lax.ppermute(value, "seq", [(i, i // 4 * 4 + (i + step) % 4) for i in range(32)])


def exchange_x(value):
    return lax.all_to_all(value, "seq", 0, 0, axis_index_groups=X_GROUPS, tiled=True)


def along_y(value, step):
    return lax.ppermute(value, "seq", [(i, i // 16 * 16 + (i + 4 * step) % 16) for i in range(32)])


def along_z(value):
    return lax.ppermute(value, "seq", [(i, (i + 16) % 32) for i in range(32)])


def along_rows(value, step):
    pairs = [(i, i + 4 * step) for i in range(32)]
    return lax.ppermute(value, "seq", [(i, j) for i, j in pairs if 0 <= j < 32])


def local(resp_len, prompt_keys, prompt_values, resp_q, resp_k, resp_v, out_grad):
    me = lax.axis_index("seq").astype(jnp.int32)
    where = jnp.stack([me // 4 * OWN_ROWS, me % 4])
    rows, bf16, f32 = resp_q.shape[0], jnp.bfloat16, jnp.float32

    *s, q_all = call(
        pack_kernel, (where,), (prompt_keys, prompt_values, resp_k, resp_v, resp_q, out_grad),
        [((192, 256), bf16)] * 4 + [((4, rows, 2 * WIDE), bf16)], "pack",
        scratch=[pltpu.SemaphoreType.DMA((24,))], space=pl.ANY, limit=60,
    )
    s = [s[0]] + [along_x(s[d], d) for d in (1, 2, 3)]
    mine, ahead, q_all = call(
        collect_kernel, (where,), s, [((256, 256), bf16), ((BACK, 256), bf16), (q_all.shape, bf16)], "collect",
        extra=(q_all,), passed={5: 2},
    )
    q_all = exchange_x(q_all)
    far = along_z(mine)
    near_keys = [mine] + [along_y(mine, d) for d in (1, 2, 3)]
    before = along_rows(ahead, 1)
    far_keys = [far] + [along_y(far, d) for d in (1, 2, 3)]

    o, h2, h1, h0, h3, l2, l1, l0, l3, back_grad, own_grad = attention(
        resp_len, where, (q_all, *s, before, *far_keys, *near_keys)
    )

    through, minus = along_y(h2, 1), along_y(h1, -1)
    plus = along_y(h3 + through, 1)
    got = along_z(h0 + minus + plus)
    one, two, three = along_y(l1, -1), along_y(l2, -2), along_y(l3, 1)
    back = along_rows(back_grad, -1)

    attn_out, q_grad = call(
        unpack_rows_kernel, (), (exchange_x(o),), [((rows, HEADS * HEAD_DIM), bf16)] * 2, "unpack_rows"
    )

    f = call(
        final_sum_kernel, (where,), (l0, one, two, three, got, own_grad, back),
        [((192, 256), bf16)] * 4, "final_sum",
    )
    f = [f[0]] + [along_x(f[d], -d) for d in (1, 2, 3)]
    resp_k_grad, resp_v_grad, prompt_k_grad, prompt_v_grad = call(
        unpack_small_kernel, (where,), f, [((rows, 512), bf16)] * 2 + [((64, 512), bf16)] * 2, "unpack_small"
    )
    return attn_out, q_grad, resp_k_grad, resp_v_grad, prompt_k_grad, prompt_v_grad


def solution(mesh):
    split = P(("grp", "seq"), None)
    return jax.shard_map(
        local,
        mesh=mesh,
        in_specs=(P("grp"),) + (split,) * 6,
        out_specs=(split,) * 6,
        check_vma=False,
    )
```

```python
import jax
import jax.numpy as jnp
from jax import lax
from jax.experimental import pallas as pl
from jax.experimental.pallas import tpu as pltpu
from jax.sharding import PartitionSpec as P

HEADS = 20
KV_HEADS = 4
HEAD_DIM = 128
PER_GROUP = HEADS // KV_HEADS
BACK = 384
NEGATIVE = -1e30
LOG2E = 1.4426950408889634
FACTOR = HEAD_DIM ** (-0.5)

X_GROUPS = [[first + x for x in range(4)] for first in range(0, 32, 4)]
ROWS = 256
KEYS = 1024
SPAN = 640
PROMPT_ROWS = 2048
OWN_ROWS = 512
WIDE = PER_GROUP * HEAD_DIM


def nt(a, b):
    return lax.dot_general(a, b, (((1,), (1,)), ((), ())), preferred_element_type=jnp.float32)


def nn(a, b):
    return lax.dot_general(a, b, (((1,), (0,)), ((), ())), preferred_element_type=jnp.float32)


def block_at(x, distance):
    return pl.ds(pl.multiple_of(lax.rem(x + 4 - distance, 4) * 128, 128), 128)


def attention_kernel(
    len_ref, where_ref, q_in, s0, s1, s2, s3, before_in, h0, h1, h2, h3, l0, l1, l2, l3,
    o_ref, g0, g1, g2, g3, g4, g5, g6, g7, back_grad_ref, own_grad_ref,
    key2, value1, key_t, value_t, s_first, s_second, p_first, p_second,
    grad2_first, grad2_second, rows_first, rows_second, key_sum, value_sum, q_all, staged, sems,
):
    base, x = where_ref[0], where_ref[1]
    all_rows = PROMPT_ROWS + BACK + OWN_ROWS

    def place(at, source):
        key2[at, :128] = source[:, :128]
        key2[at, 128:] = source[:, :128]
        value1[at, :128] = source[:, 128:]

    copies = []

    def load(source, target):
        copies.append(pltpu.make_async_copy(source, target, sems.at[len(copies)]))
        copies[-1].start()

    for i, source in enumerate((h2, h1, h0, h3, l2, l1, l0, l3)):
        load(source, staged.at[i * 256 : i * 256 + 256, :])
    load(before_in, staged.at[PROMPT_ROWS : PROMPT_ROWS + BACK, :])
    for d, source in enumerate((s0, s1, s2, s3)):
        first = PROMPT_ROWS + BACK + lax.rem(x + 4 - d, 4) * 128
        load(source.at[64:192, :], staged.at[pl.ds(pl.multiple_of(first, 128), 128), :])
    load(q_in, q_all)
    for copy in copies:
        copy.wait()
    place(slice(0, all_rows), staged)
    value1[:, 128:] = jnp.ones((all_rows, 128), jnp.bfloat16)
    value_t[128:, :] = jnp.ones((16, all_rows), jnp.bfloat16)
    for c in range(0, all_rows, 128):
        at = slice(c, c + 128)
        key_t[:, at] = key2[at, :128].astype(jnp.float32).T.astype(jnp.bfloat16)
        value_t[:128, at] = value1[at, :128].astype(jnp.float32).T.astype(jnp.bfloat16)
    for ref in (key_sum, value_sum, p_second, grad2_second, rows_second):
        ref[...] = jnp.zeros_like(ref)

    s_refs, p_refs = (s_first, s_second), (p_first, p_second)
    grad2_refs, rows_refs = (grad2_first, grad2_second), (rows_first, rows_second)

    def tiles(block):
        span = PROMPT_ROWS + block * ROWS
        out = [(c, c, KEYS) for c in range(0, PROMPT_ROWS, KEYS)] + [(span, PROMPT_ROWS, SPAN)]
        return [(slice(keys, keys + size), slice(at, at + size)) for keys, at, size in out]

    def rows_of(block, head, first):
        cols = pl.ds(pl.multiple_of(first + head * 128, 128), 128)
        return q_all[block * 2 : block * 2 + 2, :, cols].reshape(ROWS, 128)

    def scores(block, head):
        scaled = rows_of(block, head, 0).astype(jnp.float32).T * (FACTOR * LOG2E)
        high = scaled.astype(jnp.bfloat16)
        low = (scaled - high.astype(jnp.float32)).astype(jnp.bfloat16)
        q2t = jnp.concatenate([high, low], 0)
        top = None
        for keys, at in tiles(block):
            s = nn(key2[keys, :], q2t)
            if at.start == PROMPT_ROWS:
                own = base + block * ROWS
                row_pos = own + lax.broadcasted_iota(jnp.int32, (1, ROWS), 1)
                seg_start = jnp.zeros((1, ROWS), jnp.int32)
                end = jnp.int32(0)
                for j in range(16):
                    end = end + len_ref[j]
                    seg_start = jnp.maximum(seg_start, jnp.where(row_pos >= end, end, 0))
                key_pos = own - BACK + lax.broadcasted_iota(jnp.int32, (SPAN, ROWS), 0)
                s = jnp.where((key_pos <= row_pos) & (key_pos >= seg_start), s, NEGATIVE)
            s_refs[block][at, :] = s
            tile_top = jnp.max(s, axis=0, keepdims=True)
            top = tile_top if top is None else jnp.maximum(top, tile_top)
            yield top

    def weigh(block, head, top):
        total = jnp.zeros((144, ROWS), jnp.float32)
        for i, (keys, at) in enumerate(tiles(block)):
            p = jnp.exp2(s_refs[block][at, :] - top).astype(jnp.bfloat16)
            p_refs[block][at, :] = p
            total = total + nn(value_t[:, keys], p)
            if i < len(tiles(block)) - 1:
                yield
        inverse = 1.0 / total[128:129, :]
        out = (total[:128, :] * inverse).astype(jnp.bfloat16).astype(jnp.float32)
        cols = pl.ds(pl.multiple_of(head * 128, 128), 128)
        o_ref[block * 2 : block * 2 + 2, :, cols] = out.T.astype(jnp.bfloat16).reshape(2, 128, 128)
        grad_n = (rows_of(block, head, WIDE).astype(jnp.float32).T * inverse).astype(jnp.bfloat16)
        wide = grad_n.astype(jnp.float32)
        row_dot = -jnp.sum(wide * out, axis=0, keepdims=True)
        dot_high = row_dot.astype(jnp.bfloat16).astype(jnp.float32)
        line = lax.broadcasted_iota(jnp.int32, (128, ROWS), 0)
        extra = jnp.where(line == 0, dot_high, jnp.where(line == 1, row_dot - dot_high, 0.0))
        grad2_refs[block][:128, :] = grad_n
        grad2_refs[block][128:, :] = extra.astype(jnp.bfloat16)
        rows_refs[block][...] = wide.T.astype(jnp.bfloat16)
        yield

    def backward(block, head):
        q = rows_of(block, head, 0)
        dq = jnp.zeros((HEAD_DIM, ROWS), jnp.float32)
        for i, (keys, at) in enumerate(tiles(block)):
            p = p_refs[block][at, :]
            ds = (p.astype(jnp.float32) * nn(value1[keys, :], grad2_refs[block][...])).astype(jnp.bfloat16)
            dq = dq + nn(key_t[:, keys], ds)
            key_sum[keys, :] += nn(ds, q)
            value_sum[keys, :] += nn(p, rows_refs[block][...])
            if i < len(tiles(block)) - 1:
                yield
        cols = pl.ds(pl.multiple_of(WIDE + head * 128, 128), 128)
        dq = (dq * FACTOR).T.astype(jnp.bfloat16)
        o_ref[block * 2 : block * 2 + 2, :, cols] = dq.reshape(2, 128, 128)
        yield

    def beside(one, other):
        last = None
        for _, last in zip(one, other):
            pass
        return last

    def step(head, carry):
        top_first = beside(backward(1, jnp.maximum(head - 1, 0)), scores(0, head))
        top_second = beside(weigh(0, head, top_first), scores(1, head))
        beside(backward(0, head), weigh(1, head, top_second))
        return carry

    lax.fori_loop(0, PER_GROUP, step, 0)
    for _ in backward(1, PER_GROUP - 1):
        pass

    outs = [(i * 256, i * 256 + 256, ref) for i, ref in enumerate((g0, g1, g2, g3, g4, g5, g6, g7))]
    outs += [(PROMPT_ROWS, PROMPT_ROWS + BACK, back_grad_ref), (PROMPT_ROWS + BACK, all_rows, own_grad_ref)]
    for first, last, target in outs:
        target[:, :128] = key_sum[first:last, :] * FACTOR
        target[:, 128:] = value_sum[first:last, :]


def call(body, scalars, operands, outs, name, scratch=(), limit=24, cost=None, space=pltpu.VMEM, extra=()):
    smem = pl.BlockSpec(memory_space=pltpu.SMEM)
    return pl.pallas_call(
        body,
        in_specs=[smem] * len(scalars) + [pl.BlockSpec(memory_space=space)] * len(operands)
        + [pl.BlockSpec(memory_space=pl.ANY)] * len(extra),
        out_specs=[pl.BlockSpec(memory_space=pltpu.VMEM)] * len(outs),
        out_shape=[jax.ShapeDtypeStruct(shape, dtype) for shape, dtype in outs],
        scratch_shapes=list(scratch),
        compiler_params=pltpu.CompilerParams(vmem_limit_bytes=limit * 1024 * 1024),
        cost_estimate=cost,
        name=name,
    )(*scalars, *operands, *extra)


def attention(resp_len, where, operands):
    bf16, f32 = jnp.bfloat16, jnp.float32
    rows = PROMPT_ROWS + BACK + OWN_ROWS
    flops = 12 * 2560 * 2560 * 128
    return call(
        attention_kernel, (resp_len, where), operands,
        [((4, 128, 2 * WIDE), bf16)] + [((256, 256), f32)] * 8 + [((BACK, 256), f32), ((OWN_ROWS, 256), f32)],
        "attention",
        scratch=[
            pltpu.VMEM((rows, 256), bf16),
            pltpu.VMEM((rows, 256), bf16),
            pltpu.VMEM((128, rows), bf16),
            pltpu.VMEM((144, rows), bf16),
            pltpu.VMEM((PROMPT_ROWS + SPAN, ROWS), f32),
            pltpu.VMEM((PROMPT_ROWS + SPAN, ROWS), f32),
            pltpu.VMEM((PROMPT_ROWS + SPAN, ROWS), bf16),
            pltpu.VMEM((PROMPT_ROWS + SPAN, ROWS), bf16),
            pltpu.VMEM((256, ROWS), bf16),
            pltpu.VMEM((256, ROWS), bf16),
            pltpu.VMEM((ROWS, 128), bf16),
            pltpu.VMEM((ROWS, 128), bf16),
            pltpu.VMEM((rows, 128), f32),
            pltpu.VMEM((rows, 128), f32),
            pltpu.VMEM((4, 128, 2 * WIDE), bf16),
            pltpu.VMEM((rows, 256), bf16),
            pltpu.SemaphoreType.DMA((14,)),
        ],
        space=pl.ANY, limit=60,
        cost=pl.CostEstimate(flops=flops, bytes_accessed=8_000_000, transcendentals=flops // 1536),
    )


def head_columns(x, distance, width):
    return pl.ds(pl.multiple_of(lax.rem(x + distance, 4) * width, 128), width)


def pack_kernel(where_ref, pk, pv, k, v, q, g, s0, s1, s2, s3, rows, sems):
    pairs = []
    for d, target in enumerate((s0, s1, s2, s3)):
        cols = head_columns(where_ref[1], d, 128)
        for source, lines, lanes in ((pk, (0, 64), 0), (pv, (0, 64), 128), (k, (64, 192), 0), (v, (64, 192), 128)):
            pairs.append((source.at[:, cols], target.at[slice(*lines), lanes : lanes + 128]))
    for h in range(KV_HEADS):
        for source, first in ((q, 0), (g, WIDE)):
            pairs.append((source.at[:, h * WIDE : h * WIDE + WIDE], rows.at[h, :, first : first + WIDE]))
    copies = [pltpu.make_async_copy(source, target, sems.at[i]) for i, (source, target) in enumerate(pairs)]
    for copy in copies:
        copy.start()
    for copy in copies:
        copy.wait()


def collect_kernel(where_ref, s0, s1, s2, s3, mine_ref, ahead_ref):
    x = where_ref[1]
    for d, source in enumerate((s0, s1, s2, s3)):
        mine_ref[d * 64 : d * 64 + 64, :] = source[:64, :]
        block = lax.rem(x + 4 - d, 4)

        @pl.when(block > 0)
        def _():
            ahead_ref[pl.ds(pl.multiple_of((block - 1) * 128, 128), 128), :] = source[64:, :]


def final_sum_kernel(where_ref, n0, n1, n2, n3, got_ref, own_ref, back_ref, f0, f1, f2, f3):
    x = where_ref[1]
    for d, target in enumerate((f0, f1, f2, f3)):
        at = slice(d * 64, d * 64 + 64)
        total = (n0[at, :] + n1[at, :]) + (n2[at, :] + n3[at, :]) + got_ref[at, :]
        target[:64, :] = total.astype(jnp.bfloat16)
        block = lax.rem(x + 4 - d, 4)
        behind = pl.ds(pl.multiple_of(jnp.maximum(block - 1, 0) * 128, 128), 128)
        extra = jnp.where(block > 0, back_ref[behind, :], 0.0)
        target[64:, :] = (own_ref[block_at(x, d), :] + extra).astype(jnp.bfloat16)


def far_sum_kernel(a, b, c, after, out_ref):
    out_ref[...] = a[...] + b[...] + c[...]


def unpack_rows_kernel(o_ref, out_ref, dq_ref):
    for h in range(KV_HEADS):
        at = slice(h * WIDE, h * WIDE + WIDE)
        out_ref[:, at] = o_ref[h, :, :WIDE]
        dq_ref[:, at] = o_ref[h, :, WIDE:]


def unpack_small_kernel(where_ref, f0, f1, f2, f3, k_ref, v_ref, pk_ref, pv_ref):
    x = where_ref[1]
    for d, source in enumerate((f0, f1, f2, f3)):
        at = head_columns(x, d, 128)
        pk_ref[:, at] = source[:64, :128]
        pv_ref[:, at] = source[:64, 128:]
        k_ref[:, at] = source[64:, :128]
        v_ref[:, at] = source[64:, 128:]


def along_x(value, step):
    return lax.ppermute(value, "seq", [(i, i // 4 * 4 + (i + step) % 4) for i in range(32)])


def exchange_x(value):
    return lax.all_to_all(value, "seq", 0, 0, axis_index_groups=X_GROUPS, tiled=True)


def along_y(value, step):
    return lax.ppermute(value, "seq", [(i, i // 16 * 16 + (i + 4 * step) % 16) for i in range(32)])


def along_z(value):
    return lax.ppermute(value, "seq", [(i, (i + 16) % 32) for i in range(32)])


def along_rows(value, step):
    pairs = [(i, i + 4 * step) for i in range(32)]
    return lax.ppermute(value, "seq", [(i, j) for i, j in pairs if 0 <= j < 32])


def local(resp_len, prompt_keys, prompt_values, resp_q, resp_k, resp_v, out_grad):
    me = lax.axis_index("seq").astype(jnp.int32)
    where = jnp.stack([me // 4 * OWN_ROWS, me % 4])
    rows, bf16, f32 = resp_q.shape[0], jnp.bfloat16, jnp.float32

    *s, q_all = call(
        pack_kernel, (where,), (prompt_keys, prompt_values, resp_k, resp_v, resp_q, out_grad),
        [((192, 256), bf16)] * 4 + [((4, rows, 2 * WIDE), bf16)], "pack",
        scratch=[pltpu.SemaphoreType.DMA((24,))], space=pl.ANY, limit=60,
    )
    s = [s[0]] + [along_x(s[d], d) for d in (1, 2, 3)]
    *s, q_all = lax.optimization_barrier((*s, q_all))
    q_all = exchange_x(q_all)
    mine, ahead = call(collect_kernel, (where,), s, [((256, 256), bf16), ((BACK, 256), bf16)], "collect")
    far = along_z(mine)
    near_keys = [mine] + [along_y(mine, d) for d in (1, 2, 3)]
    before = along_rows(ahead, 1)
    far_keys = [far] + [along_y(far, d) for d in (1, 2, 3)]

    o, h2, h1, h0, h3, l2, l1, l0, l3, back_grad, own_grad = attention(
        resp_len, where, (q_all, *s, before, *far_keys, *near_keys)
    )

    through, minus = along_y(h2, 1), along_y(h1, -1)
    plus = along_y(h3 + through, 1)
    back = along_rows(back_grad, -1)
    (got,) = call(far_sum_kernel, (), (h0, minus, plus), [((256, 256), f32)], "far_sum", extra=(back,))
    got = along_z(got)
    one, two, three = along_y(l1, -1), along_y(l2, -2), along_y(l3, 1)

    attn_out, q_grad = call(
        unpack_rows_kernel, (), (exchange_x(o),), [((rows, HEADS * HEAD_DIM), bf16)] * 2, "unpack_rows"
    )

    f = call(
        final_sum_kernel, (where,), (l0, one, two, three, got, own_grad, back),
        [((192, 256), bf16)] * 4, "final_sum",
    )
    f = [f[0]] + [along_x(f[d], -d) for d in (1, 2, 3)]
    resp_k_grad, resp_v_grad, prompt_k_grad, prompt_v_grad = call(
        unpack_small_kernel, (where,), f, [((rows, 512), bf16)] * 2 + [((64, 512), bf16)] * 2, "unpack_small"
    )
    return attn_out, q_grad, resp_k_grad, resp_v_grad, prompt_k_grad, prompt_v_grad


def solution(mesh):
    split = P(("grp", "seq"), None)
    return jax.shard_map(
        local,
        mesh=mesh,
        in_specs=(P("grp"),) + (split,) * 6,
        out_specs=(split,) * 6,
        check_vma=False,
    )
```

```python
import jax
import jax.numpy as jnp
from jax import lax
from jax.experimental import pallas as pl
from jax.experimental.pallas import tpu as pltpu
from jax.sharding import PartitionSpec as P

HEADS = 20
KV_HEADS = 4
HEAD_DIM = 128
PER_GROUP = HEADS // KV_HEADS
BACK = 384
NEGATIVE = -1e30
LOG2E = 1.4426950408889634
FACTOR = HEAD_DIM ** (-0.5)

X_GROUPS = [[first + x for x in range(4)] for first in range(0, 32, 4)]
ROWS = 256
KEYS = 1024
SPAN = 640
PROMPT_ROWS = 2048
OWN_ROWS = 512
WIDE = PER_GROUP * HEAD_DIM


def nt(a, b):
    return lax.dot_general(a, b, (((1,), (1,)), ((), ())), preferred_element_type=jnp.float32)


def nn(a, b):
    return lax.dot_general(a, b, (((1,), (0,)), ((), ())), preferred_element_type=jnp.float32)


def block_at(x, distance):
    return pl.ds(pl.multiple_of(lax.rem(x + 4 - distance, 4) * 128, 128), 128)


def attention_kernel(
    len_ref, where_ref, q_in, s0, s1, s2, s3, before_in, h0, h1, h2, h3, l0, l1, l2, l3,
    o_ref, g0, g1, g2, g3, g4, g5, g6, g7, back_grad_ref, own_grad_ref,
    key2, value1, key_t, value_t, s_first, s_second, p_first, p_second,
    grad2_first, grad2_second, rows_first, rows_second, key_sum, value_sum, q_all, staged, sems,
):
    base, x = where_ref[0], where_ref[1]
    all_rows = PROMPT_ROWS + BACK + OWN_ROWS

    def place(at, source):
        key2[at, :128] = source[:, :128]
        key2[at, 128:] = source[:, :128]
        value1[at, :128] = source[:, 128:]

    copies = []

    def load(source, target):
        copies.append(pltpu.make_async_copy(source, target, sems.at[len(copies)]))
        copies[-1].start()

    for i, source in enumerate((h2, h1, h0, h3, l2, l1, l0, l3)):
        load(source, staged.at[i * 256 : i * 256 + 256, :])
    load(before_in, staged.at[PROMPT_ROWS : PROMPT_ROWS + BACK, :])
    for d, source in enumerate((s0, s1, s2, s3)):
        first = PROMPT_ROWS + BACK + lax.rem(x + 4 - d, 4) * 128
        load(source.at[64:192, :], staged.at[pl.ds(pl.multiple_of(first, 128), 128), :])
    load(q_in, q_all)
    for copy in copies:
        copy.wait()
    place(slice(0, all_rows), staged)
    value1[:, 128:] = jnp.ones((all_rows, 128), jnp.bfloat16)
    value_t[128:, :] = jnp.ones((16, all_rows), jnp.bfloat16)
    for c in range(0, all_rows, 128):
        at = slice(c, c + 128)
        key_t[:, at] = key2[at, :128].astype(jnp.float32).T.astype(jnp.bfloat16)
        value_t[:128, at] = value1[at, :128].astype(jnp.float32).T.astype(jnp.bfloat16)
    for ref in (key_sum, value_sum, p_second, grad2_second, rows_second):
        ref[...] = jnp.zeros_like(ref)

    s_refs, p_refs = (s_first, s_second), (p_first, p_second)
    grad2_refs, rows_refs = (grad2_first, grad2_second), (rows_first, rows_second)

    def tiles(block):
        span = PROMPT_ROWS + block * ROWS
        out = [(c, c, KEYS) for c in range(0, PROMPT_ROWS, KEYS)] + [(span, PROMPT_ROWS, SPAN)]
        return [(slice(keys, keys + size), slice(at, at + size)) for keys, at, size in out]

    def rows_of(block, head, first):
        cols = pl.ds(pl.multiple_of(first + head * 128, 128), 128)
        return q_all[block * 2 : block * 2 + 2, :, cols].reshape(ROWS, 128)

    def scores(block, head):
        scaled = rows_of(block, head, 0).astype(jnp.float32).T * (FACTOR * LOG2E)
        high = scaled.astype(jnp.bfloat16)
        low = (scaled - high.astype(jnp.float32)).astype(jnp.bfloat16)
        q2t = jnp.concatenate([high, low], 0)
        top = None
        for keys, at in tiles(block):
            s = nn(key2[keys, :], q2t)
            if at.start == PROMPT_ROWS:
                own = base + block * ROWS
                row_pos = own + lax.broadcasted_iota(jnp.int32, (1, ROWS), 1)
                seg_start = jnp.zeros((1, ROWS), jnp.int32)
                end = jnp.int32(0)
                for j in range(16):
                    end = end + len_ref[j]
                    seg_start = jnp.maximum(seg_start, jnp.where(row_pos >= end, end, 0))
                key_pos = own - BACK + lax.broadcasted_iota(jnp.int32, (SPAN, ROWS), 0)
                s = jnp.where((key_pos <= row_pos) & (key_pos >= seg_start), s, NEGATIVE)
            s_refs[block][at, :] = s
            tile_top = jnp.max(s, axis=0, keepdims=True)
            top = tile_top if top is None else jnp.maximum(top, tile_top)
            yield top

    def weigh(block, head, top):
        total = jnp.zeros((144, ROWS), jnp.float32)
        for i, (keys, at) in enumerate(tiles(block)):
            p = jnp.exp2(s_refs[block][at, :] - top).astype(jnp.bfloat16)
            p_refs[block][at, :] = p
            total = total + nn(value_t[:, keys], p)
            if i < len(tiles(block)) - 1:
                yield
        inverse = 1.0 / total[128:129, :]
        out = (total[:128, :] * inverse).astype(jnp.bfloat16).astype(jnp.float32)
        cols = pl.ds(pl.multiple_of(head * 128, 128), 128)
        o_ref[block * 2 : block * 2 + 2, :, cols] = out.T.astype(jnp.bfloat16).reshape(2, 128, 128)
        grad_n = (rows_of(block, head, WIDE).astype(jnp.float32).T * inverse).astype(jnp.bfloat16)
        wide = grad_n.astype(jnp.float32)
        row_dot = -jnp.sum(wide * out, axis=0, keepdims=True)
        dot_high = row_dot.astype(jnp.bfloat16).astype(jnp.float32)
        line = lax.broadcasted_iota(jnp.int32, (128, ROWS), 0)
        extra = jnp.where(line == 0, dot_high, jnp.where(line == 1, row_dot - dot_high, 0.0))
        grad2_refs[block][:128, :] = grad_n
        grad2_refs[block][128:, :] = extra.astype(jnp.bfloat16)
        rows_refs[block][...] = wide.T.astype(jnp.bfloat16)
        yield

    def backward(block, head):
        q = rows_of(block, head, 0)
        dq = jnp.zeros((HEAD_DIM, ROWS), jnp.float32)
        for i, (keys, at) in enumerate(tiles(block)):
            p = p_refs[block][at, :]
            ds = (p.astype(jnp.float32) * nn(value1[keys, :], grad2_refs[block][...])).astype(jnp.bfloat16)
            dq = dq + nn(key_t[:, keys], ds)
            key_sum[keys, :] += nn(ds, q)
            value_sum[keys, :] += nn(p, rows_refs[block][...])
            if i < len(tiles(block)) - 1:
                yield
        cols = pl.ds(pl.multiple_of(WIDE + head * 128, 128), 128)
        dq = (dq * FACTOR).T.astype(jnp.bfloat16)
        o_ref[block * 2 : block * 2 + 2, :, cols] = dq.reshape(2, 128, 128)
        yield

    def beside(one, other):
        last = None
        for _, last in zip(one, other):
            pass
        return last

    def step(head, carry):
        top_first = beside(backward(1, jnp.maximum(head - 1, 0)), scores(0, head))
        top_second = beside(weigh(0, head, top_first), scores(1, head))
        beside(backward(0, head), weigh(1, head, top_second))
        return carry

    lax.fori_loop(0, PER_GROUP, step, 0)
    for _ in backward(1, PER_GROUP - 1):
        pass

    outs = [(i * 256, i * 256 + 256, ref) for i, ref in enumerate((g0, g1, g2, g3, g4, g5, g6, g7))]
    outs += [(PROMPT_ROWS, PROMPT_ROWS + BACK, back_grad_ref), (PROMPT_ROWS + BACK, all_rows, own_grad_ref)]
    for first, last, target in outs:
        target[:, :128] = key_sum[first:last, :] * FACTOR
        target[:, 128:] = value_sum[first:last, :]


def call(body, scalars, operands, outs, name, scratch=(), limit=24, cost=None, space=pltpu.VMEM, extra=()):
    smem = pl.BlockSpec(memory_space=pltpu.SMEM)
    return pl.pallas_call(
        body,
        in_specs=[smem] * len(scalars) + [pl.BlockSpec(memory_space=space)] * len(operands)
        + [pl.BlockSpec(memory_space=pl.ANY)] * len(extra),
        out_specs=[pl.BlockSpec(memory_space=pltpu.VMEM)] * len(outs),
        out_shape=[jax.ShapeDtypeStruct(shape, dtype) for shape, dtype in outs],
        scratch_shapes=list(scratch),
        compiler_params=pltpu.CompilerParams(vmem_limit_bytes=limit * 1024 * 1024),
        cost_estimate=cost,
        name=name,
    )(*scalars, *operands, *extra)


def attention(resp_len, where, operands):
    bf16, f32 = jnp.bfloat16, jnp.float32
    rows = PROMPT_ROWS + BACK + OWN_ROWS
    flops = 12 * 2560 * 2560 * 128
    return call(
        attention_kernel, (resp_len, where), operands,
        [((4, 128, 2 * WIDE), bf16)] + [((256, 256), f32)] * 8 + [((BACK, 256), f32), ((OWN_ROWS, 256), f32)],
        "attention",
        scratch=[
            pltpu.VMEM((rows, 256), bf16),
            pltpu.VMEM((rows, 256), bf16),
            pltpu.VMEM((128, rows), bf16),
            pltpu.VMEM((144, rows), bf16),
            pltpu.VMEM((PROMPT_ROWS + SPAN, ROWS), f32),
            pltpu.VMEM((PROMPT_ROWS + SPAN, ROWS), f32),
            pltpu.VMEM((PROMPT_ROWS + SPAN, ROWS), bf16),
            pltpu.VMEM((PROMPT_ROWS + SPAN, ROWS), bf16),
            pltpu.VMEM((256, ROWS), bf16),
            pltpu.VMEM((256, ROWS), bf16),
            pltpu.VMEM((ROWS, 128), bf16),
            pltpu.VMEM((ROWS, 128), bf16),
            pltpu.VMEM((rows, 128), f32),
            pltpu.VMEM((rows, 128), f32),
            pltpu.VMEM((4, 128, 2 * WIDE), bf16),
            pltpu.VMEM((rows, 256), bf16),
            pltpu.SemaphoreType.DMA((14,)),
        ],
        space=pl.ANY, limit=60,
        cost=pl.CostEstimate(flops=flops, bytes_accessed=8_000_000, transcendentals=flops // 1536),
    )


def head_columns(x, distance, width):
    return pl.ds(pl.multiple_of(lax.rem(x + distance, 4) * width, 128), width)


def pack_kernel(where_ref, pk, pv, k, v, q, g, s0, s1, s2, s3, rows, sems):
    pairs = []
    for d, target in enumerate((s0, s1, s2, s3)):
        cols = head_columns(where_ref[1], d, 128)
        for source, lines, lanes in ((pk, (0, 64), 0), (pv, (0, 64), 128), (k, (64, 192), 0), (v, (64, 192), 128)):
            pairs.append((source.at[:, cols], target.at[slice(*lines), lanes : lanes + 128]))
    for h in range(KV_HEADS):
        for source, first in ((q, 0), (g, WIDE)):
            pairs.append((source.at[:, h * WIDE : h * WIDE + WIDE], rows.at[h, :, first : first + WIDE]))
    copies = [pltpu.make_async_copy(source, target, sems.at[i]) for i, (source, target) in enumerate(pairs)]
    for copy in copies:
        copy.start()
    for copy in copies:
        copy.wait()


def collect_kernel(where_ref, s0, s1, s2, s3, mine_ref, ahead_ref):
    x = where_ref[1]
    for d, source in enumerate((s0, s1, s2, s3)):
        mine_ref[d * 64 : d * 64 + 64, :] = source[:64, :]
        block = lax.rem(x + 4 - d, 4)

        @pl.when(block > 0)
        def _():
            ahead_ref[pl.ds(pl.multiple_of((block - 1) * 128, 128), 128), :] = source[64:, :]


def final_sum_kernel(where_ref, n0, n1, n2, n3, got_ref, own_ref, crossing_ref, within_ref, f0, f1, f2, f3):
    x = where_ref[1]
    for d, target in enumerate((f0, f1, f2, f3)):
        at = slice(d * 64, d * 64 + 64)
        total = (n0[at, :] + n1[at, :]) + (n2[at, :] + n3[at, :]) + got_ref[at, :]
        target[:64, :] = total.astype(jnp.bfloat16)
        block = lax.rem(x + 4 - d, 4)
        behind = pl.ds(pl.multiple_of(jnp.maximum(block - 1, 0) * 128, 128), 128)
        extra = jnp.where(block > 0, crossing_ref[behind, :] + within_ref[behind, :], 0.0)
        target[64:, :] = (own_ref[block_at(x, d), :] + extra).astype(jnp.bfloat16)


def far_sum_kernel(a, b, c, after, out_ref):
    out_ref[...] = a[...] + b[...] + c[...]


def unpack_rows_kernel(o_ref, out_ref, dq_ref):
    for h in range(KV_HEADS):
        at = slice(h * WIDE, h * WIDE + WIDE)
        out_ref[:, at] = o_ref[h, :, :WIDE]
        dq_ref[:, at] = o_ref[h, :, WIDE:]


def unpack_small_kernel(where_ref, f0, f1, f2, f3, k_ref, v_ref, pk_ref, pv_ref):
    x = where_ref[1]
    for d, source in enumerate((f0, f1, f2, f3)):
        at = head_columns(x, d, 128)
        pk_ref[:, at] = source[:64, :128]
        pv_ref[:, at] = source[:64, 128:]
        k_ref[:, at] = source[64:, :128]
        v_ref[:, at] = source[64:, 128:]


def along_x(value, step):
    return lax.ppermute(value, "seq", [(i, i // 4 * 4 + (i + step) % 4) for i in range(32)])


def exchange_x(value):
    return lax.all_to_all(value, "seq", 0, 0, axis_index_groups=X_GROUPS, tiled=True)


def along_y(value, step):
    return lax.ppermute(value, "seq", [(i, i // 16 * 16 + (i + 4 * step) % 16) for i in range(32)])


def along_z(value):
    return lax.ppermute(value, "seq", [(i, (i + 16) % 32) for i in range(32)])


def along_rows(value, step):
    pairs = [(i, i + 4 * step) for i in range(32)]
    return lax.ppermute(value, "seq", [(i, j) for i, j in pairs if 0 <= j < 32])


def local(resp_len, prompt_keys, prompt_values, resp_q, resp_k, resp_v, out_grad):
    me = lax.axis_index("seq").astype(jnp.int32)
    where = jnp.stack([me // 4 * OWN_ROWS, me % 4])
    rows, bf16, f32 = resp_q.shape[0], jnp.bfloat16, jnp.float32

    *s, q_all = call(
        pack_kernel, (where,), (prompt_keys, prompt_values, resp_k, resp_v, resp_q, out_grad),
        [((192, 256), bf16)] * 4 + [((4, rows, 2 * WIDE), bf16)], "pack",
        scratch=[pltpu.SemaphoreType.DMA((24,))], space=pl.ANY, limit=60,
    )
    s = [s[0]] + [along_x(s[d], d) for d in (1, 2, 3)]
    mine, ahead = call(collect_kernel, (where,), s, [((256, 256), bf16), ((BACK, 256), bf16)], "collect")
    mine, ahead, q_all = lax.optimization_barrier((mine, ahead, q_all))
    q_all = exchange_x(q_all)
    far = along_z(mine)
    near_keys = [mine] + [along_y(mine, d) for d in (1, 2, 3)]
    before = along_rows(ahead, 1)
    far_keys = [far] + [along_y(far, d) for d in (1, 2, 3)]

    o, h2, h1, h0, h3, l2, l1, l0, l3, back_grad, own_grad = attention(
        resp_len, where, (q_all, *s, before, *far_keys, *near_keys)
    )

    through, minus = along_y(h2, 1), along_y(h1, -1)
    plus = along_y(h3 + through, 1)
    crossing = lax.ppermute(back_grad, "seq", [(i, i - 4) for i in range(16, 20)])
    back_grad, plus = lax.optimization_barrier((back_grad, plus))
    within = lax.ppermute(back_grad, "seq", [(i, i - 4) for i in range(4, 32) if i // 4 != 4])
    (got,) = call(far_sum_kernel, (), (h0, minus, plus), [((256, 256), f32)], "far_sum", extra=(crossing,))
    got = along_z(got)
    one, two, three = along_y(l1, -1), along_y(l2, -2), along_y(l3, 1)

    attn_out, q_grad = call(
        unpack_rows_kernel, (), (exchange_x(o),), [((rows, HEADS * HEAD_DIM), bf16)] * 2, "unpack_rows"
    )
    l0, attn_out, q_grad = lax.optimization_barrier((l0, attn_out, q_grad))

    f = call(
        final_sum_kernel, (where,), (l0, one, two, three, got, own_grad, crossing, within),
        [((192, 256), bf16)] * 4, "final_sum",
    )
    f = [f[0]] + [along_x(f[d], -d) for d in (1, 2, 3)]
    resp_k_grad, resp_v_grad, prompt_k_grad, prompt_v_grad = call(
        unpack_small_kernel, (where,), f, [((rows, 512), bf16)] * 2 + [((64, 512), bf16)] * 2, "unpack_small"
    )
    return attn_out, q_grad, resp_k_grad, resp_v_grad, prompt_k_grad, prompt_v_grad


def solution(mesh):
    split = P(("grp", "seq"), None)
    return jax.shard_map(
        local,
        mesh=mesh,
        in_specs=(P("grp"),) + (split,) * 6,
        out_specs=(split,) * 6,
        check_vma=False,
    )
```

```python
import jax
import jax.numpy as jnp
from jax import lax
from jax.experimental import pallas as pl
from jax.experimental.pallas import tpu as pltpu
from jax.sharding import PartitionSpec as P

HEADS = 20
KV_HEADS = 4
HEAD_DIM = 128
PER_GROUP = HEADS // KV_HEADS
BACK = 384
NEGATIVE = -1e30
LOG2E = 1.4426950408889634
FACTOR = HEAD_DIM ** (-0.5)

X_GROUPS = [[first + x for x in range(4)] for first in range(0, 32, 4)]
ROWS = 256
KEYS = 1024
SPAN = 640
PROMPT_ROWS = 2048
OWN_ROWS = 512
WIDE = PER_GROUP * HEAD_DIM


def nt(a, b):
    return lax.dot_general(a, b, (((1,), (1,)), ((), ())), preferred_element_type=jnp.float32)


def nn(a, b):
    return lax.dot_general(a, b, (((1,), (0,)), ((), ())), preferred_element_type=jnp.float32)


def block_at(x, distance):
    return pl.ds(pl.multiple_of(lax.rem(x + 4 - distance, 4) * 128, 128), 128)


def attention_kernel(
    len_ref, where_ref, q_in, s0, s1, s2, s3, before_in, h0, h1, h2, h3, l0, l1, l2, l3,
    o_ref, g0, g1, g2, g3, g4, g5, g6, g7, back_grad_ref, own_grad_ref,
    key2, value1, key_t, value_t, s_first, s_second, p_first, p_second,
    grad2_first, grad2_second, rows_first, rows_second, key_sum, value_sum, q_all, staged, sems,
):
    base, x = where_ref[0], where_ref[1]
    all_rows = PROMPT_ROWS + BACK + OWN_ROWS

    def place(at, source):
        key2[at, :128] = source[:, :128]
        key2[at, 128:] = source[:, :128]
        value1[at, :128] = source[:, 128:]

    copies = []

    def load(source, target):
        copies.append(pltpu.make_async_copy(source, target, sems.at[len(copies)]))
        copies[-1].start()

    for i, source in enumerate((h2, h1, h0, h3, l2, l1, l0, l3)):
        load(source, staged.at[i * 256 : i * 256 + 256, :])
    load(before_in, staged.at[PROMPT_ROWS : PROMPT_ROWS + BACK, :])
    for d, source in enumerate((s0, s1, s2, s3)):
        first = PROMPT_ROWS + BACK + lax.rem(x + 4 - d, 4) * 128
        load(source.at[64:192, :], staged.at[pl.ds(pl.multiple_of(first, 128), 128), :])
    load(q_in, q_all)
    for copy in copies[:-1]:
        copy.wait()
    place(slice(0, all_rows), staged)
    value1[:, 128:] = jnp.ones((all_rows, 128), jnp.bfloat16)
    value_t[128:, :] = jnp.ones((16, all_rows), jnp.bfloat16)
    for c in range(0, all_rows, 128):
        at = slice(c, c + 128)
        key_t[:, at] = key2[at, :128].astype(jnp.float32).T.astype(jnp.bfloat16)
        value_t[:128, at] = value1[at, :128].astype(jnp.float32).T.astype(jnp.bfloat16)
    for ref in (key_sum, value_sum, p_second, grad2_second, rows_second):
        ref[...] = jnp.zeros_like(ref)
    copies[-1].wait()

    s_refs, p_refs = (s_first, s_second), (p_first, p_second)
    grad2_refs, rows_refs = (grad2_first, grad2_second), (rows_first, rows_second)

    def tiles(block):
        span = PROMPT_ROWS + block * ROWS
        out = [(c, c, KEYS) for c in range(0, PROMPT_ROWS, KEYS)] + [(span, PROMPT_ROWS, SPAN)]
        return [(slice(keys, keys + size), slice(at, at + size)) for keys, at, size in out]

    def rows_of(block, head, first):
        cols = pl.ds(pl.multiple_of(first + head * 128, 128), 128)
        return q_all[block * 2 : block * 2 + 2, :, cols].reshape(ROWS, 128)

    def scores(block, head):
        scaled = rows_of(block, head, 0).astype(jnp.float32).T * (FACTOR * LOG2E)
        high = scaled.astype(jnp.bfloat16)
        low = (scaled - high.astype(jnp.float32)).astype(jnp.bfloat16)
        q2t = jnp.concatenate([high, low], 0)
        top = None
        for keys, at in tiles(block):
            s = nn(key2[keys, :], q2t)
            if at.start == PROMPT_ROWS:
                own = base + block * ROWS
                row_pos = own + lax.broadcasted_iota(jnp.int32, (1, ROWS), 1)
                seg_start = jnp.zeros((1, ROWS), jnp.int32)
                end = jnp.int32(0)
                for j in range(16):
                    end = end + len_ref[j]
                    seg_start = jnp.maximum(seg_start, jnp.where(row_pos >= end, end, 0))
                key_pos = own - BACK + lax.broadcasted_iota(jnp.int32, (SPAN, ROWS), 0)
                s = jnp.where((key_pos <= row_pos) & (key_pos >= seg_start), s, NEGATIVE)
            s_refs[block][at, :] = s
            tile_top = jnp.max(s, axis=0, keepdims=True)
            top = tile_top if top is None else jnp.maximum(top, tile_top)
            yield top

    def weigh(block, head, top):
        total = jnp.zeros((144, ROWS), jnp.float32)
        for i, (keys, at) in enumerate(tiles(block)):
            p = jnp.exp2(s_refs[block][at, :] - top).astype(jnp.bfloat16)
            p_refs[block][at, :] = p
            total = total + nn(value_t[:, keys], p)
            if i < len(tiles(block)) - 1:
                yield
        inverse = 1.0 / total[128:129, :]
        out = (total[:128, :] * inverse).astype(jnp.bfloat16).astype(jnp.float32)
        cols = pl.ds(pl.multiple_of(head * 128, 128), 128)
        o_ref[block * 2 : block * 2 + 2, :, cols] = out.T.astype(jnp.bfloat16).reshape(2, 128, 128)
        grad_n = (rows_of(block, head, WIDE).astype(jnp.float32).T * inverse).astype(jnp.bfloat16)
        wide = grad_n.astype(jnp.float32)
        row_dot = -jnp.sum(wide * out, axis=0, keepdims=True)
        dot_high = row_dot.astype(jnp.bfloat16).astype(jnp.float32)
        line = lax.broadcasted_iota(jnp.int32, (128, ROWS), 0)
        extra = jnp.where(line == 0, dot_high, jnp.where(line == 1, row_dot - dot_high, 0.0))
        grad2_refs[block][:128, :] = grad_n
        grad2_refs[block][128:, :] = extra.astype(jnp.bfloat16)
        rows_refs[block][...] = wide.T.astype(jnp.bfloat16)
        yield

    def backward(block, head):
        q = rows_of(block, head, 0)
        dq = jnp.zeros((HEAD_DIM, ROWS), jnp.float32)
        for i, (keys, at) in enumerate(tiles(block)):
            p = p_refs[block][at, :]
            ds = (p.astype(jnp.float32) * nn(value1[keys, :], grad2_refs[block][...])).astype(jnp.bfloat16)
            dq = dq + nn(key_t[:, keys], ds)
            key_sum[keys, :] += nn(ds, q)
            value_sum[keys, :] += nn(p, rows_refs[block][...])
            if i < len(tiles(block)) - 1:
                yield
        cols = pl.ds(pl.multiple_of(WIDE + head * 128, 128), 128)
        dq = (dq * FACTOR).T.astype(jnp.bfloat16)
        o_ref[block * 2 : block * 2 + 2, :, cols] = dq.reshape(2, 128, 128)
        yield

    def beside(one, other):
        last = None
        for _, last in zip(one, other):
            pass
        return last

    def step(head, carry):
        top_first = beside(backward(1, jnp.maximum(head - 1, 0)), scores(0, head))
        top_second = beside(weigh(0, head, top_first), scores(1, head))
        beside(backward(0, head), weigh(1, head, top_second))
        return carry

    lax.fori_loop(0, PER_GROUP, step, 0)
    for _ in backward(1, PER_GROUP - 1):
        pass

    outs = [(i * 256, i * 256 + 256, ref) for i, ref in enumerate((g0, g1, g2, g3, g4, g5, g6, g7))]
    outs += [(PROMPT_ROWS, PROMPT_ROWS + BACK, back_grad_ref), (PROMPT_ROWS + BACK, all_rows, own_grad_ref)]
    for first, last, target in outs:
        target[:, :128] = key_sum[first:last, :] * FACTOR
        target[:, 128:] = value_sum[first:last, :]


def call(body, scalars, operands, outs, name, scratch=(), limit=24, cost=None, space=pltpu.VMEM, extra=()):
    smem = pl.BlockSpec(memory_space=pltpu.SMEM)
    return pl.pallas_call(
        body,
        in_specs=[smem] * len(scalars) + [pl.BlockSpec(memory_space=space)] * len(operands)
        + [pl.BlockSpec(memory_space=pl.ANY)] * len(extra),
        out_specs=[pl.BlockSpec(memory_space=pltpu.VMEM)] * len(outs),
        out_shape=[jax.ShapeDtypeStruct(shape, dtype) for shape, dtype in outs],
        scratch_shapes=list(scratch),
        compiler_params=pltpu.CompilerParams(vmem_limit_bytes=limit * 1024 * 1024),
        cost_estimate=cost,
        name=name,
    )(*scalars, *operands, *extra)


def attention(resp_len, where, operands):
    bf16, f32 = jnp.bfloat16, jnp.float32
    rows = PROMPT_ROWS + BACK + OWN_ROWS
    flops = 12 * 2560 * 2560 * 128
    return call(
        attention_kernel, (resp_len, where), operands,
        [((4, 128, 2 * WIDE), bf16)] + [((256, 256), f32)] * 8 + [((BACK, 256), f32), ((OWN_ROWS, 256), f32)],
        "attention",
        scratch=[
            pltpu.VMEM((rows, 256), bf16),
            pltpu.VMEM((rows, 256), bf16),
            pltpu.VMEM((128, rows), bf16),
            pltpu.VMEM((144, rows), bf16),
            pltpu.VMEM((PROMPT_ROWS + SPAN, ROWS), f32),
            pltpu.VMEM((PROMPT_ROWS + SPAN, ROWS), f32),
            pltpu.VMEM((PROMPT_ROWS + SPAN, ROWS), bf16),
            pltpu.VMEM((PROMPT_ROWS + SPAN, ROWS), bf16),
            pltpu.VMEM((256, ROWS), bf16),
            pltpu.VMEM((256, ROWS), bf16),
            pltpu.VMEM((ROWS, 128), bf16),
            pltpu.VMEM((ROWS, 128), bf16),
            pltpu.VMEM((rows, 128), f32),
            pltpu.VMEM((rows, 128), f32),
            pltpu.VMEM((4, 128, 2 * WIDE), bf16),
            pltpu.VMEM((rows, 256), bf16),
            pltpu.SemaphoreType.DMA((14,)),
        ],
        space=pl.ANY, limit=60,
        cost=pl.CostEstimate(flops=flops, bytes_accessed=8_000_000, transcendentals=flops // 1536),
    )


def head_columns(x, distance, width):
    return pl.ds(pl.multiple_of(lax.rem(x + distance, 4) * width, 128), width)


def pack_kernel(where_ref, pk, pv, k, v, q, g, s0, s1, s2, s3, rows, sems):
    pairs = []
    for d, target in enumerate((s0, s1, s2, s3)):
        cols = head_columns(where_ref[1], d, 128)
        for source, lines, lanes in ((pk, (0, 64), 0), (pv, (0, 64), 128), (k, (64, 192), 0), (v, (64, 192), 128)):
            pairs.append((source.at[:, cols], target.at[slice(*lines), lanes : lanes + 128]))
    for h in range(KV_HEADS):
        for source, first in ((q, 0), (g, WIDE)):
            pairs.append((source.at[:, h * WIDE : h * WIDE + WIDE], rows.at[h, :, first : first + WIDE]))
    copies = [pltpu.make_async_copy(source, target, sems.at[i]) for i, (source, target) in enumerate(pairs)]
    for copy in copies:
        copy.start()
    for copy in copies:
        copy.wait()


def collect_kernel(where_ref, s0, s1, s2, s3, mine_ref, ahead_ref):
    x = where_ref[1]
    for d, source in enumerate((s0, s1, s2, s3)):
        mine_ref[d * 64 : d * 64 + 64, :] = source[:64, :]
        block = lax.rem(x + 4 - d, 4)

        @pl.when(block > 0)
        def _():
            ahead_ref[pl.ds(pl.multiple_of((block - 1) * 128, 128), 128), :] = source[64:, :]


def final_sum_kernel(where_ref, n0, n1, n2, n3, own_ref, crossing_ref, within_ref, f0, f1, f2, f3):
    x = where_ref[1]
    for d, target in enumerate((f0, f1, f2, f3)):
        at = slice(d * 64, d * 64 + 64)
        total = (n0[at, :] + n1[at, :]) + (n2[at, :] + n3[at, :])
        target[:64, :] = total.astype(jnp.bfloat16)
        block = lax.rem(x + 4 - d, 4)
        behind = pl.ds(pl.multiple_of(jnp.maximum(block - 1, 0) * 128, 128), 128)
        extra = jnp.where(block > 0, crossing_ref[behind, :] + within_ref[behind, :], 0.0)
        target[64:, :] = (own_ref[block_at(x, d), :] + extra).astype(jnp.bfloat16)


def two_sums_kernel(a, b, c, d, ab_ref, cd_ref):
    ab_ref[...] = a[...] + b[...]
    cd_ref[...] = c[...] + d[...]


def sum_kernel(a, b, *refs):
    refs[-1][...] = a[...] + b[...]


def unpack_rows_kernel(o_ref, out_ref, dq_ref):
    for h in range(KV_HEADS):
        at = slice(h * WIDE, h * WIDE + WIDE)
        out_ref[:, at] = o_ref[h, :, :WIDE]
        dq_ref[:, at] = o_ref[h, :, WIDE:]


def unpack_small_kernel(where_ref, f0, f1, f2, f3, k_ref, v_ref, pk_ref, pv_ref):
    x = where_ref[1]
    for d, source in enumerate((f0, f1, f2, f3)):
        at = head_columns(x, d, 128)
        pk_ref[:, at] = source[:64, :128]
        pv_ref[:, at] = source[:64, 128:]
        k_ref[:, at] = source[64:, :128]
        v_ref[:, at] = source[64:, 128:]


def along_x(value, step):
    return lax.ppermute(value, "seq", [(i, i // 4 * 4 + (i + step) % 4) for i in range(32)])


def exchange_x(value):
    return lax.all_to_all(value, "seq", 0, 0, axis_index_groups=X_GROUPS, tiled=True)


def along_y(value, step):
    return lax.ppermute(value, "seq", [(i, i // 16 * 16 + (i + 4 * step) % 16) for i in range(32)])


def along_z(value):
    return lax.ppermute(value, "seq", [(i, (i + 16) % 32) for i in range(32)])


def along_rows(value, step):
    pairs = [(i, i + 4 * step) for i in range(32)]
    return lax.ppermute(value, "seq", [(i, j) for i, j in pairs if 0 <= j < 32])


def local(resp_len, prompt_keys, prompt_values, resp_q, resp_k, resp_v, out_grad):
    me = lax.axis_index("seq").astype(jnp.int32)
    where = jnp.stack([me // 4 * OWN_ROWS, me % 4])
    rows, bf16, f32 = resp_q.shape[0], jnp.bfloat16, jnp.float32

    *s, q_all = call(
        pack_kernel, (where,), (prompt_keys, prompt_values, resp_k, resp_v, resp_q, out_grad),
        [((192, 256), bf16)] * 4 + [((4, rows, 2 * WIDE), bf16)], "pack",
        scratch=[pltpu.SemaphoreType.DMA((24,))], space=pl.ANY, limit=60,
    )
    s = [s[0]] + [along_x(s[d], d) for d in (1, 2, 3)]
    mine, ahead = call(collect_kernel, (where,), s, [((256, 256), bf16), ((BACK, 256), bf16)], "collect")
    mine, ahead, q_all = lax.optimization_barrier((mine, ahead, q_all))
    q_all = exchange_x(q_all)
    far = along_z(mine)
    near_keys = [mine] + [along_y(mine, d) for d in (1, 2, 3)]
    before = along_rows(ahead, 1)
    far_keys = [far] + [along_y(far, d) for d in (1, 2, 3)]

    o, h2, h1, h0, h3, l2, l1, l0, l3, back_grad, own_grad = attention(
        resp_len, where, (q_all, *s, before, *far_keys, *near_keys)
    )

    through, minus = along_y(h2, 1), along_y(h1, -1)
    crossing = lax.ppermute(back_grad, "seq", [(i, i - 4) for i in range(16, 20)])
    part = [((256, 256), f32)]
    plus, stay = call(two_sums_kernel, (), (h3, through, h0, minus), part * 2, "two_sums")
    plus = along_y(plus, 1)
    (give,) = call(sum_kernel, (), (stay, plus), part, "far_sum", extra=(crossing,))
    give, back_grad, l1, l2, l3 = lax.optimization_barrier((give, back_grad, l1, l2, l3))
    got = along_z(give)
    one, two, three = along_y(l1, -1), along_y(l2, -2), along_y(l3, 1)
    within = lax.ppermute(back_grad, "seq", [(i, i - 4) for i in range(4, 32) if i // 4 != 4])

    attn_out, q_grad = call(
        unpack_rows_kernel, (), (exchange_x(o),), [((rows, HEADS * HEAD_DIM), bf16)] * 2, "unpack_rows"
    )
    l0, attn_out, q_grad = lax.optimization_barrier((l0, attn_out, q_grad))
    (stay,) = call(sum_kernel, (), (l0, got), part, "near_sum")

    f = call(
        final_sum_kernel, (where,), (stay, one, two, three, own_grad, crossing, within),
        [((192, 256), bf16)] * 4, "final_sum",
    )
    f = [f[0]] + [along_x(f[d], -d) for d in (1, 2, 3)]
    resp_k_grad, resp_v_grad, prompt_k_grad, prompt_v_grad = call(
        unpack_small_kernel, (where,), f, [((rows, 512), bf16)] * 2 + [((64, 512), bf16)] * 2, "unpack_small"
    )
    return attn_out, q_grad, resp_k_grad, resp_v_grad, prompt_k_grad, prompt_v_grad


def solution(mesh):
    split = P(("grp", "seq"), None)
    return jax.shard_map(
        local,
        mesh=mesh,
        in_specs=(P("grp"),) + (split,) * 6,
        out_specs=(split,) * 6,
        check_vma=False,
    )
```

```python
import jax
import jax.numpy as jnp
from jax import lax
from jax.experimental import pallas as pl
from jax.experimental.pallas import tpu as pltpu
from jax.sharding import PartitionSpec as P

HEADS = 20
KV_HEADS = 4
HEAD_DIM = 128
PER_GROUP = HEADS // KV_HEADS
BACK = 384
NEGATIVE = -1e30
LOG2E = 1.4426950408889634
FACTOR = HEAD_DIM ** (-0.5)

X_GROUPS = [[first + x for x in range(4)] for first in range(0, 32, 4)]
ROWS = 256
KEYS = 1024
SPAN = 640
PROMPT_ROWS = 2048
OWN_ROWS = 512
WIDE = PER_GROUP * HEAD_DIM


def nt(a, b):
    return lax.dot_general(a, b, (((1,), (1,)), ((), ())), preferred_element_type=jnp.float32)


def nn(a, b):
    return lax.dot_general(a, b, (((1,), (0,)), ((), ())), preferred_element_type=jnp.float32)


def block_at(x, distance):
    return pl.ds(pl.multiple_of(lax.rem(x + 4 - distance, 4) * 128, 128), 128)


def attention_kernel(
    len_ref, where_ref, q_in, s0, s1, s2, s3, before_in, h0, h1, h2, h3, l0, l1, l2, l3,
    o_ref, g0, g1, g2, g3, g4, g5, g6, g7, own_grad_ref, back_k_ref, back_v_ref,
    key2, value1, key_t, value_t, s_first, s_second, p_first, p_second,
    grad2_first, grad2_second, rows_first, rows_second, key_sum, value_sum, q_all, staged, sems,
):
    base, x = where_ref[0], where_ref[1]
    all_rows = PROMPT_ROWS + BACK + OWN_ROWS

    def place(at, source):
        key2[at, :128] = source[:, :128]
        key2[at, 128:] = source[:, :128]
        value1[at, :128] = source[:, 128:]

    copies = []

    def load(source, target):
        copies.append(pltpu.make_async_copy(source, target, sems.at[len(copies)]))
        copies[-1].start()

    for i, source in enumerate((h2, h1, h0, h3, l2, l1, l0, l3)):
        load(source, staged.at[i * 256 : i * 256 + 256, :])
    load(before_in, staged.at[PROMPT_ROWS : PROMPT_ROWS + BACK, :])
    for d, source in enumerate((s0, s1, s2, s3)):
        first = PROMPT_ROWS + BACK + lax.rem(x + 4 - d, 4) * 128
        load(source.at[64:192, :], staged.at[pl.ds(pl.multiple_of(first, 128), 128), :])
    load(q_in, q_all)
    for copy in copies[:-1]:
        copy.wait()
    place(slice(0, all_rows), staged)
    value1[:, 128:] = jnp.ones((all_rows, 128), jnp.bfloat16)
    value_t[128:, :] = jnp.ones((16, all_rows), jnp.bfloat16)
    for c in range(0, all_rows, 128):
        at = slice(c, c + 128)
        key_t[:, at] = key2[at, :128].astype(jnp.float32).T.astype(jnp.bfloat16)
        value_t[:128, at] = value1[at, :128].astype(jnp.float32).T.astype(jnp.bfloat16)
    for ref in (key_sum, value_sum, p_second, grad2_second, rows_second):
        ref[...] = jnp.zeros_like(ref)
    copies[-1].wait()

    s_refs, p_refs = (s_first, s_second), (p_first, p_second)
    grad2_refs, rows_refs = (grad2_first, grad2_second), (rows_first, rows_second)

    def tiles(block):
        span = PROMPT_ROWS + block * ROWS
        out = [(c, c, KEYS) for c in range(0, PROMPT_ROWS, KEYS)] + [(span, PROMPT_ROWS, SPAN)]
        return [(slice(keys, keys + size), slice(at, at + size)) for keys, at, size in out]

    def rows_of(block, head, first):
        cols = pl.ds(pl.multiple_of(first + head * 128, 128), 128)
        return q_all[block * 2 : block * 2 + 2, :, cols].reshape(ROWS, 128)

    def scores(block, head):
        scaled = rows_of(block, head, 0).astype(jnp.float32).T * (FACTOR * LOG2E)
        high = scaled.astype(jnp.bfloat16)
        low = (scaled - high.astype(jnp.float32)).astype(jnp.bfloat16)
        q2t = jnp.concatenate([high, low], 0)
        top = None
        for keys, at in tiles(block):
            s = nn(key2[keys, :], q2t)
            if at.start == PROMPT_ROWS:
                own = base + block * ROWS
                row_pos = own + lax.broadcasted_iota(jnp.int32, (1, ROWS), 1)
                seg_start = jnp.zeros((1, ROWS), jnp.int32)
                end = jnp.int32(0)
                for j in range(16):
                    end = end + len_ref[j]
                    seg_start = jnp.maximum(seg_start, jnp.where(row_pos >= end, end, 0))
                key_pos = own - BACK + lax.broadcasted_iota(jnp.int32, (SPAN, ROWS), 0)
                s = jnp.where((key_pos <= row_pos) & (key_pos >= seg_start), s, NEGATIVE)
            s_refs[block][at, :] = s
            tile_top = jnp.max(s, axis=0, keepdims=True)
            top = tile_top if top is None else jnp.maximum(top, tile_top)
            yield top

    def weigh(block, head, top):
        total = jnp.zeros((144, ROWS), jnp.float32)
        for i, (keys, at) in enumerate(tiles(block)):
            p = jnp.exp2(s_refs[block][at, :] - top).astype(jnp.bfloat16)
            p_refs[block][at, :] = p
            total = total + nn(value_t[:, keys], p)
            if i < len(tiles(block)) - 1:
                yield
        inverse = 1.0 / total[128:129, :]
        out = (total[:128, :] * inverse).astype(jnp.bfloat16).astype(jnp.float32)
        cols = pl.ds(pl.multiple_of(head * 128, 128), 128)
        o_ref[block * 2 : block * 2 + 2, :, cols] = out.T.astype(jnp.bfloat16).reshape(2, 128, 128)
        grad_n = (rows_of(block, head, WIDE).astype(jnp.float32).T * inverse).astype(jnp.bfloat16)
        wide = grad_n.astype(jnp.float32)
        row_dot = -jnp.sum(wide * out, axis=0, keepdims=True)
        dot_high = row_dot.astype(jnp.bfloat16).astype(jnp.float32)
        line = lax.broadcasted_iota(jnp.int32, (128, ROWS), 0)
        extra = jnp.where(line == 0, dot_high, jnp.where(line == 1, row_dot - dot_high, 0.0))
        grad2_refs[block][:128, :] = grad_n
        grad2_refs[block][128:, :] = extra.astype(jnp.bfloat16)
        rows_refs[block][...] = wide.T.astype(jnp.bfloat16)
        yield

    def backward(block, head):
        q = rows_of(block, head, 0)
        dq = jnp.zeros((HEAD_DIM, ROWS), jnp.float32)
        for i, (keys, at) in enumerate(tiles(block)):
            p = p_refs[block][at, :]
            ds = (p.astype(jnp.float32) * nn(value1[keys, :], grad2_refs[block][...])).astype(jnp.bfloat16)
            dq = dq + nn(key_t[:, keys], ds)
            key_sum[keys, :] += nn(ds, q)
            value_sum[keys, :] += nn(p, rows_refs[block][...])
            if i < len(tiles(block)) - 1:
                yield
        cols = pl.ds(pl.multiple_of(WIDE + head * 128, 128), 128)
        dq = (dq * FACTOR).T.astype(jnp.bfloat16)
        o_ref[block * 2 : block * 2 + 2, :, cols] = dq.reshape(2, 128, 128)
        yield

    def beside(one, other):
        last = None
        for _, last in zip(one, other):
            pass
        return last

    def step(head, carry):
        top_first = beside(backward(1, jnp.maximum(head - 1, 0)), scores(0, head))
        top_second = beside(weigh(0, head, top_first), scores(1, head))
        beside(backward(0, head), weigh(1, head, top_second))
        return carry

    lax.fori_loop(0, PER_GROUP, step, 0)
    for _ in backward(1, PER_GROUP - 1):
        pass

    outs = [(i * 256, i * 256 + 256, ref) for i, ref in enumerate((g0, g1, g2, g3, g4, g5, g6, g7))]
    outs += [(PROMPT_ROWS + BACK, all_rows, own_grad_ref)]
    for first, last, target in outs:
        target[:, :128] = key_sum[first:last, :] * FACTOR
        target[:, 128:] = value_sum[first:last, :]
    before = slice(PROMPT_ROWS, PROMPT_ROWS + BACK)
    back_k_ref[...] = key_sum[before, :] * FACTOR
    back_v_ref[...] = value_sum[before, :]


def call(body, scalars, operands, outs, name, scratch=(), limit=24, cost=None, space=pltpu.VMEM, extra=()):
    smem = pl.BlockSpec(memory_space=pltpu.SMEM)
    return pl.pallas_call(
        body,
        in_specs=[smem] * len(scalars) + [pl.BlockSpec(memory_space=space)] * len(operands)
        + [pl.BlockSpec(memory_space=pl.ANY)] * len(extra),
        out_specs=[pl.BlockSpec(memory_space=pltpu.VMEM)] * len(outs),
        out_shape=[jax.ShapeDtypeStruct(shape, dtype) for shape, dtype in outs],
        scratch_shapes=list(scratch),
        compiler_params=pltpu.CompilerParams(vmem_limit_bytes=limit * 1024 * 1024),
        cost_estimate=cost,
        name=name,
    )(*scalars, *operands, *extra)


def attention(resp_len, where, operands):
    bf16, f32 = jnp.bfloat16, jnp.float32
    rows = PROMPT_ROWS + BACK + OWN_ROWS
    flops = 12 * 2560 * 2560 * 128
    return call(
        attention_kernel, (resp_len, where), operands,
        [((4, 128, 2 * WIDE), bf16)] + [((256, 256), f32)] * 8
        + [((OWN_ROWS, 256), f32)] + [((BACK, 128), f32)] * 2,
        "attention",
        scratch=[
            pltpu.VMEM((rows, 256), bf16),
            pltpu.VMEM((rows, 256), bf16),
            pltpu.VMEM((128, rows), bf16),
            pltpu.VMEM((144, rows), bf16),
            pltpu.VMEM((PROMPT_ROWS + SPAN, ROWS), f32),
            pltpu.VMEM((PROMPT_ROWS + SPAN, ROWS), f32),
            pltpu.VMEM((PROMPT_ROWS + SPAN, ROWS), bf16),
            pltpu.VMEM((PROMPT_ROWS + SPAN, ROWS), bf16),
            pltpu.VMEM((256, ROWS), bf16),
            pltpu.VMEM((256, ROWS), bf16),
            pltpu.VMEM((ROWS, 128), bf16),
            pltpu.VMEM((ROWS, 128), bf16),
            pltpu.VMEM((rows, 128), f32),
            pltpu.VMEM((rows, 128), f32),
            pltpu.VMEM((4, 128, 2 * WIDE), bf16),
            pltpu.VMEM((rows, 256), bf16),
            pltpu.SemaphoreType.DMA((14,)),
        ],
        space=pl.ANY, limit=60,
        cost=pl.CostEstimate(flops=flops, bytes_accessed=8_000_000, transcendentals=flops // 1536),
    )


def head_columns(x, distance, width):
    return pl.ds(pl.multiple_of(lax.rem(x + distance, 4) * width, 128), width)


def pack_kernel(where_ref, pk, pv, k, v, q, g, s0, s1, s2, s3, rows, sems):
    pairs = []
    for d, target in enumerate((s0, s1, s2, s3)):
        cols = head_columns(where_ref[1], d, 128)
        for source, lines, lanes in ((pk, (0, 64), 0), (pv, (0, 64), 128), (k, (64, 192), 0), (v, (64, 192), 128)):
            pairs.append((source.at[:, cols], target.at[slice(*lines), lanes : lanes + 128]))
    for h in range(KV_HEADS):
        for source, first in ((q, 0), (g, WIDE)):
            pairs.append((source.at[:, h * WIDE : h * WIDE + WIDE], rows.at[h, :, first : first + WIDE]))
    copies = [pltpu.make_async_copy(source, target, sems.at[i]) for i, (source, target) in enumerate(pairs)]
    for copy in copies:
        copy.start()
    for copy in copies:
        copy.wait()


def collect_kernel(where_ref, s0, s1, s2, s3, mine_ref, ahead_ref):
    x = where_ref[1]
    for d, source in enumerate((s0, s1, s2, s3)):
        mine_ref[d * 64 : d * 64 + 64, :] = source[:64, :]
        block = lax.rem(x + 4 - d, 4)

        @pl.when(block > 0)
        def _():
            ahead_ref[pl.ds(pl.multiple_of((block - 1) * 128, 128), 128), :] = source[64:, :]


def final_sum_kernel(where_ref, n0, n1, n2, n3, own_ref, crossing_ref, within_ref, f0, f1, f2, f3):
    x = where_ref[1]
    for d, target in enumerate((f0, f1, f2, f3)):
        at = slice(d * 64, d * 64 + 64)
        total = (n0[at, :] + n1[at, :]) + (n2[at, :] + n3[at, :])
        target[:64, :] = total.astype(jnp.bfloat16)
        block = lax.rem(x + 4 - d, 4)
        behind = pl.ds(pl.multiple_of(jnp.maximum(block - 1, 0) * 128, 128), 128)
        for lanes, extra in (
            (slice(0, 128), crossing_ref[behind, :] + within_ref[behind, :128]),
            (slice(128, 256), within_ref[behind, 128:]),
        ):
            total = own_ref[block_at(x, d), lanes] + jnp.where(block > 0, extra, 0.0)
            target[64:, lanes] = total.astype(jnp.bfloat16)


def two_sums_kernel(a, b, c, d, ab_ref, cd_ref):
    ab_ref[...] = a[...] + b[...]
    cd_ref[...] = c[...] + d[...]


def pack_window_kernel(where_ref, k_ref, v_ref, over_z, out_ref):
    first = where_ref[0] == 0
    out_ref[:, :128] = jnp.where(first, 0.0, k_ref[...])
    out_ref[:, 128:] = jnp.where(first, over_z[...], v_ref[...])


def sum_kernel(a, b, *refs):
    refs[-1][...] = a[...] + b[...]


def unpack_rows_kernel(o_ref, out_ref, dq_ref):
    for h in range(KV_HEADS):
        at = slice(h * WIDE, h * WIDE + WIDE)
        out_ref[:, at] = o_ref[h, :, :WIDE]
        dq_ref[:, at] = o_ref[h, :, WIDE:]


def unpack_small_kernel(where_ref, f0, f1, f2, f3, k_ref, v_ref, pk_ref, pv_ref):
    x = where_ref[1]
    for d, source in enumerate((f0, f1, f2, f3)):
        at = head_columns(x, d, 128)
        pk_ref[:, at] = source[:64, :128]
        pv_ref[:, at] = source[:64, 128:]
        k_ref[:, at] = source[64:, :128]
        v_ref[:, at] = source[64:, 128:]


def along_x(value, step):
    return lax.ppermute(value, "seq", [(i, i // 4 * 4 + (i + step) % 4) for i in range(32)])


def exchange_x(value):
    return lax.all_to_all(value, "seq", 0, 0, axis_index_groups=X_GROUPS, tiled=True)


def along_y(value, step):
    return lax.ppermute(value, "seq", [(i, i // 16 * 16 + (i + 4 * step) % 16) for i in range(32)])


def along_z(value):
    return lax.ppermute(value, "seq", [(i, (i + 16) % 32) for i in range(32)])


def along_rows(value, step):
    pairs = [(i, i + 4 * step) for i in range(32)]
    return lax.ppermute(value, "seq", [(i, j) for i, j in pairs if 0 <= j < 32])


def local(resp_len, prompt_keys, prompt_values, resp_q, resp_k, resp_v, out_grad):
    me = lax.axis_index("seq").astype(jnp.int32)
    where = jnp.stack([me // 4 * OWN_ROWS, me % 4])
    rows, bf16, f32 = resp_q.shape[0], jnp.bfloat16, jnp.float32

    *s, q_all = call(
        pack_kernel, (where,), (prompt_keys, prompt_values, resp_k, resp_v, resp_q, out_grad),
        [((192, 256), bf16)] * 4 + [((4, rows, 2 * WIDE), bf16)], "pack",
        scratch=[pltpu.SemaphoreType.DMA((24,))], space=pl.ANY, limit=60,
    )
    s = [s[0]] + [along_x(s[d], d) for d in (1, 2, 3)]
    mine, ahead = call(collect_kernel, (where,), s, [((256, 256), bf16), ((BACK, 256), bf16)], "collect")
    mine, ahead, q_all = lax.optimization_barrier((mine, ahead, q_all))
    q_all = exchange_x(q_all)
    far = along_z(mine)
    near_keys = [mine] + [along_y(mine, d) for d in (1, 2, 3)]
    before = along_rows(ahead, 1)
    far_keys = [far] + [along_y(far, d) for d in (1, 2, 3)]

    o, h2, h1, h0, h3, l2, l1, l0, l3, own_grad, back_k, back_v = attention(
        resp_len, where, (q_all, *s, before, *far_keys, *near_keys)
    )

    through, minus = along_y(h2, 1), along_y(h1, -1)
    crossing = lax.ppermute(back_k, "seq", [(i, i - 4) for i in range(16, 20)])
    over_z = lax.ppermute(back_v, "seq", [(i, i - 16) for i in range(16, 20)])
    part = [((256, 256), f32)]
    plus, stay = call(two_sums_kernel, (), (h3, through, h0, minus), part * 2, "two_sums")
    plus = along_y(plus, 1)
    (give,) = call(sum_kernel, (), (stay, plus), part, "far_sum", extra=(crossing, over_z))
    got = along_z(give)
    one, two, three = along_y(l1, -1), along_y(l2, -2), along_y(l3, 1)
    (back,) = call(pack_window_kernel, (where,), (back_k, back_v, over_z), [((BACK, 256), f32)], "pack_window")
    pairs = [(i, i - 4) for i in range(4, 32) if i // 4 != 4] + [(i, i + 12) for i in range(4)]
    within = lax.ppermute(back, "seq", pairs)

    attn_out, q_grad = call(
        unpack_rows_kernel, (), (exchange_x(o),), [((rows, HEADS * HEAD_DIM), bf16)] * 2, "unpack_rows"
    )
    l0, attn_out, q_grad = lax.optimization_barrier((l0, attn_out, q_grad))
    (stay,) = call(sum_kernel, (), (l0, got), part, "near_sum")

    f = call(
        final_sum_kernel, (where,), (stay, one, two, three, own_grad, crossing, within),
        [((192, 256), bf16)] * 4, "final_sum",
    )
    f = [f[0]] + [along_x(f[d], -d) for d in (1, 2, 3)]
    resp_k_grad, resp_v_grad, prompt_k_grad, prompt_v_grad = call(
        unpack_small_kernel, (where,), f, [((rows, 512), bf16)] * 2 + [((64, 512), bf16)] * 2, "unpack_small"
    )
    return attn_out, q_grad, resp_k_grad, resp_v_grad, prompt_k_grad, prompt_v_grad


def solution(mesh):
    split = P(("grp", "seq"), None)
    return jax.shard_map(
        local,
        mesh=mesh,
        in_specs=(P("grp"),) + (split,) * 6,
        out_specs=(split,) * 6,
        check_vma=False,
    )
```

```python
import jax
import jax.numpy as jnp
from jax import lax
from jax.experimental import pallas as pl
from jax.experimental.pallas import tpu as pltpu
from jax.sharding import PartitionSpec as P

HEADS = 20
KV_HEADS = 4
HEAD_DIM = 128
PER_GROUP = HEADS // KV_HEADS
BACK = 384
NEGATIVE = -1e30
LOG2E = 1.4426950408889634
FACTOR = HEAD_DIM ** (-0.5)

X_GROUPS = [[first + x for x in range(4)] for first in range(0, 32, 4)]
ROWS = 256
KEYS = 1024
SPAN = 640
PROMPT_ROWS = 2048
OWN_ROWS = 512
WIDE = PER_GROUP * HEAD_DIM


def nt(a, b):
    return lax.dot_general(a, b, (((1,), (1,)), ((), ())), preferred_element_type=jnp.float32)


def nn(a, b):
    return lax.dot_general(a, b, (((1,), (0,)), ((), ())), preferred_element_type=jnp.float32)


def block_at(x, distance):
    return pl.ds(pl.multiple_of(lax.rem(x + 4 - distance, 4) * 128, 128), 128)


def attention_kernel(
    len_ref, where_ref, q_in, s0, s1, s2, s3, before_in, h0, h1, h2, h3, l0, l1, l2, l3,
    o_ref, g0, g1, g2, g3, g4, g5, g6, g7, own_grad_ref, back_k_ref, back_v_ref,
    key2, value1, key_t, value_t, s_first, s_second, p_first, p_second,
    grad2_first, grad2_second, rows_first, rows_second, key_sum, value_sum, q_all, staged, sems,
):
    base, x = where_ref[0], where_ref[1]
    all_rows = PROMPT_ROWS + BACK + OWN_ROWS

    def place(at, source):
        key2[at, :128] = source[:, :128]
        key2[at, 128:] = source[:, :128]
        value1[at, :128] = source[:, 128:]

    copies = []

    def load(source, target):
        copies.append(pltpu.make_async_copy(source, target, sems.at[len(copies)]))
        copies[-1].start()

    for i, source in enumerate((h2, h1, h0, h3, l2, l1, l0, l3)):
        load(source, staged.at[i * 256 : i * 256 + 256, :])
    load(before_in, staged.at[PROMPT_ROWS : PROMPT_ROWS + BACK, :])
    for d, source in enumerate((s0, s1, s2, s3)):
        first = PROMPT_ROWS + BACK + lax.rem(x + 4 - d, 4) * 128
        load(source.at[64:192, :], staged.at[pl.ds(pl.multiple_of(first, 128), 128), :])
    load(q_in, q_all)
    for copy in copies[:-1]:
        copy.wait()
    place(slice(0, all_rows), staged)
    value1[:, 128:] = jnp.ones((all_rows, 128), jnp.bfloat16)
    value_t[128:, :] = jnp.ones((16, all_rows), jnp.bfloat16)
    for c in range(0, all_rows, 128):
        at = slice(c, c + 128)
        key_t[:, at] = key2[at, :128].astype(jnp.float32).T.astype(jnp.bfloat16)
        value_t[:128, at] = value1[at, :128].astype(jnp.float32).T.astype(jnp.bfloat16)
    for ref in (key_sum, value_sum, p_second, grad2_second, rows_second):
        ref[...] = jnp.zeros_like(ref)
    copies[-1].wait()

    s_refs, p_refs = (s_first, s_second), (p_first, p_second)
    grad2_refs, rows_refs = (grad2_first, grad2_second), (rows_first, rows_second)

    def tiles(block):
        span = PROMPT_ROWS + block * ROWS
        out = [(c, c, KEYS) for c in range(0, PROMPT_ROWS, KEYS)] + [(span, PROMPT_ROWS, SPAN)]
        return [(slice(keys, keys + size), slice(at, at + size)) for keys, at, size in out]

    def rows_of(block, head, first):
        cols = pl.ds(pl.multiple_of(first + head * 128, 128), 128)
        return q_all[block * 2 : block * 2 + 2, :, cols].reshape(ROWS, 128)

    def scores(block, head):
        scaled = rows_of(block, head, 0).astype(jnp.float32).T * (FACTOR * LOG2E)
        high = scaled.astype(jnp.bfloat16)
        low = (scaled - high.astype(jnp.float32)).astype(jnp.bfloat16)
        q2t = jnp.concatenate([high, low], 0)
        top = None
        for keys, at in tiles(block):
            s = nn(key2[keys, :], q2t)
            if at.start == PROMPT_ROWS:
                own = base + block * ROWS
                row_pos = own + lax.broadcasted_iota(jnp.int32, (1, ROWS), 1)
                seg_start = jnp.zeros((1, ROWS), jnp.int32)
                end = jnp.int32(0)
                for j in range(16):
                    end = end + len_ref[j]
                    seg_start = jnp.maximum(seg_start, jnp.where(row_pos >= end, end, 0))
                key_pos = own - BACK + lax.broadcasted_iota(jnp.int32, (SPAN, ROWS), 0)
                s = jnp.where((key_pos <= row_pos) & (key_pos >= seg_start), s, NEGATIVE)
            s_refs[block][at, :] = s
            tile_top = jnp.max(s, axis=0, keepdims=True)
            top = tile_top if top is None else jnp.maximum(top, tile_top)
            yield top

    def weigh(block, head, top):
        total = jnp.zeros((144, ROWS), jnp.float32)
        for i, (keys, at) in enumerate(tiles(block)):
            p = jnp.exp2(s_refs[block][at, :] - top).astype(jnp.bfloat16)
            p_refs[block][at, :] = p
            total = total + nn(value_t[:, keys], p)
            if i < len(tiles(block)) - 1:
                yield
        inverse = 1.0 / total[128:129, :]
        out = (total[:128, :] * inverse).astype(jnp.bfloat16).astype(jnp.float32)
        cols = pl.ds(pl.multiple_of(head * 128, 128), 128)
        o_ref[block * 2 : block * 2 + 2, :, cols] = out.T.astype(jnp.bfloat16).reshape(2, 128, 128)
        grad_n = (rows_of(block, head, WIDE).astype(jnp.float32).T * inverse).astype(jnp.bfloat16)
        wide = grad_n.astype(jnp.float32)
        row_dot = -jnp.sum(wide * out, axis=0, keepdims=True)
        dot_high = row_dot.astype(jnp.bfloat16).astype(jnp.float32)
        line = lax.broadcasted_iota(jnp.int32, (128, ROWS), 0)
        extra = jnp.where(line == 0, dot_high, jnp.where(line == 1, row_dot - dot_high, 0.0))
        grad2_refs[block][:128, :] = grad_n
        grad2_refs[block][128:, :] = extra.astype(jnp.bfloat16)
        rows_refs[block][...] = wide.T.astype(jnp.bfloat16)
        yield

    def backward(block, head):
        q = rows_of(block, head, 0)
        dq = jnp.zeros((HEAD_DIM, ROWS), jnp.float32)
        for i, (keys, at) in enumerate(tiles(block)):
            p = p_refs[block][at, :]
            ds = (p.astype(jnp.float32) * nn(value1[keys, :], grad2_refs[block][...])).astype(jnp.bfloat16)
            dq = dq + nn(key_t[:, keys], ds)
            key_sum[keys, :] += nn(ds, q)
            value_sum[keys, :] += nn(p, rows_refs[block][...])
            if i < len(tiles(block)) - 1:
                yield
        cols = pl.ds(pl.multiple_of(WIDE + head * 128, 128), 128)
        dq = (dq * FACTOR).T.astype(jnp.bfloat16)
        o_ref[block * 2 : block * 2 + 2, :, cols] = dq.reshape(2, 128, 128)
        yield

    def beside(one, other):
        last = None
        for _, last in zip(one, other):
            pass
        return last

    def step(head, carry):
        top_first = beside(backward(1, jnp.maximum(head - 1, 0)), scores(0, head))
        top_second = beside(weigh(0, head, top_first), scores(1, head))
        beside(backward(0, head), weigh(1, head, top_second))
        return carry

    lax.fori_loop(0, PER_GROUP, step, 0)
    for _ in backward(1, PER_GROUP - 1):
        pass

    outs = [(i * 256, i * 256 + 256, ref) for i, ref in enumerate((g0, g1, g2, g3, g4, g5, g6, g7))]
    outs += [(PROMPT_ROWS + BACK, all_rows, own_grad_ref)]
    for first, last, target in outs:
        target[:, :128] = key_sum[first:last, :] * FACTOR
        target[:, 128:] = value_sum[first:last, :]
    before = slice(PROMPT_ROWS, PROMPT_ROWS + BACK)
    back_k_ref[...] = key_sum[before, :] * FACTOR
    back_v_ref[...] = value_sum[before, :]


def call(body, scalars, operands, outs, name, scratch=(), limit=24, cost=None, space=pltpu.VMEM, extra=()):
    smem = pl.BlockSpec(memory_space=pltpu.SMEM)
    return pl.pallas_call(
        body,
        in_specs=[smem] * len(scalars) + [pl.BlockSpec(memory_space=space)] * len(operands)
        + [pl.BlockSpec(memory_space=pl.ANY)] * len(extra),
        out_specs=[pl.BlockSpec(memory_space=pltpu.VMEM)] * len(outs),
        out_shape=[jax.ShapeDtypeStruct(shape, dtype) for shape, dtype in outs],
        scratch_shapes=list(scratch),
        compiler_params=pltpu.CompilerParams(vmem_limit_bytes=limit * 1024 * 1024),
        cost_estimate=cost,
        name=name,
    )(*scalars, *operands, *extra)


def attention(resp_len, where, operands):
    bf16, f32 = jnp.bfloat16, jnp.float32
    rows = PROMPT_ROWS + BACK + OWN_ROWS
    flops = 12 * 2560 * 2560 * 128
    return call(
        attention_kernel, (resp_len, where), operands,
        [((4, 128, 2 * WIDE), bf16)] + [((256, 256), f32)] * 8
        + [((OWN_ROWS, 256), f32)] + [((BACK, 128), f32)] * 2,
        "attention",
        scratch=[
            pltpu.VMEM((rows, 256), bf16),
            pltpu.VMEM((rows, 256), bf16),
            pltpu.VMEM((128, rows), bf16),
            pltpu.VMEM((144, rows), bf16),
            pltpu.VMEM((PROMPT_ROWS + SPAN, ROWS), f32),
            pltpu.VMEM((PROMPT_ROWS + SPAN, ROWS), f32),
            pltpu.VMEM((PROMPT_ROWS + SPAN, ROWS), bf16),
            pltpu.VMEM((PROMPT_ROWS + SPAN, ROWS), bf16),
            pltpu.VMEM((256, ROWS), bf16),
            pltpu.VMEM((256, ROWS), bf16),
            pltpu.VMEM((ROWS, 128), bf16),
            pltpu.VMEM((ROWS, 128), bf16),
            pltpu.VMEM((rows, 128), f32),
            pltpu.VMEM((rows, 128), f32),
            pltpu.VMEM((4, 128, 2 * WIDE), bf16),
            pltpu.VMEM((rows, 256), bf16),
            pltpu.SemaphoreType.DMA((14,)),
        ],
        space=pl.ANY, limit=60,
        cost=pl.CostEstimate(flops=flops, bytes_accessed=8_000_000, transcendentals=flops // 1536),
    )


def head_columns(x, distance, width):
    return pl.ds(pl.multiple_of(lax.rem(x + distance, 4) * width, 128), width)


def pack_kernel(where_ref, pk, pv, k, v, q, g, s0, s1, s2, s3, rows, sems):
    pairs = []
    for d, target in enumerate((s0, s1, s2, s3)):
        cols = head_columns(where_ref[1], d, 128)
        for source, lines, lanes in ((pk, (0, 64), 0), (pv, (0, 64), 128), (k, (64, 192), 0), (v, (64, 192), 128)):
            pairs.append((source.at[:, cols], target.at[slice(*lines), lanes : lanes + 128]))
    for h in range(KV_HEADS):
        for source, first in ((q, 0), (g, WIDE)):
            pairs.append((source.at[:, h * WIDE : h * WIDE + WIDE], rows.at[h, :, first : first + WIDE]))
    copies = [pltpu.make_async_copy(source, target, sems.at[i]) for i, (source, target) in enumerate(pairs)]
    for copy in copies:
        copy.start()
    for copy in copies:
        copy.wait()


def collect_kernel(where_ref, s0, s1, s2, s3, mine_ref, ahead_ref):
    x = where_ref[1]
    for d, source in enumerate((s0, s1, s2, s3)):
        mine_ref[d * 64 : d * 64 + 64, :] = source[:64, :]
        block = lax.rem(x + 4 - d, 4)

        @pl.when(block > 0)
        def _():
            ahead_ref[pl.ds(pl.multiple_of((block - 1) * 128, 128), 128), :] = source[64:, :]


def final_sum_kernel(where_ref, n0, n1, n2, n3, own_ref, crossing_ref, within_ref, f0, f1, f2, f3):
    x = where_ref[1]
    for d, target in enumerate((f0, f1, f2, f3)):
        at = slice(d * 64, d * 64 + 64)
        total = (n0[at, :] + n1[at, :]) + (n2[at, :] + n3[at, :])
        target[:64, :] = total.astype(jnp.bfloat16)
        block = lax.rem(x + 4 - d, 4)
        behind = pl.ds(pl.multiple_of(jnp.maximum(block - 1, 0) * 128, 128), 128)
        for lanes, extra in (
            (slice(0, 128), crossing_ref[behind, :] + within_ref[behind, :128]),
            (slice(128, 256), within_ref[behind, 128:]),
        ):
            total = own_ref[block_at(x, d), lanes] + jnp.where(block > 0, extra, 0.0)
            target[64:, lanes] = total.astype(jnp.bfloat16)


def two_sums_kernel(a, b, c, d, ab_ref, cd_ref):
    ab_ref[...] = a[...] + b[...]
    cd_ref[...] = c[...] + d[...]


def pack_window_kernel(where_ref, k_ref, v_ref, over_z, after, out_ref):
    first = where_ref[0] == 0
    out_ref[:, :128] = jnp.where(first, 0.0, k_ref[...])
    out_ref[:, 128:] = jnp.where(first, over_z[...], v_ref[...])


def sum_kernel(a, b, *refs):
    refs[-1][...] = a[...] + b[...]


def unpack_rows_kernel(o_ref, out_ref, dq_ref):
    for h in range(KV_HEADS):
        at = slice(h * WIDE, h * WIDE + WIDE)
        out_ref[:, at] = o_ref[h, :, :WIDE]
        dq_ref[:, at] = o_ref[h, :, WIDE:]


def unpack_small_kernel(where_ref, f0, f1, f2, f3, k_ref, v_ref, pk_ref, pv_ref):
    x = where_ref[1]
    for d, source in enumerate((f0, f1, f2, f3)):
        at = head_columns(x, d, 128)
        pk_ref[:, at] = source[:64, :128]
        pv_ref[:, at] = source[:64, 128:]
        k_ref[:, at] = source[64:, :128]
        v_ref[:, at] = source[64:, 128:]


def along_x(value, step):
    return lax.ppermute(value, "seq", [(i, i // 4 * 4 + (i + step) % 4) for i in range(32)])


def exchange_x(value):
    return lax.all_to_all(value, "seq", 0, 0, axis_index_groups=X_GROUPS, tiled=True)


def along_y(value, step):
    return lax.ppermute(value, "seq", [(i, i // 16 * 16 + (i + 4 * step) % 16) for i in range(32)])


def along_z(value):
    return lax.ppermute(value, "seq", [(i, (i + 16) % 32) for i in range(32)])


def along_rows(value, step):
    pairs = [(i, i + 4 * step) for i in range(32)]
    return lax.ppermute(value, "seq", [(i, j) for i, j in pairs if 0 <= j < 32])


def local(resp_len, prompt_keys, prompt_values, resp_q, resp_k, resp_v, out_grad):
    me = lax.axis_index("seq").astype(jnp.int32)
    where = jnp.stack([me // 4 * OWN_ROWS, me % 4])
    rows, bf16, f32 = resp_q.shape[0], jnp.bfloat16, jnp.float32

    *s, q_all = call(
        pack_kernel, (where,), (prompt_keys, prompt_values, resp_k, resp_v, resp_q, out_grad),
        [((192, 256), bf16)] * 4 + [((4, rows, 2 * WIDE), bf16)], "pack",
        scratch=[pltpu.SemaphoreType.DMA((24,))], space=pl.ANY, limit=60,
    )
    s = [s[0]] + [along_x(s[d], d) for d in (1, 2, 3)]
    mine, ahead = call(collect_kernel, (where,), s, [((256, 256), bf16), ((BACK, 256), bf16)], "collect")
    mine, ahead, q_all = lax.optimization_barrier((mine, ahead, q_all))
    q_all = exchange_x(q_all)
    far = along_z(mine)
    near_keys = [mine] + [along_y(mine, d) for d in (1, 2, 3)]
    before = along_rows(ahead, 1)
    far_keys = [far] + [along_y(far, d) for d in (1, 2, 3)]

    o, h2, h1, h0, h3, l2, l1, l0, l3, own_grad, back_k, back_v = attention(
        resp_len, where, (q_all, *s, before, *far_keys, *near_keys)
    )

    through, minus = along_y(h2, 1), along_y(h1, -1)
    crossing = lax.ppermute(back_k, "seq", [(i, i - 4) for i in range(16, 20)])
    over_z = lax.ppermute(back_v, "seq", [(i, i - 16) for i in range(16, 20)])
    part = [((256, 256), f32)]
    plus, stay = call(two_sums_kernel, (), (h3, through, h0, minus), part * 2, "two_sums")
    plus, stay, o = lax.optimization_barrier((plus, stay, o))
    plus = along_y(plus, 1)
    (give,) = call(sum_kernel, (), (stay, plus), part, "far_sum", extra=(crossing, over_z))
    got = along_z(give)
    one, two, three = along_y(l1, -1), along_y(l2, -2), along_y(l3, 1)
    (back,) = call(pack_window_kernel, (where,), (back_k, back_v, over_z), [((BACK, 256), f32)], "pack_window", extra=(crossing,))
    pairs = [(i, i - 4) for i in range(4, 32) if i // 4 != 4] + [(i, i + 12) for i in range(4)]
    within = lax.ppermute(back, "seq", pairs)

    attn_out, q_grad = call(
        unpack_rows_kernel, (), (exchange_x(o),), [((rows, HEADS * HEAD_DIM), bf16)] * 2, "unpack_rows"
    )
    l0, attn_out, q_grad = lax.optimization_barrier((l0, attn_out, q_grad))
    (stay,) = call(sum_kernel, (), (l0, got), part, "near_sum")

    f = call(
        final_sum_kernel, (where,), (stay, one, two, three, own_grad, crossing, within),
        [((192, 256), bf16)] * 4, "final_sum",
    )
    f = [f[0]] + [along_x(f[d], -d) for d in (1, 2, 3)]
    resp_k_grad, resp_v_grad, prompt_k_grad, prompt_v_grad = call(
        unpack_small_kernel, (where,), f, [((rows, 512), bf16)] * 2 + [((64, 512), bf16)] * 2, "unpack_small"
    )
    return attn_out, q_grad, resp_k_grad, resp_v_grad, prompt_k_grad, prompt_v_grad


def solution(mesh):
    split = P(("grp", "seq"), None)
    return jax.shard_map(
        local,
        mesh=mesh,
        in_specs=(P("grp"),) + (split,) * 6,
        out_specs=(split,) * 6,
        check_vma=False,
    )
```

```python
import jax
import jax.numpy as jnp
from jax import lax
from jax.experimental import pallas as pl
from jax.experimental.pallas import tpu as pltpu
from jax.sharding import PartitionSpec as P

HEADS = 20
KV_HEADS = 4
HEAD_DIM = 128
PER_GROUP = HEADS // KV_HEADS
BACK = 384
NEGATIVE = -1e30
LOG2E = 1.4426950408889634
FACTOR = HEAD_DIM ** (-0.5)

X_GROUPS = [[first + x for x in range(4)] for first in range(0, 32, 4)]
ROWS = 256
KEYS = 1024
SPAN = 640
PROMPT_ROWS = 2048
OWN_ROWS = 512
WIDE = PER_GROUP * HEAD_DIM


def nt(a, b):
    return lax.dot_general(a, b, (((1,), (1,)), ((), ())), preferred_element_type=jnp.float32)


def nn(a, b):
    return lax.dot_general(a, b, (((1,), (0,)), ((), ())), preferred_element_type=jnp.float32)


def block_at(x, distance):
    return pl.ds(pl.multiple_of(lax.rem(x + 4 - distance, 4) * 128, 128), 128)


def attention_kernel(
    len_ref, where_ref, q_in, s0, s1, s2, s3, before_in, h0, h1, h2, h3, l0, l1, l2, l3,
    o_ref, g0, g1, g2, g3, g4, g5, g6, g7, back_grad_ref, own_grad_ref,
    key2, value1, key_t, value_t, s_first, s_second, p_first, p_second,
    grad2_first, grad2_second, rows_first, rows_second, key_sum, value_sum, q_all, staged, sems,
):
    base, x = where_ref[0], where_ref[1]
    all_rows = PROMPT_ROWS + BACK + OWN_ROWS

    def place(at, source):
        key2[at, :128] = source[:, :128]
        key2[at, 128:] = source[:, :128]
        value1[at, :128] = source[:, 128:]

    copies = []

    def load(source, target):
        copies.append(pltpu.make_async_copy(source, target, sems.at[len(copies)]))
        copies[-1].start()

    for i, source in enumerate((h2, h1, h0, h3, l2, l1, l0, l3)):
        load(source, staged.at[i * 256 : i * 256 + 256, :])
    load(before_in, staged.at[PROMPT_ROWS : PROMPT_ROWS + BACK, :])
    for d, source in enumerate((s0, s1, s2, s3)):
        first = PROMPT_ROWS + BACK + lax.rem(x + 4 - d, 4) * 128
        load(source.at[64:192, :], staged.at[pl.ds(pl.multiple_of(first, 128), 128), :])
    load(q_in, q_all)
    for copy in copies[:-1]:
        copy.wait()
    place(slice(0, all_rows), staged)
    value1[:, 128:] = jnp.ones((all_rows, 128), jnp.bfloat16)
    value_t[128:, :] = jnp.ones((16, all_rows), jnp.bfloat16)
    for c in range(0, all_rows, 128):
        at = slice(c, c + 128)
        key_t[:, at] = key2[at, :128].astype(jnp.float32).T.astype(jnp.bfloat16)
        value_t[:128, at] = value1[at, :128].astype(jnp.float32).T.astype(jnp.bfloat16)
    for ref in (key_sum, value_sum, p_second, grad2_second, rows_second):
        ref[...] = jnp.zeros_like(ref)
    copies[-1].wait()

    s_refs, p_refs = (s_first, s_second), (p_first, p_second)
    grad2_refs, rows_refs = (grad2_first, grad2_second), (rows_first, rows_second)

    def tiles(block):
        span = PROMPT_ROWS + block * ROWS
        out = [(c, c, KEYS) for c in range(0, PROMPT_ROWS, KEYS)] + [(span, PROMPT_ROWS, SPAN)]
        return [(slice(keys, keys + size), slice(at, at + size)) for keys, at, size in out]

    def rows_of(block, head, first):
        cols = pl.ds(pl.multiple_of(first + head * 128, 128), 128)
        return q_all[block * 2 : block * 2 + 2, :, cols].reshape(ROWS, 128)

    def scores(block, head):
        scaled = rows_of(block, head, 0).astype(jnp.float32).T * (FACTOR * LOG2E)
        high = scaled.astype(jnp.bfloat16)
        low = (scaled - high.astype(jnp.float32)).astype(jnp.bfloat16)
        q2t = jnp.concatenate([high, low], 0)
        top = None
        for keys, at in tiles(block):
            s = nn(key2[keys, :], q2t)
            if at.start == PROMPT_ROWS:
                own = base + block * ROWS
                row_pos = own + lax.broadcasted_iota(jnp.int32, (1, ROWS), 1)
                seg_start = jnp.zeros((1, ROWS), jnp.int32)
                end = jnp.int32(0)
                for j in range(16):
                    end = end + len_ref[j]
                    seg_start = jnp.maximum(seg_start, jnp.where(row_pos >= end, end, 0))
                key_pos = own - BACK + lax.broadcasted_iota(jnp.int32, (SPAN, ROWS), 0)
                s = jnp.where((key_pos <= row_pos) & (key_pos >= seg_start), s, NEGATIVE)
            s_refs[block][at, :] = s
            tile_top = jnp.max(s, axis=0, keepdims=True)
            top = tile_top if top is None else jnp.maximum(top, tile_top)
            yield top

    def weigh(block, head, top):
        total = jnp.zeros((144, ROWS), jnp.float32)
        for i, (keys, at) in enumerate(tiles(block)):
            p = jnp.exp2(s_refs[block][at, :] - top).astype(jnp.bfloat16)
            p_refs[block][at, :] = p
            total = total + nn(value_t[:, keys], p)
            if i < len(tiles(block)) - 1:
                yield
        inverse = 1.0 / total[128:129, :]
        out = (total[:128, :] * inverse).astype(jnp.bfloat16).astype(jnp.float32)
        cols = pl.ds(pl.multiple_of(head * 128, 128), 128)
        o_ref[block * 2 : block * 2 + 2, :, cols] = out.T.astype(jnp.bfloat16).reshape(2, 128, 128)
        grad_n = (rows_of(block, head, WIDE).astype(jnp.float32).T * inverse).astype(jnp.bfloat16)
        wide = grad_n.astype(jnp.float32)
        row_dot = -jnp.sum(wide * out, axis=0, keepdims=True)
        dot_high = row_dot.astype(jnp.bfloat16).astype(jnp.float32)
        line = lax.broadcasted_iota(jnp.int32, (128, ROWS), 0)
        extra = jnp.where(line == 0, dot_high, jnp.where(line == 1, row_dot - dot_high, 0.0))
        grad2_refs[block][:128, :] = grad_n
        grad2_refs[block][128:, :] = extra.astype(jnp.bfloat16)
        rows_refs[block][...] = wide.T.astype(jnp.bfloat16)
        yield

    def backward(block, head):
        q = rows_of(block, head, 0)
        dq = jnp.zeros((HEAD_DIM, ROWS), jnp.float32)
        for i, (keys, at) in enumerate(tiles(block)):
            p = p_refs[block][at, :]
            ds = (p.astype(jnp.float32) * nn(value1[keys, :], grad2_refs[block][...])).astype(jnp.bfloat16)
            dq = dq + nn(key_t[:, keys], ds)
            key_sum[keys, :] += nn(ds, q)
            value_sum[keys, :] += nn(p, rows_refs[block][...])
            if i < len(tiles(block)) - 1:
                yield
        cols = pl.ds(pl.multiple_of(WIDE + head * 128, 128), 128)
        dq = (dq * FACTOR).T.astype(jnp.bfloat16)
        o_ref[block * 2 : block * 2 + 2, :, cols] = dq.reshape(2, 128, 128)
        yield

    def beside(one, other):
        last = None
        for _, last in zip(one, other):
            pass
        return last

    def step(head, carry):
        top_first = beside(backward(1, jnp.maximum(head - 1, 0)), scores(0, head))
        top_second = beside(weigh(0, head, top_first), scores(1, head))
        beside(backward(0, head), weigh(1, head, top_second))
        return carry

    lax.fori_loop(0, PER_GROUP, step, 0)
    for _ in backward(1, PER_GROUP - 1):
        pass

    outs = [(i * 256, i * 256 + 256, ref) for i, ref in enumerate((g0, g1, g2, g3, g4, g5, g6, g7))]
    outs += [(PROMPT_ROWS, PROMPT_ROWS + BACK, back_grad_ref), (PROMPT_ROWS + BACK, all_rows, own_grad_ref)]
    for first, last, target in outs:
        target[:, :128] = key_sum[first:last, :] * FACTOR
        target[:, 128:] = value_sum[first:last, :]


def call(body, scalars, operands, outs, name, scratch=(), limit=24, cost=None, space=pltpu.VMEM, extra=()):
    smem = pl.BlockSpec(memory_space=pltpu.SMEM)
    return pl.pallas_call(
        body,
        in_specs=[smem] * len(scalars) + [pl.BlockSpec(memory_space=space)] * len(operands)
        + [pl.BlockSpec(memory_space=pl.ANY)] * len(extra),
        out_specs=[pl.BlockSpec(memory_space=pltpu.VMEM)] * len(outs),
        out_shape=[jax.ShapeDtypeStruct(shape, dtype) for shape, dtype in outs],
        scratch_shapes=list(scratch),
        compiler_params=pltpu.CompilerParams(vmem_limit_bytes=limit * 1024 * 1024),
        cost_estimate=cost,
        name=name,
    )(*scalars, *operands, *extra)


def attention(resp_len, where, operands):
    bf16, f32 = jnp.bfloat16, jnp.float32
    rows = PROMPT_ROWS + BACK + OWN_ROWS
    flops = 12 * 2560 * 2560 * 128
    return call(
        attention_kernel, (resp_len, where), operands,
        [((4, 128, 2 * WIDE), bf16)] + [((256, 256), f32)] * 8 + [((BACK, 256), f32), ((OWN_ROWS, 256), f32)],
        "attention",
        scratch=[
            pltpu.VMEM((rows, 256), bf16),
            pltpu.VMEM((rows, 256), bf16),
            pltpu.VMEM((128, rows), bf16),
            pltpu.VMEM((144, rows), bf16),
            pltpu.VMEM((PROMPT_ROWS + SPAN, ROWS), f32),
            pltpu.VMEM((PROMPT_ROWS + SPAN, ROWS), f32),
            pltpu.VMEM((PROMPT_ROWS + SPAN, ROWS), bf16),
            pltpu.VMEM((PROMPT_ROWS + SPAN, ROWS), bf16),
            pltpu.VMEM((256, ROWS), bf16),
            pltpu.VMEM((256, ROWS), bf16),
            pltpu.VMEM((ROWS, 128), bf16),
            pltpu.VMEM((ROWS, 128), bf16),
            pltpu.VMEM((rows, 128), f32),
            pltpu.VMEM((rows, 128), f32),
            pltpu.VMEM((4, 128, 2 * WIDE), bf16),
            pltpu.VMEM((rows, 256), bf16),
            pltpu.SemaphoreType.DMA((14,)),
        ],
        space=pl.ANY, limit=60,
        cost=pl.CostEstimate(flops=flops, bytes_accessed=8_000_000, transcendentals=flops // 1536),
    )


def head_columns(x, distance, width):
    return pl.ds(pl.multiple_of(lax.rem(x + distance, 4) * width, 128), width)


def pack_kernel(where_ref, pk, pv, k, v, q, g, s0, s1, s2, s3, rows, sems):
    pairs = []
    for d, target in enumerate((s0, s1, s2, s3)):
        cols = head_columns(where_ref[1], d, 128)
        for source, lines, lanes in ((pk, (0, 64), 0), (pv, (0, 64), 128), (k, (64, 192), 0), (v, (64, 192), 128)):
            pairs.append((source.at[:, cols], target.at[slice(*lines), lanes : lanes + 128]))
    for h in range(KV_HEADS):
        for source, first in ((q, 0), (g, WIDE)):
            pairs.append((source.at[:, h * WIDE : h * WIDE + WIDE], rows.at[h, :, first : first + WIDE]))
    copies = [pltpu.make_async_copy(source, target, sems.at[i]) for i, (source, target) in enumerate(pairs)]
    for copy in copies:
        copy.start()
    for copy in copies:
        copy.wait()


def collect_kernel(where_ref, s0, s1, s2, s3, mine_ref, ahead_ref):
    x = where_ref[1]
    for d, source in enumerate((s0, s1, s2, s3)):
        mine_ref[d * 64 : d * 64 + 64, :] = source[:64, :]
        block = lax.rem(x + 4 - d, 4)

        @pl.when(block > 0)
        def _():
            ahead_ref[pl.ds(pl.multiple_of((block - 1) * 128, 128), 128), :] = source[64:, :]


def final_sum_kernel(where_ref, n0, n1, n2, n3, got_ref, own_ref, crossing_ref, within_ref, f0, f1, f2, f3):
    x = where_ref[1]
    for d, target in enumerate((f0, f1, f2, f3)):
        at = slice(d * 64, d * 64 + 64)
        total = (n0[at, :] + n1[at, :]) + (n2[at, :] + n3[at, :]) + got_ref[at, :]
        target[:64, :] = total.astype(jnp.bfloat16)
        block = lax.rem(x + 4 - d, 4)
        behind = pl.ds(pl.multiple_of(jnp.maximum(block - 1, 0) * 128, 128), 128)
        extra = jnp.where(block > 0, crossing_ref[behind, :] + within_ref[behind, :], 0.0)
        target[64:, :] = (own_ref[block_at(x, d), :] + extra).astype(jnp.bfloat16)


def far_sum_kernel(a, b, c, out_ref):
    out_ref[...] = a[...] + b[...] + c[...]


def unpack_rows_kernel(o_ref, out_ref, dq_ref):
    for h in range(KV_HEADS):
        at = slice(h * WIDE, h * WIDE + WIDE)
        out_ref[:, at] = o_ref[h, :, :WIDE]
        dq_ref[:, at] = o_ref[h, :, WIDE:]


def unpack_small_kernel(where_ref, f0, f1, f2, f3, k_ref, v_ref, pk_ref, pv_ref):
    x = where_ref[1]
    for d, source in enumerate((f0, f1, f2, f3)):
        at = head_columns(x, d, 128)
        pk_ref[:, at] = source[:64, :128]
        pv_ref[:, at] = source[:64, 128:]
        k_ref[:, at] = source[64:, :128]
        v_ref[:, at] = source[64:, 128:]


def along_x(value, step):
    return lax.ppermute(value, "seq", [(i, i // 4 * 4 + (i + step) % 4) for i in range(32)])


def exchange_x(value):
    return lax.all_to_all(value, "seq", 0, 0, axis_index_groups=X_GROUPS, tiled=True)


def along_y(value, step):
    return lax.ppermute(value, "seq", [(i, i // 16 * 16 + (i + 4 * step) % 16) for i in range(32)])


def along_z(value):
    return lax.ppermute(value, "seq", [(i, (i + 16) % 32) for i in range(32)])


def along_rows(value, step):
    pairs = [(i, i + 4 * step) for i in range(32)]
    return lax.ppermute(value, "seq", [(i, j) for i, j in pairs if 0 <= j < 32])


def local(resp_len, prompt_keys, prompt_values, resp_q, resp_k, resp_v, out_grad):
    me = lax.axis_index("seq").astype(jnp.int32)
    where = jnp.stack([me // 4 * OWN_ROWS, me % 4])
    rows, bf16, f32 = resp_q.shape[0], jnp.bfloat16, jnp.float32

    *s, q_all = call(
        pack_kernel, (where,), (prompt_keys, prompt_values, resp_k, resp_v, resp_q, out_grad),
        [((192, 256), bf16)] * 4 + [((4, rows, 2 * WIDE), bf16)], "pack",
        scratch=[pltpu.SemaphoreType.DMA((24,))], space=pl.ANY, limit=60,
    )
    s = [s[0]] + [along_x(s[d], d) for d in (1, 2, 3)]
    mine, ahead = call(collect_kernel, (where,), s, [((256, 256), bf16), ((BACK, 256), bf16)], "collect")
    mine, ahead, q_all = lax.optimization_barrier((mine, ahead, q_all))
    q_all = exchange_x(q_all)
    far = along_z(mine)
    near_keys = [mine] + [along_y(mine, d) for d in (1, 2, 3)]
    before = along_rows(ahead, 1)
    far_keys = [far] + [along_y(far, d) for d in (1, 2, 3)]

    o, h2, h1, h0, h3, l2, l1, l0, l3, back_grad, own_grad = attention(
        resp_len, where, (q_all, *s, before, *far_keys, *near_keys)
    )

    through, minus = along_y(h2, 1), along_y(h1, -1)
    plus = along_y(h3 + through, 1)
    crossing = lax.ppermute(back_grad, "seq", [(i, i - 4) for i in range(16, 20)])
    back_grad, plus = lax.optimization_barrier((back_grad, plus))
    within = lax.ppermute(back_grad, "seq", [(i, i - 4) for i in range(4, 32) if i // 4 != 4])
    (got,) = call(far_sum_kernel, (), (h0, minus, plus), [((256, 256), f32)], "far_sum")
    got = along_z(got)
    one, two, three = along_y(l1, -1), along_y(l2, -2), along_y(l3, 1)

    o, crossing = lax.optimization_barrier((exchange_x(o), crossing))
    attn_out, q_grad = call(
        unpack_rows_kernel, (), (o,), [((rows, HEADS * HEAD_DIM), bf16)] * 2, "unpack_rows"
    )
    l0, attn_out, q_grad = lax.optimization_barrier((l0, attn_out, q_grad))

    f = call(
        final_sum_kernel, (where,), (l0, one, two, three, got, own_grad, crossing, within),
        [((192, 256), bf16)] * 4, "final_sum",
    )
    f = [f[0]] + [along_x(f[d], -d) for d in (1, 2, 3)]
    resp_k_grad, resp_v_grad, prompt_k_grad, prompt_v_grad = call(
        unpack_small_kernel, (where,), f, [((rows, 512), bf16)] * 2 + [((64, 512), bf16)] * 2, "unpack_small"
    )
    return attn_out, q_grad, resp_k_grad, resp_v_grad, prompt_k_grad, prompt_v_grad


def solution(mesh):
    split = P(("grp", "seq"), None)
    return jax.shard_map(
        local,
        mesh=mesh,
        in_specs=(P("grp"),) + (split,) * 6,
        out_specs=(split,) * 6,
        check_vma=False,
    )
```
